32 devices in a mesh: dp: 2 (over core), fsdp: 16 (over z, y, x).
Axes of the slice: x: 2, y: 2, z: 4, core: 2. Of those that a mesh axis runs over, the one named last changes fastest.
Arguments:
- tokens: bfloat16 [16, 4096, 512], P('fsdp', 'dp'), may hold values from -6 to 6
- segments: int32 [16, 4096], P('fsdp'), may hold values from 0 to 4, as said below
- cotangent: bfloat16 [16, 4096, 512], P('fsdp', 'dp')
- w_qkv: float32 [512, 1536], P('fsdp'), may hold values from -0.25 to 0.25
- w_out: float32 [512, 512], P(None, 'fsdp'), may hold values from -6 to 6
- w_up: float32 [512, 2048], P('fsdp'), may hold values from -0.25 to 0.25
- w_down: float32 [2048, 512], P(None, 'fsdp'), may hold values from -0.125 to 0.125
- small_params: float32 [6, 512], P(None, 'fsdp')
- up_bias: float32 [2048], P('fsdp'), may hold values from -3 to 3
- first_qkv: float32 [512, 1536], P('fsdp'), may hold values from -0.0009765625 to 0.0009765625
- first_out: float32 [512, 512], P(None, 'fsdp'), may hold values from -0.0009765625 to 0.0009765625
- first_up: float32 [512, 2048], P('fsdp'), may hold values from -0.0009765625 to 0.0009765625
- first_down: float32 [2048, 512], P(None, 'fsdp'), may hold values from -0.0009765625 to 0.0009765625
- first_small: float32 [6, 512], P(None, 'fsdp'), may hold values from -0.001953125 to 0.001953125
- first_bias: float32 [2048], P('fsdp'), may hold values from -0.00024414062 to 0.00024414062
- second_qkv: float32 [512, 1536], P('fsdp'), may hold values from 3.1737488e-11 to 1.2694995e-10
- second_out: float32 [512, 512], P(None, 'fsdp'), may hold values from 3.1737488e-11 to 1.2694995e-10
- second_up: float32 [512, 2048], P('fsdp'), may hold values from 3.1737488e-11 to 1.2694995e-10
- second_down: float32 [2048, 512], P(None, 'fsdp'), may hold values from 3.1737488e-11 to 1.2694995e-10
- second_small: float32 [6, 512], P(None, 'fsdp'), may hold values from 1.2694995e-09 to 5.077998e-09
- second_bias: float32 [2048], P('fsdp'), may hold values from 3.1737488e-12 to 1.2694995e-11
Outputs:
- layer_out: bfloat16 [16, 4096, 512], P('fsdp', 'dp')
- input_grad: bfloat16 [16, 4096, 512], P('fsdp', 'dp')
- grad_norm: float32 [], replicated
- new_qkv: float32 [512, 1536], P('fsdp')
- new_out: float32 [512, 512], P(None, 'fsdp')
- new_up: float32 [512, 2048], P('fsdp')
- new_down: float32 [2048, 512], P(None, 'fsdp')
- new_small: float32 [6, 512], P(None, 'fsdp')
- new_bias: float32 [2048], P('fsdp')
- new_first_qkv: float32 [512, 1536], P('fsdp')
- new_first_out: float32 [512, 512], P(None, 'fsdp')
- new_first_up: float32 [512, 2048], P('fsdp')
- new_first_down: float32 [2048, 512], P(None, 'fsdp')
- new_first_small: float32 [6, 512], P(None, 'fsdp')
- new_first_bias: float32 [2048], P('fsdp')
- new_second_qkv: float32 [512, 1536], P('fsdp')
- new_second_out: float32 [512, 512], P(None, 'fsdp')
- new_second_up: float32 [512, 2048], P('fsdp')
- new_second_down: float32 [2048, 512], P(None, 'fsdp')
- new_second_small: float32 [6, 512], P(None, 'fsdp')
- new_second_bias: float32 [2048], P('fsdp')
The draws below stay inside these ranges and needn't reach their ends.
Inputs may be any that keep to these rules, and one draw needn't show every extreme that they name: `segments`: along each packed row the document numbers never fall; the last slot of every row holds 4.
All inputs are finite; a program needn't handle non-finite values.
Results may differ from the reference program's by a relative error of at most 0.014.
The reference program's roundings to bfloat16 on the way count: a program that leaves them out, or rounds other values in their place, can miss the bound.
Values may be sent and summed in bfloat16 or wider, within the bound.
No kernel may reach another device: no remote copies, remote signals or barrier semaphores. Data moves between devices by JAX's collectives and lax.ppermute only.
A program may use at most 448 MiB of HBM per device.

```python
import math
import jax
import jax.numpy as jnp
from jax import lax

D = 512
FF = 2048
HEADS = 8
HEAD = 64
DOCS = 4
STEP = 10
ROW_LEN = 4096
SEQS = 16
PARAMS = 3150848
OUT_FAN = 1


def draw_segments(key, part):
    key = jax.random.fold_in(key, 2)
    below_key, above_key, chosen_key = jax.random.split(key, 3)
    margin = ROW_LEN // 8
    centre = ROW_LEN // 2
    lower_cut = jax.random.randint(below_key, (SEQS, DOCS), 1, centre - margin)
    upper_cut = jax.random.randint(above_key, (SEQS, DOCS), centre + margin + 1, ROW_LEN)
    chosen = jax.random.randint(chosen_key, (SEQS, DOCS), 0, 2)
    cut_at = jnp.where(chosen == 1, upper_cut, lower_cut)
    places = jnp.arange(ROW_LEN, dtype=jnp.int32)
    return jnp.sum((cut_at[:, None, :] <= places[None, :, None]).astype(jnp.int32), axis=-1).astype(jnp.int32)


def draw_cotangent(key, part):
    key = jax.random.fold_in(key, 3)
    position_ramp = jnp.arange(D, dtype=jnp.float32) / D
    randoms = jax.random.normal(key, (SEQS, ROW_LEN, D), jnp.float32)
    rising = 0.6 + 1.2 * position_ramp
    return (randoms * rising).astype(jnp.bfloat16)


def draw_small_params(key, part):
    key = jax.random.fold_in(key, 5)
    gain_key, shift_key = jax.random.split(key)
    position_ramp = jnp.arange(D, dtype=jnp.float32) / D
    rising = 0.6 + 1.2 * position_ramp
    wobble = jnp.clip(0.12 * jax.random.normal(gain_key, (2, D), jnp.float32), -0.4, 0.4)
    shifts = 0.5 * jax.random.normal(shift_key, (4, D), jnp.float32)
    gains = rising[None, :] * (1.0 + wobble)
    return jnp.stack([gains[0], shifts[0], gains[1], shifts[1], shifts[2], shifts[3]]).astype(jnp.float32)


def block_levels(key, dims, cuts, smallest, high):
    def one(position, blocks):
        heights = jax.random.uniform(jax.random.fold_in(jax.random.fold_in(key, 6), position), (blocks,), jnp.float32, smallest / len(cuts), high / len(cuts))
        return jnp.repeat(jnp.exp(heights), dims[position] // blocks).reshape((-1,) + (1,) * (len(dims) - position - 1))

    factor_of = one(*cuts[0])
    for cut in cuts[1:]:
        factor_of = factor_of * one(*cut)
    return factor_of


def noise(own_key, extent, scale, reach, cuts=(), held_as=jnp.bfloat16):
    drawn = scale * jax.random.normal(own_key, extent, jnp.float32)
    if cuts:
        drawn = drawn * block_levels(own_key, extent, cuts, -0.22, 0.18)
    return jnp.clip(drawn, -reach, reach).astype(held_as)


def setup_inputs(seed: int = 0) -> dict:
    seeds = jax.random.split(jax.random.key(seed), 22)
    tokens = noise(seeds[0], (SEQS, ROW_LEN, D), 1.0, 6.0, ((0, 16), (1, 2)))
    segments = draw_segments(jax.random.fold_in(seeds[21], 71), 0)
    cotangent = draw_cotangent(jax.random.fold_in(seeds[21], 71), 0)
    w_qkv = noise(seeds[3], (D, 3 * D), D ** -0.5, 0.25, ((0, 16),), jnp.float32)
    w_out = noise(seeds[4], (D, D), OUT_FAN ** -0.5, 6.0, ((1, 16),), jnp.float32)
    w_up = noise(seeds[5], (D, FF), D ** -0.5, 0.25, ((0, 16),), jnp.float32)
    w_down = noise(seeds[6], (FF, D), FF ** -0.5, 0.125, ((1, 16),), jnp.float32)
    small_params = draw_small_params(jax.random.fold_in(seeds[21], 71), 0)
    up_bias = noise(seeds[8], (FF,), 0.5, 3.0, ((0, 16),), jnp.float32)
    first_qkv = noise(seeds[9], (D, 3 * D), (0.11 / PARAMS ** 0.5), 0.0009765625, ((0, 16),), jnp.float32)
    first_out = noise(seeds[10], (D, D), (0.11 / PARAMS ** 0.5), 0.0009765625, ((1, 16),), jnp.float32)
    first_up = noise(seeds[11], (D, FF), (0.11 / PARAMS ** 0.5), 0.0009765625, ((0, 16),), jnp.float32)
    first_down = noise(seeds[12], (FF, D), (0.11 / PARAMS ** 0.5), 0.0009765625, ((1, 16),), jnp.float32)
    first_small = noise(seeds[13], (6, D), (0.22 / PARAMS ** 0.5), 0.001953125, ((1, 16),), jnp.float32)
    first_bias = noise(seeds[14], (FF,), (0.03 / PARAMS ** 0.5), 0.00024414062, ((0, 16),), jnp.float32)
    second_qkv = jnp.clip(jnp.exp(math.log(1.2694995055184677e-10) - 1.3862944 * jax.random.uniform(seeds[15], (D, 3 * D), jnp.float32) ** block_levels(seeds[15], (D, 3 * D), ((0, 16),), -0.2, 0.2)), 3.173748763796169e-11, 1.2694995055184677e-10)
    second_out = jnp.clip(jnp.exp(math.log(1.2694995055184677e-10) - 1.3862944 * jax.random.uniform(seeds[16], (D, D), jnp.float32) ** block_levels(seeds[16], (D, D), ((1, 16),), -0.2, 0.2)), 3.173748763796169e-11, 1.2694995055184677e-10)
    second_up = jnp.clip(jnp.exp(math.log(1.2694995055184677e-10) - 1.3862944 * jax.random.uniform(seeds[17], (D, FF), jnp.float32) ** block_levels(seeds[17], (D, FF), ((0, 16),), -0.2, 0.2)), 3.173748763796169e-11, 1.2694995055184677e-10)
    second_down = jnp.clip(jnp.exp(math.log(1.2694995055184677e-10) - 1.3862944 * jax.random.uniform(seeds[18], (FF, D), jnp.float32) ** block_levels(seeds[18], (FF, D), ((1, 16),), -0.2, 0.2)), 3.173748763796169e-11, 1.2694995055184677e-10)
    second_small = jnp.clip(jnp.exp(math.log(5.077998022073871e-09) - 1.3862944 * jax.random.uniform(seeds[19], (6, D), jnp.float32) ** block_levels(seeds[19], (6, D), ((1, 16),), -0.2, 0.2)), 1.2694995055184677e-09, 5.077998022073871e-09)
    second_bias = jnp.clip(jnp.exp(math.log(1.2694995228657024e-11) - 1.3862944 * jax.random.uniform(seeds[20], (FF,), jnp.float32) ** block_levels(seeds[20], (FF,), ((0, 16),), -0.2, 0.2)), 3.173748807164256e-12, 1.2694995228657024e-11)
    return {"tokens": tokens, "segments": segments, "cotangent": cotangent, "w_qkv": w_qkv, "w_out": w_out, "w_up": w_up, "w_down": w_down, "small_params": small_params, "up_bias": up_bias, "first_qkv": first_qkv, "first_out": first_out, "first_up": first_up, "first_down": first_down, "first_small": first_small, "first_bias": first_bias, "second_qkv": second_qkv, "second_out": second_out, "second_up": second_up, "second_down": second_down, "second_small": second_small, "second_bias": second_bias}


PRECISE = lax.Precision.HIGHEST
LN_EPS = 1e-05
CLIP_NORM = 1.0
BETA_ONE = 0.9
BETA_TWO = 0.999
ADAM_EPS = 1e-08
RATE_MATRIX = 0.04
RATE_VECTOR = 0.5
DECAY_MATRIX = 0.1
MASKED_SCORE = -1e+30

@jax.custom_vjp
def low(v):
    return lax.optimization_barrier(v.astype(jnp.bfloat16)).astype(jnp.float32)

@jax.custom_vjp
def low_back(v):
    return v

def low_keep(v):
    return (low(v), None)

def low_pass(kept, grad):
    return (grad,)

def back_keep(v):
    return (v, None)

def back_low(kept, grad):
    return (low(grad),)
low.defvjp(low_keep, low_pass)
low_back.defvjp(back_keep, back_low)

def layer_norm(values, gain, shift):
    centre = lax.optimization_barrier(jnp.mean(values, axis=-1, keepdims=True))
    centered = values - centre
    spread = lax.optimization_barrier(jnp.mean(centered * centered, axis=-1, keepdims=True))
    return centered * lax.rsqrt(spread + LN_EPS) * gain + shift

def encode_row(token_row, segment_row, weights):
    w_qkv, w_out, w_up, w_down, small_params, up_bias = weights
    length = token_row.shape[0]
    normed = low(layer_norm(token_row, small_params[0], small_params[1]))
    packed = low_back(low(jnp.dot(normed, w_qkv, precision=PRECISE)))
    queries = packed[:, :D].reshape(length, HEADS, HEAD)
    keys_all = packed[:, D:2 * D].reshape(length, HEADS, HEAD)
    values_all = packed[:, 2 * D:].reshape(length, HEADS, HEAD)
    scale = 1.0 / math.sqrt(HEAD)
    scores = low_back(jnp.einsum('qhd,khd->hqk', queries, keys_all, precision=PRECISE) * scale)
    allowed = (segment_row[:, None] == segment_row[None, :])[None]
    masked = jnp.where(allowed, scores, MASKED_SCORE)
    highest = lax.optimization_barrier(jnp.max(masked, axis=-1, keepdims=True))
    expo = jnp.where(allowed, jnp.exp(masked - highest), 0.0)
    probs = low(expo / lax.optimization_barrier(jnp.sum(expo, axis=-1, keepdims=True)))
    mixed = jnp.einsum('hqk,khd->qhd', probs, values_all, precision=PRECISE).reshape(length, D)
    mixed = low_back(low(mixed))
    branch = low_back(jnp.dot(mixed, w_out, precision=PRECISE))
    middle = token_row + branch + small_params[4]
    normed_two = low(layer_norm(middle, small_params[2], small_params[3]))
    pre_act = low_back(jnp.dot(normed_two, w_up, precision=PRECISE) + up_bias)
    hidden = low(jax.nn.gelu(pre_act, approximate=True))
    down_part = low_back(jnp.dot(hidden, w_down, precision=PRECISE))
    return middle + down_part + small_params[5]

def adamw(weight, grad, first, second, rate, decay):
    first = BETA_ONE * first + (1.0 - BETA_ONE) * grad
    second = BETA_TWO * second + (1.0 - BETA_TWO) * grad * grad
    fixed_one = first / (1.0 - BETA_ONE ** STEP)
    fixed_two = second / (1.0 - BETA_TWO ** STEP)
    weight = weight - rate * (fixed_one / (jnp.sqrt(fixed_two) + ADAM_EPS) + decay * weight)
    return (weight, first, second)

def reference(tokens, segments, cotangent, w_qkv, w_out, w_up, w_down, small_params, up_bias, first_qkv, first_out, first_up, first_down, first_small, first_bias, second_qkv, second_out, second_up, second_down, second_small, second_bias):
    rate_out = RATE_MATRIX * math.sqrt(D / OUT_FAN)

    def forward(token_all, qkv_in, out_in, up_in, down_in, small_in, bias_in):
        rounded = (low(qkv_in), low(out_in), low(up_in), low(down_in), low(small_in), low(bias_in))

        def step_row(carry, pair):
            return (carry, jax.checkpoint(encode_row)(pair[0], pair[1], rounded))
        _, outputs = lax.scan(step_row, jnp.zeros((), jnp.float32), (token_all, segments))
        return outputs
    outputs, pullback = jax.vjp(forward, tokens.astype(jnp.float32), w_qkv, w_out, w_up, w_down, small_params, up_bias)
    grad_tokens, grad_qkv, grad_out, grad_up, grad_down, grad_small, grad_bias = pullback(cotangent.astype(jnp.float32))
    squares = jnp.sum(grad_qkv * grad_qkv) + jnp.sum(grad_out * grad_out) + jnp.sum(grad_up * grad_up) + jnp.sum(grad_down * grad_down) + jnp.sum(grad_small * grad_small) + jnp.sum(grad_bias * grad_bias)
    grad_norm = jnp.sqrt(squares)
    factor = jnp.minimum(1.0, CLIP_NORM / (grad_norm + 1e-06))
    new_qkv, new_first_qkv, new_second_qkv = adamw(w_qkv, grad_qkv * factor, first_qkv, second_qkv, RATE_MATRIX, DECAY_MATRIX)
    new_out, new_first_out, new_second_out = adamw(w_out, grad_out * factor, first_out, second_out, rate_out, DECAY_MATRIX)
    new_up, new_first_up, new_second_up = adamw(w_up, grad_up * factor, first_up, second_up, RATE_MATRIX, DECAY_MATRIX)
    new_down, new_first_down, new_second_down = adamw(w_down, grad_down * factor, first_down, second_down, RATE_MATRIX, DECAY_MATRIX)
    new_small, new_first_small, new_second_small = adamw(small_params, grad_small * factor, first_small, second_small, RATE_VECTOR, 0.0)
    new_bias, new_first_bias, new_second_bias = adamw(up_bias, grad_bias * factor, first_bias, second_bias, RATE_VECTOR, 0.0)
    return (outputs.astype(jnp.bfloat16), grad_tokens.astype(jnp.bfloat16), grad_norm, new_qkv, new_out, new_up, new_down, new_small, new_bias, new_first_qkv, new_first_out, new_first_up, new_first_down, new_first_small, new_first_bias, new_second_qkv, new_second_out, new_second_up, new_second_down, new_second_small, new_second_bias)
```

```python
import functools
import math

import jax
import jax.numpy as jnp
from jax import lax
from jax.experimental import pallas as pl
from jax.experimental.pallas import tpu as pltpu
from jax.sharding import PartitionSpec as P

HEADS = 8
DOCS = 4
STEP = 10


LN_EPS = 1e-05
CLIP_NORM = 1.0
BETA_ONE = 0.9
BETA_TWO = 0.999
ADAM_EPS = 1e-08
RATE_MATRIX = 0.04
RATE_VECTOR = 0.5
DECAY_MATRIX = 0.1
MASKED_SCORE = -1e30
LOWEST = -3e38

HEAD = 64
LANES = 128
SEG_AT = HEAD
LSE_AT = HEAD + 16
VMEM = 60 << 20

bf16 = jnp.bfloat16
f32 = jnp.float32
NN = (((1,), (0,)), ((), ()))
NT = (((1,), (1,)), ((), ()))
TN = (((0,), (0,)), ((), ()))


def mm(left, right, dims):
    return lax.dot_general(left, right, dims, preferred_element_type=f32)


def params():
    return pltpu.CompilerParams(vmem_limit_bytes=VMEM)


def whole(*shape):
    return pl.BlockSpec(shape, lambda i, *_: (0,) * len(shape))


def cost(flops, nbytes, trans=0):
    return pl.CostEstimate(flops=int(flops), bytes_accessed=int(nbytes), transcendentals=int(trans))


def normalize(values):
    centre = jnp.mean(values, axis=-1, keepdims=True)
    centered = values - centre
    spread = jnp.mean(centered * centered, axis=-1, keepdims=True)
    rstd = lax.rsqrt(spread + LN_EPS)
    return centered * rstd, rstd


def normalize_back(grad, hat, rstd):
    along = jnp.mean(grad, axis=-1, keepdims=True)
    across = jnp.mean(grad * hat, axis=-1, keepdims=True)
    return rstd * (grad - along - hat * across)


def project_body(tok, w, small, kmask, qmask, normed_o, k_o, qt_o, vt_o, wqt, wvt, *, heads):
    half = heads * HEAD

    @pl.when(pl.program_id(0) == 0)
    def _():
        wqt[...] = w[:, :half].T
        wvt[...] = w[:, 2 * half :].T

    hat, _ = normalize(tok[...].astype(f32))
    normed = (hat * small[0:1] + small[1:2]).astype(bf16)
    normed_o[...] = normed
    keys = mm(normed, w[:, half : 2 * half], NN).astype(bf16)
    queries = (mm(wqt[...], normed, NT).astype(bf16).astype(f32) * (1.0 / math.sqrt(HEAD))).astype(bf16)
    values = mm(wvt[...], normed, NT).astype(bf16)
    rows = lax.broadcasted_iota(jnp.int32, (HEAD, tok.shape[0]), 0)
    ones = jnp.where(rows < 2, 1.0, 0.0).astype(bf16)
    for h in range(heads):
        part = slice(h * HEAD, (h + 1) * HEAD)
        k_o[h] = jnp.concatenate([keys[:, part], kmask[...]], axis=1)
        qt_o[h] = jnp.concatenate([queries[part], qmask[...]], axis=0)
        vt_o[h] = jnp.concatenate([values[part], ones], axis=0)


def project(tok, w, small, kmask, qmask, heads, block=512):
    length, width = tok.shape
    half = heads * HEAD
    return pl.pallas_call(
        functools.partial(project_body, heads=heads),
        grid=(length // block,),
        in_specs=[
            pl.BlockSpec((block, width), lambda i: (i, 0)),
            whole(width, 3 * half),
            whole(8, width),
            pl.BlockSpec((block, HEAD), lambda i: (i, 0)),
            pl.BlockSpec((HEAD, block), lambda i: (0, i)),
        ],
        out_specs=[
            pl.BlockSpec((block, width), lambda i: (i, 0)),
            pl.BlockSpec((heads, block, LANES), lambda i: (0, i, 0)),
            pl.BlockSpec((heads, LANES, block), lambda i: (0, 0, i)),
            pl.BlockSpec((heads, LANES, block), lambda i: (0, 0, i)),
        ],
        out_shape=[
            jax.ShapeDtypeStruct((length, width), bf16),
            jax.ShapeDtypeStruct((heads, length, LANES), bf16),
            jax.ShapeDtypeStruct((heads, LANES, length), bf16),
            jax.ShapeDtypeStruct((heads, LANES, length), bf16),
        ],
        scratch_shapes=[pltpu.VMEM((half, width), bf16), pltpu.VMEM((half, width), bf16)],
        compiler_params=params(),
        cost_estimate=cost(6 * length * width * half, 20 << 20),
        name="project",
    )(tok, w, small, kmask, qmask)


def attend_body(lo, hi, shift, k, qt, vt, mine_o, other_o, qa_o, acc, *, block, step, heads, depth):
    i = pl.program_id(0)
    count = k.shape[1] // step
    acc[...] = jnp.zeros_like(acc)

    def body(j, tops):
        at = lax.rem(j + shift[0], count)
        ks = pl.ds(pl.multiple_of(at * step, step), step)
        scores = [mm(k[h, ks, :], qt[h], NN) for h in range(heads)]
        now = [jnp.maximum(tops[h], jnp.max(scores[h], axis=0, keepdims=True)) for h in range(heads)]
        for h in range(heads):
            probs = jnp.exp(scores[h] - now[h]).astype(bf16)
            acc[h] = acc[h] * jnp.exp(tops[h] - now[h]) + mm(vt[h, :depth, ks], probs, NN)
        return tuple(now)

    tops = lax.fori_loop(
        lo[i], hi[i], body, tuple(jnp.full((1, block), LOWEST, f32) for _ in range(heads))
    )
    mixed = []
    row = lax.broadcasted_iota(jnp.int32, (16, block), 0)
    for h in range(heads):
        totals = acc[h, HEAD : HEAD + 1, :]
        mixed.append(acc[h, :HEAD, :] / totals)
        lse = tops[h] + jnp.log(totals)
        top = lse.astype(bf16).astype(f32)
        mid = (lse - top).astype(bf16).astype(f32)
        low = lse - top - mid
        tail = jnp.where(row == 0, top, jnp.where(row == 1, mid, jnp.where(row == 2, low, 0.0)))
        full = jnp.concatenate(
            [qt[h, :LSE_AT, :].astype(f32), tail, jnp.zeros((LANES - LSE_AT - 16, block), f32)], axis=0
        )
        qa_o[h] = full.T.astype(bf16)
    out = jnp.concatenate(mixed, axis=0).T.astype(bf16)
    own = pl.num_programs(0) // 2

    @pl.when(i < own)
    def _():
        mine_o[...] = out

    @pl.when(i >= own)
    def _():
        other_o[...] = out


def attend(lo, hi, shift, k, qt, vt, block, step):
    heads, length, _ = k.shape
    half = heads * HEAD
    count = length // block
    own = count // 2
    return pl.pallas_call(
        functools.partial(attend_body, block=block, step=step, heads=heads, depth=HEAD + 16),
        grid_spec=pltpu.PrefetchScalarGridSpec(
            num_scalar_prefetch=3,
            grid=(count,),
            in_specs=[
                whole(heads, length, LANES),
                pl.BlockSpec((heads, LANES, block), lambda i, *_: (0, 0, i)),
                whole(heads, LANES, length),
            ],
            out_specs=[
                pl.BlockSpec((block, half), lambda i, *_: (jnp.minimum(i, own - 1), 0)),
                pl.BlockSpec((block, half), lambda i, *_: (jnp.maximum(i - own, 0), 0)),
                pl.BlockSpec((heads, block, LANES), lambda i, *_: (0, i, 0)),
            ],
            scratch_shapes=[pltpu.VMEM((heads, HEAD + 16, block), f32)],
        ),
        out_shape=[
            jax.ShapeDtypeStruct((length // 2, half), bf16),
            jax.ShapeDtypeStruct((length // 2, half), bf16),
            jax.ShapeDtypeStruct((heads, length, LANES), bf16),
        ],
        compiler_params=params(),
        cost_estimate=cost(8 * heads * length * length * LANES, 20 << 20, heads * length * length),
        name="attend",
    )(lo, hi, shift, k, qt, vt)


def feed_body(
    tok, cot, mix_m, mix_o, w_m, w_o, small, bias, out_o, mid_o, do_m, do_o, gw_m, gw_o, gs_o, gb_o, acc_o, pick, *, heads, width, hid
):
    i = pl.program_id(0)
    half = heads * HEAD
    down = hid
    top = 2 * hid

    @pl.when(i == 0)
    def _():
        gw_m[...] = jnp.zeros_like(gw_m)
        acc_o[...] = jnp.zeros_like(acc_o)
        gs_o[...] = jnp.zeros_like(gs_o)
        gb_o[...] = jnp.zeros_like(gb_o)
        rows = lax.broadcasted_iota(jnp.int32, pick.shape, 0)
        cols = lax.broadcasted_iota(jnp.int32, pick.shape, 1)
        inside = (cols >= rows // HEAD * LANES + HEAD) & (cols < rows // HEAD * LANES + HEAD + 2)
        pick[...] = jnp.where(inside, 1.0, 0.0).astype(bf16)

    grad_top = cot[...]
    grad_top_f = grad_top.astype(f32)
    mixed = (mix_m[...], mix_o[...])
    weights = (w_m, w_o)
    branch = mm(mixed[0], w_m[:, top:], NT) + mm(mixed[1], w_o[:, top:], NT)
    middle = tok[...].astype(f32) + branch + small[4:5]
    hat, rstd = normalize(middle)
    normed = (hat * small[2:3] + small[3:4]).astype(bf16)
    result = middle + small[5:6]
    grad_normed = jnp.zeros_like(middle)
    for s in range(2):
        w = weights[s]
        pre = mm(normed, w[:, :hid], NN) + bias[:, s * hid : (s + 1) * hid]
        square = pre * pre
        slope = math.sqrt(2.0 / math.pi)
        bent = jnp.tanh(pre * (slope + slope * 0.044715 * square))
        gate = 0.5 + 0.5 * bent
        hidden = (pre * gate).astype(bf16)
        result = result + mm(hidden, w[:, down:top], NT)
        grad_hidden = mm(grad_top, w[:, down:top], NN)
        bend = (0.5 * pre) * (1.0 - bent * bent) * (slope + 3.0 * slope * 0.044715 * square)
        grad_pre = (grad_hidden * (gate + bend)).astype(bf16)
        gb_o[:, s * hid : (s + 1) * hid] += jnp.sum(grad_pre.astype(f32), axis=0, keepdims=True)
        gw = gw_m if s == 0 else acc_o
        gw[:, down:top] += mm(grad_top, hidden, TN)
        gw[:, :hid] += mm(normed, grad_pre, TN)
        grad_normed = grad_normed + mm(grad_pre, w[:, :hid], NT)
    out_o[...] = result.astype(bf16)
    grad_middle = grad_top_f + normalize_back(grad_normed * small[2:3], hat, rstd)
    mid_o[...] = grad_middle
    gs_o[...] += jnp.concatenate(
        [
            jnp.zeros((2, width), f32),
            jnp.sum(grad_normed * hat, axis=0, keepdims=True),
            jnp.sum(grad_normed, axis=0, keepdims=True),
            jnp.sum(grad_middle, axis=0, keepdims=True),
            jnp.sum(grad_top_f, axis=0, keepdims=True),
            jnp.zeros((2, width), f32),
        ],
        axis=0,
    )
    grad_branch = grad_middle.astype(bf16)
    lane = lax.broadcasted_iota(jnp.int32, (tok.shape[0], HEAD), 1)
    for s in range(2):
        gw = gw_m if s == 0 else acc_o
        gw[:, top:] += mm(grad_branch, mixed[s], TN)
        grad_mixed = mm(grad_branch, weights[s][:, top:], NN).astype(bf16)
        product = grad_mixed.astype(f32) * mixed[s].astype(f32)
        rough = product.astype(bf16)
        fine = (product - rough.astype(f32)).astype(bf16)
        inner = mm(rough, pick[...], NN) + mm(fine, pick[...], NN)
        out = do_m if s == 0 else do_o
        for h in range(heads):
            total = -inner[:, h * LANES + HEAD : (h + 1) * LANES]
            first = total.astype(bf16)
            rest = (total - first.astype(f32)).astype(bf16)
            tail = jnp.where(lane == 0, first.astype(f32), rest.astype(f32)).astype(bf16)
            out[h] = jnp.concatenate([grad_mixed[:, h * HEAD : (h + 1) * HEAD], tail], axis=1)

    @pl.when(i == pl.num_programs(0) - 1)
    def _():
        gw_o[...] = acc_o[...].astype(bf16)


def feed(tok, cot, mix_m, mix_o, w_m, w_o, small, bias, heads, block=256):
    length, width = tok.shape
    half = heads * HEAD
    cols = w_m.shape[1]
    hid = (cols - half) // 2
    by_rows = lambda n: pl.BlockSpec((block, n), lambda i: (i, 0))
    by_heads = pl.BlockSpec((heads, block, LANES), lambda i: (0, i, 0))
    return pl.pallas_call(
        functools.partial(feed_body, heads=heads, width=width, hid=hid),
        grid=(length // block,),
        in_specs=[
            by_rows(width),
            by_rows(width),
            by_rows(half),
            by_rows(half),
            whole(width, cols),
            whole(width, cols),
            whole(8, width),
            whole(1, 2 * hid),
        ],
        out_specs=[
            by_rows(width),
            by_rows(width),
            by_heads,
            by_heads,
            whole(width, cols),
            whole(width, cols),
            whole(8, width),
            whole(1, 2 * hid),
        ],
        out_shape=[
            jax.ShapeDtypeStruct((length, width), bf16),
            jax.ShapeDtypeStruct((length, width), f32),
            jax.ShapeDtypeStruct((heads, length, LANES), bf16),
            jax.ShapeDtypeStruct((heads, length, LANES), bf16),
            jax.ShapeDtypeStruct((width, cols), f32),
            jax.ShapeDtypeStruct((width, cols), bf16),
            jax.ShapeDtypeStruct((8, width), f32),
            jax.ShapeDtypeStruct((1, 2 * hid), f32),
        ],
        scratch_shapes=[pltpu.VMEM((width, cols), f32), pltpu.VMEM((half, heads * LANES), bf16)],
        compiler_params=params(),
        cost_estimate=cost(12 * length * width * cols, 40 << 20, length * 2 * hid),
        name="feed",
    )(tok, cot, mix_m, mix_o, w_m, w_o, small, bias)


def attend_back_body(
    lo, hi, shift, qa, k, qt, vt, do_m, do_o, dq_o, dk_o, dv_o, dk, dv, dq, do, dot, *, block, step, heads
):
    i = pl.program_id(0)
    count = k.shape[1] // step
    own = pl.num_programs(0) // 2

    @pl.when(i == 0)
    def _():
        dk[...] = jnp.zeros_like(dk)
        dv[...] = jnp.zeros_like(dv)

    @pl.when(i < own)
    def _():
        do[...] = do_m[...]

    @pl.when(i >= own)
    def _():
        do[...] = do_o[...]

    dq[...] = jnp.zeros_like(dq)
    for h in range(heads):
        dot[h] = do[h].T[:HEAD]

    def body(j, carry):
        at = lax.rem(j + shift[0], count)
        ks = pl.ds(pl.multiple_of(at * step, step), step)
        for h in range(heads):
            probs = jnp.exp(mm(qa[h], k[h, ks, :], NT))
            grad = (probs * mm(do[h], vt[h, :, ks], NN)).astype(bf16)
            dv[h, :, ks] += mm(dot[h], probs.astype(bf16), NN)
            dk[h, :, ks] += mm(qt[h, :HEAD, :], grad, NN)
            dq[h] += mm(grad, k[h, ks, :], NN)
        return carry

    lax.fori_loop(lo[i], hi[i], body, 0)
    scale = 1.0 / math.sqrt(HEAD)
    dq_o[...] = jnp.concatenate([dq[h][:, :HEAD] * scale for h in range(heads)], axis=1).astype(bf16)

    @pl.when(i == pl.num_programs(0) - 1)
    def _():
        for h in range(heads):
            dk_o[h * HEAD : (h + 1) * HEAD, :] = dk[h].astype(bf16)
            dv_o[h * HEAD : (h + 1) * HEAD, :] = dv[h].astype(bf16)


def attend_back(lo, hi, shift, qa, k, qt, vt, do_m, do_o, block, step):
    heads, length, _ = k.shape
    half = heads * HEAD
    count = length // block
    own = count // 2
    return pl.pallas_call(
        functools.partial(attend_back_body, block=block, step=step, heads=heads),
        grid_spec=pltpu.PrefetchScalarGridSpec(
            num_scalar_prefetch=3,
            grid=(count,),
            in_specs=[
                pl.BlockSpec((heads, block, LANES), lambda i, *_: (0, i, 0)),
                whole(heads, length, LANES),
                pl.BlockSpec((heads, LANES, block), lambda i, *_: (0, 0, i)),
                whole(heads, LANES, length),
                pl.BlockSpec((heads, block, LANES), lambda i, *_: (0, jnp.minimum(i, own - 1), 0)),
                pl.BlockSpec((heads, block, LANES), lambda i, *_: (0, jnp.maximum(i - own, 0), 0)),
            ],
            out_specs=[
                pl.BlockSpec((block, half), lambda i, *_: (i, 0)),
                whole(half, length),
                whole(half, length),
            ],
            scratch_shapes=[
                pltpu.VMEM((heads, HEAD, length), f32),
                pltpu.VMEM((heads, HEAD, length), f32),
                pltpu.VMEM((heads, block, LANES), f32),
                pltpu.VMEM((heads, block, LANES), bf16),
                pltpu.VMEM((heads, HEAD, block), bf16),
            ],
        ),
        out_shape=[
            jax.ShapeDtypeStruct((length, half), bf16),
            jax.ShapeDtypeStruct((half, length), bf16),
            jax.ShapeDtypeStruct((half, length), bf16),
        ],
        compiler_params=params(),
        cost_estimate=cost(20 * heads * length * length * LANES, 24 << 20, heads * length * length),
        name="attend_back",
    )(lo, hi, shift, qa, k, qt, vt, do_m, do_o)


def unproject_body(normed, dq, dk, dv, w, before, gw, gn):
    @pl.when(pl.program_id(0) == 0)
    def _():
        gw[...] = before[...]

    packed = jnp.concatenate([dq[...], dk[...].T, dv[...].T], axis=1)
    gw[...] += mm(normed[...], packed, TN)
    gn[...] = mm(packed, w[...], NT).astype(gn.dtype)


def unproject(normed, dq, dk, dv, w, before, first, dtype, block=512):
    length, width = normed.shape
    own = length // 2
    half = dq.shape[1]
    off = first // block
    return pl.pallas_call(
        unproject_body,
        grid=(own // block,),
        in_specs=[
            pl.BlockSpec((block, width), lambda i: (i + off, 0)),
            pl.BlockSpec((block, half), lambda i: (i + off, 0)),
            pl.BlockSpec((half, block), lambda i: (0, i + off)),
            pl.BlockSpec((half, block), lambda i: (0, i + off)),
            whole(width, 3 * half),
            whole(width, 3 * half),
        ],
        out_specs=[whole(width, 3 * half), pl.BlockSpec((block, width), lambda i: (i, 0))],
        out_shape=[
            jax.ShapeDtypeStruct((width, 3 * half), f32),
            jax.ShapeDtypeStruct((own, width), dtype),
        ],
        compiler_params=params(),
        cost_estimate=cost(12 * own * width * half, 12 << 20),
        name="unproject",
    )(normed, dq, dk, dv, w, before)


def finish_body(tok, gn_m, gn_o, mid, small, out, gs):
    @pl.when(pl.program_id(0) == 0)
    def _():
        gs[...] = jnp.zeros_like(gs)

    hat, rstd = normalize(tok[...].astype(f32))
    grad = gn_m[...] + gn_o[...].astype(f32)
    out[...] = (mid[...] + normalize_back(grad * small[0:1], hat, rstd)).astype(bf16)
    gs[...] += jnp.concatenate(
        [
            jnp.sum(grad * hat, axis=0, keepdims=True),
            jnp.sum(grad, axis=0, keepdims=True),
            jnp.zeros((6, grad.shape[1]), f32),
        ],
        axis=0,
    )


def finish(tok, gn_m, gn_o, mid, small, block=512):
    length, width = tok.shape
    rows = pl.BlockSpec((block, width), lambda i: (i, 0))
    return pl.pallas_call(
        finish_body,
        grid=(length // block,),
        in_specs=[rows, rows, rows, rows, whole(8, width)],
        out_specs=[rows, whole(8, width)],
        out_shape=[jax.ShapeDtypeStruct((length, width), bf16), jax.ShapeDtypeStruct((8, width), f32)],
        compiler_params=params(),
        cost_estimate=cost(0, 16 << 20),
        name="finish",
    )(tok, gn_m, gn_o, mid, small)


def adamw(weight, grad, first, second, rate, decay):
    first = BETA_ONE * first + (1.0 - BETA_ONE) * grad
    second = BETA_TWO * second + (1.0 - BETA_TWO) * grad * grad
    fixed_one = first / (1.0 - BETA_ONE**STEP)
    fixed_two = second / (1.0 - BETA_TWO**STEP)
    weight = weight - rate * (fixed_one / (jnp.sqrt(fixed_two) + ADAM_EPS) + decay * weight)
    return (weight, first, second)


def swap(values):
    return lax.ppermute(values, "dp", [(0, 1), (1, 0)])


def across(values, count, bit):
    return lax.ppermute(values, "fsdp", [(i, i ^ bit) for i in range(count)])


def gather(shard, count):
    if count & (count - 1):
        return lax.all_gather(shard, "fsdp", axis=0)
    me = lax.axis_index("fsdp")
    held = shard
    depth = 0
    bit = count // 2
    while bit:
        there = across(held, count, bit)
        above = (me & bit) != 0
        held = jnp.where(above, jnp.stack([there, held], axis=depth), jnp.stack([held, there], axis=depth))
        depth += 1
        bit //= 2
    return held.reshape((count,) + shard.shape)


def scatter_sum(blocks, count):
    if count > 16 or count & (count - 1):
        return jnp.sum(lax.all_to_all(blocks, "fsdp", 0, 0).astype(f32), axis=0)
    me = lax.axis_index("fsdp")
    total = lax.dynamic_index_in_dim(blocks, me, 0, keepdims=False).astype(f32)
    arrived = [
        across(lax.dynamic_index_in_dim(blocks, me ^ j, 0, keepdims=False), count, j)
        for j in range(1, count)
    ]
    for part in arrived:
        total = total + part.astype(f32)
    return total


def local(
    tokens,
    segments,
    cotangent,
    w_qkv,
    w_out,
    w_up,
    w_down,
    small_params,
    up_bias,
    first_qkv,
    first_out,
    first_up,
    first_down,
    first_small,
    first_bias,
    second_qkv,
    second_out,
    second_up,
    second_down,
    second_small,
    second_bias,
    *,
    count,
):
    own, width = tokens.shape[1:]
    length = segments.shape[1]
    heads = HEADS // 2
    half = heads * HEAD
    hid = w_up.shape[1] // 2
    cols = 2 * hid + half
    rows = w_qkv.shape[0]
    out_fan = max(1, width * (DOCS + 1) // length)
    rate_out = RATE_MATRIX * math.sqrt(width / out_fan)
    dp = lax.axis_index("dp")
    block, step = 512, 512

    def mine_of(values, axis):
        return lax.dynamic_index_in_dim(values, dp, axis, keepdims=False)

    def in_order(mine, other, axis):
        return jnp.where(
            dp == 0, jnp.stack([mine, other], axis=axis), jnp.stack([other, mine], axis=axis)
        )

    qkv_shard = mine_of(w_qkv.astype(bf16).reshape(rows, 3, 2, half), 2).reshape(rows, 3 * half)
    tiny = jnp.concatenate([small_params.T.reshape(-1), up_bias]).astype(bf16)
    w_one = gather(qkv_shard, count).reshape(width, 3 * half)
    tiny_all = gather(tiny, count).astype(f32)
    small = jnp.pad(tiny_all[:, : 6 * rows].reshape(width, 6).T, ((0, 2), (0, 0)))
    bias_all = tiny_all[:, 6 * rows :].reshape(1, 2, hid)
    bias = jnp.where(dp == 0, bias_all, bias_all[:, ::-1]).reshape(1, 2 * hid)
    rest_shard = jnp.concatenate(
        [
            mine_of(w_up.astype(bf16).reshape(rows, 2, hid), 1),
            mine_of(w_down.astype(bf16).reshape(2, hid, rows), 0).T,
            mine_of(w_out.astype(bf16).reshape(2, half, rows), 0).T,
        ],
        axis=1,
    )
    w_mine = lax.all_gather(rest_shard, "fsdp", axis=0, tiled=True)

    tok = tokens[0]
    tok_all = jnp.concatenate([tok, swap(tok)], axis=0)
    seg = segments[0]
    seg_here = jnp.where(dp == 0, seg, jnp.roll(seg, own))
    docs = jnp.arange(HEAD, dtype=jnp.int32)
    same = seg_here[:, None] == docs[None, :]
    lse_cols = ((docs >= LSE_AT - HEAD) & (docs < LSE_AT - HEAD + 3))[None, :]
    kmask = jnp.where(same & (docs <= DOCS), MASKED_SCORE, jnp.where(lse_cols, -1.0, 0.0)).astype(bf16)
    differs = (seg_here[None, :] != docs[:, None]) & (docs <= DOCS)[:, None]
    qmask = jnp.where(differs, 1.0, 0.0).astype(bf16)
    below = jnp.sum((seg[None, :] < seg_here[::block, None]).astype(jnp.int32), axis=1)
    until = jnp.sum((seg[None, :] <= seg_here[block - 1 :: block, None]).astype(jnp.int32), axis=1)
    lo = below // step
    hi = (until + step - 1) // step
    shift = (dp * (own // step)).astype(jnp.int32).reshape(1)

    normed, keys, queries_t, values_t = project(tok_all, w_one, small, kmask, qmask, heads)
    mix_m, mix_send, queries = attend(lo, hi, shift, keys, queries_t, values_t, block, step)
    mix_o = swap(mix_send)
    w_other = swap(w_mine)
    layer_out, grad_mid, do_m, do_send, gw_m, gw_send, gs_two, gb = feed(
        tok, cotangent[0], mix_m, mix_o, w_mine, w_other, small, bias, heads
    )
    do_o = swap(do_send)
    gw_pair = (gw_m + swap(gw_send).astype(f32)).astype(bf16)
    rest_grad = scatter_sum(gw_pair.reshape(count, rows, cols), count)
    dq, dk, dv = attend_back(lo, hi, shift, queries, keys, queries_t, values_t, do_m, do_o, block, step)
    zero = jnp.zeros((width, 3 * half), f32)
    gw_part, gn_send = unproject(normed, dq, dk, dv, w_one, zero, own, bf16)
    gn_o = swap(gn_send)
    gw_one, gn_m = unproject(normed, dq, dk, dv, w_one, gw_part, 0, f32)
    input_grad, gs_one = finish(tok, gn_m, gn_o, grad_mid, small)

    tiny_len = tiny.shape[0]
    wide = 3 * half
    lines = -(-tiny_len // wide)
    grad_small = (gs_one + gs_two)[:6].T.reshape(count, 6 * rows)
    gb_all = jnp.where(dp == 0, gb.reshape(2, hid), gb.reshape(2, hid)[::-1]).reshape(count, -1)
    grad_tiny = jnp.pad(
        jnp.concatenate([grad_small, gb_all], axis=1), ((0, 0), (0, lines * wide - tiny_len))
    ).reshape(count, lines, wide)
    last = jnp.concatenate([gw_one.reshape(count, rows, wide), grad_tiny], axis=1).astype(bf16)
    last_sum = jnp.sum(lax.all_to_all(last, "fsdp", 0, 0).astype(f32), axis=0)
    qkv_mine, tiny_mine = last_sum[:rows], last_sum[rows:].reshape(-1)[:tiny_len]
    qkv_other, tiny_other, rest_other = swap(qkv_mine), swap(tiny_mine), swap(rest_grad)

    own_qkv = in_order(qkv_mine.reshape(rows, 3, half), qkv_other.reshape(rows, 3, half), 2).reshape(rows, -1)
    own_up = in_order(rest_grad[:, :hid], rest_other[:, :hid], 1).reshape(rows, -1)
    own_down = in_order(rest_grad[:, hid : 2 * hid], rest_other[:, hid : 2 * hid], 1).reshape(rows, -1).T
    own_out = in_order(rest_grad[:, 2 * hid :], rest_other[:, 2 * hid :], 1).reshape(rows, -1).T
    tiny_sum = tiny_mine + tiny_other
    own_small = tiny_sum[: 6 * rows].reshape(rows, 6).T
    own_bias = tiny_sum[6 * rows :]
    local_squares = (
        jnp.sum(qkv_mine * qkv_mine)
        + jnp.sum(qkv_other * qkv_other)
        + jnp.sum(rest_grad * rest_grad)
        + jnp.sum(rest_other * rest_other)
        + jnp.sum(tiny_sum * tiny_sum)
    )
    local_squares = jnp.where(dp == 0, local_squares, swap(local_squares))
    spread = lax.all_to_all(jnp.broadcast_to(local_squares, (count, 1, LANES)), "fsdp", 0, 0)
    grad_norm = jnp.sqrt(jnp.sum(spread[:, 0, 0]))
    factor = jnp.minimum(1.0, CLIP_NORM / (grad_norm + 1e-06))
    new_qkv, new_first_qkv, new_second_qkv = adamw(
        w_qkv, own_qkv * factor, first_qkv, second_qkv, RATE_MATRIX, DECAY_MATRIX
    )
    new_out, new_first_out, new_second_out = adamw(
        w_out, own_out * factor, first_out, second_out, rate_out, DECAY_MATRIX
    )
    new_up, new_first_up, new_second_up = adamw(
        w_up, own_up * factor, first_up, second_up, RATE_MATRIX, DECAY_MATRIX
    )
    new_down, new_first_down, new_second_down = adamw(
        w_down, own_down * factor, first_down, second_down, RATE_MATRIX, DECAY_MATRIX
    )
    new_small, new_first_small, new_second_small = adamw(
        small_params, own_small * factor, first_small, second_small, RATE_VECTOR, 0.0
    )
    new_bias, new_first_bias, new_second_bias = adamw(
        up_bias, own_bias * factor, first_bias, second_bias, RATE_VECTOR, 0.0
    )
    return (
        layer_out[None],
        input_grad[None],
        grad_norm,
        new_qkv,
        new_out,
        new_up,
        new_down,
        new_small,
        new_bias,
        new_first_qkv,
        new_first_out,
        new_first_up,
        new_first_down,
        new_first_small,
        new_first_bias,
        new_second_qkv,
        new_second_out,
        new_second_up,
        new_second_down,
        new_second_small,
        new_second_bias,
    )


def solution(mesh):
    rows, cols, flat = P("fsdp", None), P(None, "fsdp"), P("fsdp")
    by_token = P("fsdp", "dp", None)
    weights = (rows, cols, rows, cols, cols, flat)
    in_specs = (by_token, rows, by_token) + 3 * weights
    out_specs = (by_token, by_token, P()) + 3 * weights
    body = functools.partial(local, count=mesh.shape["fsdp"])
    return jax.shard_map(body, mesh=mesh, in_specs=in_specs, out_specs=out_specs, check_vma=False)
```

```python
import functools
import math

import jax
import jax.numpy as jnp
from jax import lax
from jax.experimental import pallas as pl
from jax.experimental.pallas import tpu as pltpu
from jax.sharding import PartitionSpec as P

HEADS = 8
DOCS = 4
STEP = 10


LN_EPS = 1e-05
CLIP_NORM = 1.0
BETA_ONE = 0.9
BETA_TWO = 0.999
ADAM_EPS = 1e-08
RATE_MATRIX = 0.04
RATE_VECTOR = 0.5
DECAY_MATRIX = 0.1
MASKED_SCORE = -1e30
LOWEST = -3e38
SAFE_SCORE = 60.0

HEAD = 64
LANES = 128
SEG_AT = HEAD
LSE_AT = HEAD + 16
VMEM = 60 << 20

bf16 = jnp.bfloat16
f32 = jnp.float32
NN = (((1,), (0,)), ((), ()))
NT = (((1,), (1,)), ((), ()))
TN = (((0,), (0,)), ((), ()))


def mm(left, right, dims):
    return lax.dot_general(left, right, dims, preferred_element_type=f32)


def params():
    return pltpu.CompilerParams(vmem_limit_bytes=VMEM)


def whole(*shape):
    return pl.BlockSpec(shape, lambda i, *_: (0,) * len(shape))


def cost(flops, nbytes, trans=0):
    return pl.CostEstimate(flops=int(flops), bytes_accessed=int(nbytes), transcendentals=int(trans))


def normalize(values):
    centre = jnp.mean(values, axis=-1, keepdims=True)
    centered = values - centre
    spread = jnp.mean(centered * centered, axis=-1, keepdims=True)
    rstd = lax.rsqrt(spread + LN_EPS)
    return centered * rstd, rstd


def normalize_back(grad, hat, rstd):
    along = jnp.mean(grad, axis=-1, keepdims=True)
    across = jnp.mean(grad * hat, axis=-1, keepdims=True)
    return rstd * (grad - along - hat * across)


def project_body(tok_m, tok_o, w, small, seg, normed_o, k_o, qt_o, vt_o, qtop_o, ktop_o, wqt, wvt, pick, *, heads):
    half = heads * HEAD
    i = pl.program_id(0)
    size = tok_m.shape[0]

    @pl.when(i == 0)
    def _():
        wqt[...] = w[:, :half].T
        wvt[...] = w[:, 2 * half :].T
        rows = lax.broadcasted_iota(jnp.int32, pick.shape, 0)
        cols = lax.broadcasted_iota(jnp.int32, pick.shape, 1)
        pick[...] = jnp.where(rows // HEAD == cols, 1.0, 0.0).astype(bf16)
        qtop_o[...] = jnp.zeros_like(qtop_o)
        ktop_o[...] = jnp.zeros_like(ktop_o)

    tok = jnp.where(i < pl.num_programs(0) // 2, tok_m[...], tok_o[...])
    hat, _ = normalize(tok.astype(f32))
    normed = (hat * small[0:1] + small[1:2]).astype(bf16)
    normed_o[...] = normed
    keys = mm(normed, w[:, half : 2 * half], NN).astype(bf16)
    queries = mm(wqt[...], normed, NT).astype(bf16).astype(f32) * (1.0 / math.sqrt(HEAD))
    values = mm(wvt[...], normed, NT).astype(bf16)
    rows = lax.broadcasted_iota(jnp.int32, (HEAD, size), 0)
    ones = jnp.where(rows < 2, 1.0, 0.0).astype(bf16)
    known = rows <= DOCS
    same = rows == seg[...]
    qmask = jnp.where(known & ~same, 1.0, 0.0).astype(bf16)
    lse_rows = (rows >= LSE_AT - HEAD) & (rows < LSE_AT - HEAD + 3)
    kmask = jnp.where(known & same, MASKED_SCORE, jnp.where(lse_rows, -1.0, 0.0)).T.astype(bf16)
    keys_f = keys.astype(f32)
    lengths = mm((keys_f * keys_f).astype(bf16), pick[...], NN)
    ktop_o[0:1] = jnp.maximum(ktop_o[0:1], jnp.max(lengths, axis=0, keepdims=True))
    for h in range(heads):
        part = slice(h * HEAD, (h + 1) * HEAD)
        qtop_o[h : h + 1] = jnp.maximum(
            qtop_o[h : h + 1], jnp.sum(queries[part] * queries[part], axis=0, keepdims=True)
        )
        k_o[h] = jnp.concatenate([keys[:, part], kmask], axis=1)
        qt_o[h] = jnp.concatenate([queries[part].astype(bf16), qmask], axis=0)
        vt_o[h] = jnp.concatenate([values[part], ones], axis=0)


def project(tok_m, tok_o, w, small, seg, heads, block=512):
    own, width = tok_m.shape
    length = 2 * own
    half = heads * HEAD
    steps = own // block
    return pl.pallas_call(
        functools.partial(project_body, heads=heads),
        grid=(2 * steps,),
        in_specs=[
            pl.BlockSpec((block, width), lambda i: (jnp.minimum(i, steps - 1), 0)),
            pl.BlockSpec((block, width), lambda i: (jnp.maximum(i - steps, 0), 0)),
            whole(width, 3 * half),
            whole(8, width),
            pl.BlockSpec((1, block), lambda i: (0, i)),
        ],
        out_specs=[
            pl.BlockSpec((block, width), lambda i: (i, 0)),
            pl.BlockSpec((heads, block, LANES), lambda i: (0, i, 0)),
            pl.BlockSpec((heads, LANES, block), lambda i: (0, 0, i)),
            pl.BlockSpec((heads, LANES, block), lambda i: (0, 0, i)),
            whole(8, block),
            whole(8, LANES),
        ],
        out_shape=[
            jax.ShapeDtypeStruct((length, width), bf16),
            jax.ShapeDtypeStruct((heads, length, LANES), bf16),
            jax.ShapeDtypeStruct((heads, LANES, length), bf16),
            jax.ShapeDtypeStruct((heads, LANES, length), bf16),
            jax.ShapeDtypeStruct((8, block), f32),
            jax.ShapeDtypeStruct((8, LANES), f32),
        ],
        scratch_shapes=[
            pltpu.VMEM((half, width), bf16),
            pltpu.VMEM((half, width), bf16),
            pltpu.VMEM((half, LANES), bf16),
        ],
        compiler_params=params(),
        cost_estimate=cost(6 * length * width * half, 20 << 20),
        name="project",
    )(tok_m, tok_o, w, small, seg)


def tiles(lo, hi, shift, count, block, step):
    def after(q, k):
        last = k + 1 >= hi[q]
        q_next = jnp.where(last, q + 1, q)
        return q_next, jnp.where(last, lo[q_next], k + 1)

    def slices(q, k):
        at = lax.rem(k + shift[0], count)
        return pl.ds(pl.multiple_of(q * block, block), block), pl.ds(pl.multiple_of(at * step, step), step)

    return (jnp.int32(0), lo[0]), after, slices


def run_tiles(n, first, after, fill, use):
    @pl.when(n > 0)
    def _():
        fill(0, *first)

        def pair(_, at):
            mid = after(*at)
            end = after(*mid)
            use(0, *at)
            fill(1, *mid)
            use(1, *mid)
            fill(0, *end)
            return end

        at = lax.fori_loop(0, (n - 1) // 2, pair, first)

        @pl.when(n % 2 == 1)
        def _():
            use(0, *at)

        @pl.when(n % 2 == 0)
        def _():
            mid = after(*at)
            fill(1, *mid)
            use(0, *at)
            use(1, *mid)


def attend_body(
    lo, hi, n, shift, k, qt, vt, qtop, ktop, mine_o, other_o, qa_o, acc, top, slot_a, slot_b, *, block, step, heads, depth
):
    length = k.shape[1]
    own = length // 2
    acc[...] = jnp.zeros_like(acc)
    first, after, slices = tiles(lo, hi, shift, length // step, block, step)
    slots = (slot_a, slot_b)

    def fill(s, q, kk):
        qs, ks = slices(q, kk)
        for h in range(heads):
            slots[s][h] = jnp.exp(mm(k[h, ks, :], qt[h, :, qs], NN)).astype(bf16)

    def use(s, q, kk):
        qs, ks = slices(q, kk)
        for h in range(heads):
            acc[h, :, qs] += mm(vt[h, :depth, ks], slots[s][h], NN)

    def careful(_, at):
        qs, ks = slices(*at)
        for h in range(heads):
            score = mm(k[h, ks, :], qt[h, :, qs], NN)
            old = top[h : h + 1, qs]
            now = jnp.maximum(old, jnp.max(score, axis=0, keepdims=True))
            probs = jnp.exp(score - now).astype(bf16)
            acc[h, :, qs] = acc[h, :, qs] * jnp.exp(old - now) + mm(vt[h, :depth, ks], probs, NN)
            top[h : h + 1, qs] = now
        return after(*at)

    small = jnp.max(qtop[...]) * jnp.max(ktop[...]) <= SAFE_SCORE * SAFE_SCORE
    top[...] = jnp.where(small, 0.0, LOWEST) + jnp.zeros_like(top)
    run_tiles(jnp.where(small, n[0], 0), first, after, fill, use)
    lax.fori_loop(0, jnp.where(small, 0, n[0]), careful, first)

    wide = 512
    row = lax.broadcasted_iota(jnp.int32, (16, wide), 0)
    for part, out in ((0, mine_o), (1, other_o)):

        def finish(i, carry):
            at = pl.ds(pl.multiple_of(i * wide, wide), wide)
            qs = pl.ds(pl.multiple_of(i * wide + part * own, wide), wide)
            mixed = []
            for h in range(heads):
                totals = acc[h, HEAD : HEAD + 1, qs]
                mixed.append((acc[h, :HEAD, qs] / totals).astype(bf16))
                lse = top[h : h + 1, qs] + jnp.log(totals)
                one = lse.astype(bf16).astype(f32)
                two = (lse - one).astype(bf16).astype(f32)
                three = lse - one - two
                tail = jnp.where(row == 0, one, jnp.where(row == 1, two, jnp.where(row == 2, three, 0.0)))
                rest = jnp.zeros((LANES - LSE_AT - 16, wide), bf16)
                full = jnp.concatenate([qt[h, :LSE_AT, qs], tail.astype(bf16), rest], axis=0)
                qa_o[h, qs, :] = full.T
            out[at, :] = jnp.concatenate(mixed, axis=0).T
            return carry

        lax.fori_loop(0, own // wide, finish, 0)


IN_VMEM = pl.BlockSpec(memory_space=pltpu.VMEM)
IN_SMEM = pl.BlockSpec(memory_space=pltpu.SMEM)


def attend(lo, hi, n, shift, k, qt, vt, qtop, ktop, block, step):
    heads, length, _ = k.shape
    half = heads * HEAD
    depth = HEAD + 16
    return pl.pallas_call(
        functools.partial(attend_body, block=block, step=step, heads=heads, depth=depth),
        in_specs=[IN_SMEM] * 4 + [IN_VMEM] * 5,
        out_specs=[IN_VMEM] * 3,
        scratch_shapes=[
            pltpu.VMEM((heads, depth, length), f32),
            pltpu.VMEM((8, length), f32),
            pltpu.VMEM((heads, step, block), bf16),
            pltpu.VMEM((heads, step, block), bf16),
        ],
        out_shape=[
            jax.ShapeDtypeStruct((length // 2, half), bf16),
            jax.ShapeDtypeStruct((length // 2, half), bf16),
            jax.ShapeDtypeStruct((heads, length, LANES), bf16),
        ],
        compiler_params=params(),
        cost_estimate=cost(8 * heads * length * length * LANES, 20 << 20, heads * length * length),
        name="attend",
    )(lo, hi, n, shift, k, qt, vt, qtop, ktop)


def feed_body(
    who, tok, cot, mix_m, mix_o, w_m, w_o, small, bias, out_o, mid_o, do_m, do_o, gw_m, gw_o, gs_o, gb_o, acc_m, acc_o, pick, *, heads, width, hid
):
    i = pl.program_id(0)
    half = heads * HEAD
    down = hid
    top = 2 * hid

    @pl.when(i == 0)
    def _():
        acc_m[...] = jnp.zeros_like(acc_m)
        acc_o[...] = jnp.zeros_like(acc_o)
        gs_o[...] = jnp.zeros_like(gs_o)
        gb_o[...] = jnp.zeros_like(gb_o)
        rows = lax.broadcasted_iota(jnp.int32, pick.shape, 0)
        cols = lax.broadcasted_iota(jnp.int32, pick.shape, 1)
        inside = (cols >= rows // HEAD * LANES + HEAD) & (cols < rows // HEAD * LANES + HEAD + 2)
        pick[...] = jnp.where(inside, 1.0, 0.0).astype(bf16)

    grad_top = cot[...]
    grad_top_f = grad_top.astype(f32)
    mixed = (mix_m[...], mix_o[...])

    def weight(s, first, last):
        part = (w_m, w_o)[s][:, 0, :, first:last]
        return part.reshape(width, last - first)

    last = top + half
    branch = mm(mixed[0], weight(0, top, last), NT) + mm(mixed[1], weight(1, top, last), NT)
    middle = tok[...].astype(f32) + branch + small[4:5]
    hat, rstd = normalize(middle)
    normed = (hat * small[2:3] + small[3:4]).astype(bf16)
    result = middle + small[5:6]
    grad_normed = jnp.zeros_like(middle)
    for s in range(2):
        w_up = weight(s, 0, hid)
        w_down = weight(s, down, top)
        pre = mm(normed, w_up, NN) + bias[:, s * hid : (s + 1) * hid]
        square = pre * pre
        slope = math.sqrt(2.0 / math.pi)
        bent = jnp.tanh(pre * (slope + slope * 0.044715 * square))
        gate = 0.5 + 0.5 * bent
        hidden = (pre * gate).astype(bf16)
        result = result + mm(hidden, w_down, NT)
        grad_hidden = mm(grad_top, w_down, NN)
        bend = (0.5 * pre) * (1.0 - bent * bent) * (slope + 3.0 * slope * 0.044715 * square)
        grad_pre = (grad_hidden * (gate + bend)).astype(bf16)
        gb_o[:, s * hid : (s + 1) * hid] += jnp.sum(grad_pre.astype(f32), axis=0, keepdims=True)
        gw = acc_m if s == 0 else acc_o
        gw[:, down:top] += mm(grad_top, hidden, TN)
        gw[:, :hid] += mm(normed, grad_pre, TN)
        grad_normed = grad_normed + mm(grad_pre, w_up, NT)
    out_o[...] = result.astype(bf16)
    grad_middle = grad_top_f + normalize_back(grad_normed * small[2:3], hat, rstd)
    mid_o[...] = grad_middle
    gs_o[...] += jnp.concatenate(
        [
            jnp.zeros((2, width), f32),
            jnp.sum(grad_normed * hat, axis=0, keepdims=True),
            jnp.sum(grad_normed, axis=0, keepdims=True),
            jnp.sum(grad_middle, axis=0, keepdims=True),
            jnp.sum(grad_top_f, axis=0, keepdims=True),
            jnp.zeros((2, width), f32),
        ],
        axis=0,
    )
    grad_branch = grad_middle.astype(bf16)
    lane = lax.broadcasted_iota(jnp.int32, (tok.shape[0], HEAD), 1)
    for s in range(2):
        gw = acc_m if s == 0 else acc_o
        gw[:, top:] += mm(grad_branch, mixed[s], TN)
        grad_mixed = mm(grad_branch, weight(s, top, last), NN).astype(bf16)
        product = grad_mixed.astype(f32) * mixed[s].astype(f32)
        rough = product.astype(bf16)
        fine = (product - rough.astype(f32)).astype(bf16)
        inner = mm(rough, pick[...], NN) + mm(fine, pick[...], NN)
        out = do_m if s == 0 else do_o
        for h in range(heads):
            total = -inner[:, h * LANES + HEAD : (h + 1) * LANES]
            first = total.astype(bf16)
            rest = (total - first.astype(f32)).astype(bf16)
            tail = jnp.where(lane == 0, first.astype(f32), rest.astype(f32)).astype(bf16)
            out[h] = jnp.concatenate([grad_mixed[:, h * HEAD : (h + 1) * HEAD], tail], axis=1)

    @pl.when(i == pl.num_programs(0) - 1)
    def _():
        gw_m[...] = acc_m[...].astype(bf16)
        gw_o[...] = acc_o[...].astype(bf16)


def feed(who, tok, cot, mix_m, mix_o, weights, small, bias, heads, block=256):
    length, width = tok.shape
    half = heads * HEAD
    outer, _, inner, cols = weights.shape
    hid = (cols - half) // 2
    by_rows = lambda n: pl.BlockSpec((block, n), lambda i, *_: (i, 0))
    by_heads = pl.BlockSpec((heads, block, LANES), lambda i, *_: (0, i, 0))
    return pl.pallas_call(
        functools.partial(feed_body, heads=heads, width=width, hid=hid),
        grid_spec=pltpu.PrefetchScalarGridSpec(
            num_scalar_prefetch=1,
            grid=(length // block,),
            in_specs=[
                by_rows(width),
                by_rows(width),
                by_rows(half),
                by_rows(half),
                pl.BlockSpec((outer, 1, inner, cols), lambda i, who: (0, who[0], 0, 0)),
                pl.BlockSpec((outer, 1, inner, cols), lambda i, who: (0, 1 - who[0], 0, 0)),
                whole(8, width),
                whole(1, 2 * hid),
            ],
            out_specs=[
                by_rows(width),
                by_rows(width),
                by_heads,
                by_heads,
                whole(width, cols),
                whole(width, cols),
                whole(8, width),
                whole(1, 2 * hid),
            ],
            scratch_shapes=[
                pltpu.VMEM((width, cols), f32),
                pltpu.VMEM((width, cols), f32),
                pltpu.VMEM((half, heads * LANES), bf16),
            ],
        ),
        out_shape=[
            jax.ShapeDtypeStruct((length, width), bf16),
            jax.ShapeDtypeStruct((length, width), f32),
            jax.ShapeDtypeStruct((heads, length, LANES), bf16),
            jax.ShapeDtypeStruct((heads, length, LANES), bf16),
            jax.ShapeDtypeStruct((width, cols), bf16),
            jax.ShapeDtypeStruct((width, cols), bf16),
            jax.ShapeDtypeStruct((8, width), f32),
            jax.ShapeDtypeStruct((1, 2 * hid), f32),
        ],
        compiler_params=params(),
        cost_estimate=cost(12 * length * width * cols, 40 << 20, length * 2 * hid),
        name="feed",
    )(who, tok, cot, mix_m, mix_o, weights, weights, small, bias)


def attend_back_body(
    lo, hi, n, shift, qa, k, qt, vt, do_m, do_o, dq_o, dk_o, dv_o, dk, dv, dq, do, dot, pa, pb, ga, gb, *, block, step, heads
):
    length = k.shape[1]
    own = length // 2
    wide = 512
    dk[...] = jnp.zeros_like(dk)
    dv[...] = jnp.zeros_like(dv)
    dq[...] = jnp.zeros_like(dq)
    for part, source in ((0, do_m), (1, do_o)):

        def begin(i, carry):
            at = pl.ds(pl.multiple_of(i * wide, wide), wide)
            qs = pl.ds(pl.multiple_of(i * wide + part * own, wide), wide)
            for h in range(heads):
                grad = source[h, at, :]
                do[h, qs, :] = grad
                dot[h, :, qs] = grad.T[:HEAD]
            return carry

        lax.fori_loop(0, own // wide, begin, 0)
    first, after, slices = tiles(lo, hi, shift, length // step, block, step)
    probs_at, grads_at = (pa, pb), (ga, gb)

    def fill(s, q, kk):
        qs, ks = slices(q, kk)
        for h in range(heads):
            probs = jnp.exp(mm(qa[h, qs, :], k[h, ks, :], NT))
            probs_at[s][h] = probs.astype(bf16)
            grads_at[s][h] = (probs * mm(do[h, qs, :], vt[h, :, ks], NN)).astype(bf16)

    def use(s, q, kk):
        qs, ks = slices(q, kk)
        for h in range(heads):
            dv[h, :, ks] += mm(dot[h, :, qs], probs_at[s][h], NN)
            dk[h, :, ks] += mm(qt[h, :HEAD, qs], grads_at[s][h], NN)
            dq[h, qs, :] += mm(grads_at[s][h], k[h, ks, :], NN)

    run_tiles(n[0], first, after, fill, use)
    scale = 1.0 / math.sqrt(HEAD)

    def finish(i, carry):
        qs = pl.ds(pl.multiple_of(i * wide, wide), wide)
        dq_o[qs, :] = jnp.concatenate([dq[h, qs, :][:, :HEAD] * scale for h in range(heads)], axis=1).astype(bf16)
        return carry

    lax.fori_loop(0, length // wide, finish, 0)
    for h in range(heads):
        dk_o[h * HEAD : (h + 1) * HEAD, :] = dk[h].astype(bf16)
        dv_o[h * HEAD : (h + 1) * HEAD, :] = dv[h].astype(bf16)


def attend_back(lo, hi, n, shift, qa, k, qt, vt, do_m, do_o, block, step):
    heads, length, _ = k.shape
    half = heads * HEAD
    return pl.pallas_call(
        functools.partial(attend_back_body, block=block, step=step, heads=heads),
        in_specs=[IN_SMEM] * 4 + [IN_VMEM] * 6,
        out_specs=[IN_VMEM] * 3,
        scratch_shapes=[
            pltpu.VMEM((heads, HEAD, length), f32),
            pltpu.VMEM((heads, HEAD, length), f32),
            pltpu.VMEM((heads, length, LANES), f32),
            pltpu.VMEM((heads, length, LANES), bf16),
            pltpu.VMEM((heads, HEAD, length), bf16),
        ]
        + [pltpu.VMEM((heads, block, step), bf16)] * 4,
        out_shape=[
            jax.ShapeDtypeStruct((length, half), bf16),
            jax.ShapeDtypeStruct((half, length), bf16),
            jax.ShapeDtypeStruct((half, length), bf16),
        ],
        compiler_params=params(),
        cost_estimate=cost(20 * heads * length * length * LANES, 24 << 20, heads * length * length),
        name="attend_back",
    )(lo, hi, n, shift, qa, k, qt, vt, do_m, do_o)


def unproject_body(normed, dq, dk, dv, w, before, gw, gn):
    @pl.when(pl.program_id(0) == 0)
    def _():
        gw[...] = before[...]

    packed = jnp.concatenate([dq[...], dk[...].T, dv[...].T], axis=1)
    gw[...] += mm(normed[...], packed, TN)
    gn[...] = mm(packed, w[...], NT).astype(gn.dtype)


def unproject(normed, dq, dk, dv, w, before, first, dtype, block=512):
    length, width = normed.shape
    own = length // 2
    half = dq.shape[1]
    off = first // block
    return pl.pallas_call(
        unproject_body,
        grid=(own // block,),
        in_specs=[
            pl.BlockSpec((block, width), lambda i: (i + off, 0)),
            pl.BlockSpec((block, half), lambda i: (i + off, 0)),
            pl.BlockSpec((half, block), lambda i: (0, i + off)),
            pl.BlockSpec((half, block), lambda i: (0, i + off)),
            whole(width, 3 * half),
            whole(width, 3 * half),
        ],
        out_specs=[whole(width, 3 * half), pl.BlockSpec((block, width), lambda i: (i, 0))],
        out_shape=[
            jax.ShapeDtypeStruct((width, 3 * half), f32),
            jax.ShapeDtypeStruct((own, width), dtype),
        ],
        compiler_params=params(),
        cost_estimate=cost(12 * own * width * half, 12 << 20),
        name="unproject",
    )(normed, dq, dk, dv, w, before)


def finish_body(tok, gn_m, gn_o, mid, small, out, gs):
    @pl.when(pl.program_id(0) == 0)
    def _():
        gs[...] = jnp.zeros_like(gs)

    hat, rstd = normalize(tok[...].astype(f32))
    grad = gn_m[...] + gn_o[...].astype(f32)
    out[...] = (mid[...] + normalize_back(grad * small[0:1], hat, rstd)).astype(bf16)
    gs[...] += jnp.concatenate(
        [
            jnp.sum(grad * hat, axis=0, keepdims=True),
            jnp.sum(grad, axis=0, keepdims=True),
            jnp.zeros((6, grad.shape[1]), f32),
        ],
        axis=0,
    )


def finish(tok, gn_m, gn_o, mid, small, block=512):
    length, width = tok.shape
    rows = pl.BlockSpec((block, width), lambda i: (i, 0))
    return pl.pallas_call(
        finish_body,
        grid=(length // block,),
        in_specs=[rows, rows, rows, rows, whole(8, width)],
        out_specs=[rows, whole(8, width)],
        out_shape=[jax.ShapeDtypeStruct((length, width), bf16), jax.ShapeDtypeStruct((8, width), f32)],
        compiler_params=params(),
        cost_estimate=cost(0, 16 << 20),
        name="finish",
    )(tok, gn_m, gn_o, mid, small)


def adamw(weight, grad, first, second, rate, decay):
    first = BETA_ONE * first + (1.0 - BETA_ONE) * grad
    second = BETA_TWO * second + (1.0 - BETA_TWO) * grad * grad
    fixed_one = first / (1.0 - BETA_ONE**STEP)
    fixed_two = second / (1.0 - BETA_TWO**STEP)
    weight = weight - rate * (fixed_one / (jnp.sqrt(fixed_two) + ADAM_EPS) + decay * weight)
    return (weight, first, second)


def swap(values):
    return lax.ppermute(values, "dp", [(0, 1), (1, 0)])


def across(values, count, bit):
    return lax.ppermute(values, "fsdp", [(i, i ^ bit) for i in range(count)])


def gather(shard, count):
    if count & (count - 1):
        return lax.all_gather(shard, "fsdp", axis=0)
    me = lax.axis_index("fsdp")
    held = shard
    depth = 0
    bit = count // 2
    while bit:
        there = across(held, count, bit)
        above = (me & bit) != 0
        held = jnp.where(above, jnp.stack([there, held], axis=depth), jnp.stack([held, there], axis=depth))
        depth += 1
        bit //= 2
    return held.reshape((count,) + shard.shape)


def local(
    tokens,
    segments,
    cotangent,
    w_qkv,
    w_out,
    w_up,
    w_down,
    small_params,
    up_bias,
    first_qkv,
    first_out,
    first_up,
    first_down,
    first_small,
    first_bias,
    second_qkv,
    second_out,
    second_up,
    second_down,
    second_small,
    second_bias,
    *,
    count,
):
    own, width = tokens.shape[1:]
    length = segments.shape[1]
    heads = HEADS // 2
    half = heads * HEAD
    hid = w_up.shape[1] // 2
    cols = 2 * hid + half
    rows = w_qkv.shape[0]
    out_fan = max(1, width * (DOCS + 1) // length)
    rate_out = RATE_MATRIX * math.sqrt(width / out_fan)
    dp = lax.axis_index("dp")
    block, step = 256, 512

    def mine_of(values, axis):
        return lax.dynamic_index_in_dim(values, dp, axis, keepdims=False)

    def in_order(mine, other, axis):
        return jnp.where(
            dp == 0, jnp.stack([mine, other], axis=axis), jnp.stack([other, mine], axis=axis)
        )

    wide = 3 * half
    tiny_len = 6 * rows + up_bias.shape[0]
    lines = -(-tiny_len // wide)
    qkv_shard = mine_of(w_qkv.reshape(rows, 3, 2, half), 2).reshape(rows, wide)
    tiny = jnp.concatenate([small_params.T.reshape(-1), up_bias])
    tiny = jnp.pad(tiny, (0, lines * wide - tiny_len)).reshape(lines, wide)
    first_all = gather(jnp.concatenate([qkv_shard, tiny], axis=0).astype(bf16), count)
    w_one = first_all[:, :rows].reshape(width, wide)
    tiny_all = first_all[:, rows:].reshape(count, -1)[:, :tiny_len].astype(f32)
    small = jnp.pad(tiny_all[:, : 6 * rows].reshape(width, 6).T, ((0, 2), (0, 0)))
    bias_all = tiny_all[:, 6 * rows :].reshape(1, 2, hid)
    bias = jnp.where(dp == 0, bias_all, bias_all[:, ::-1]).reshape(1, 2 * hid)
    rest_shard = jnp.concatenate(
        [
            mine_of(w_up.reshape(rows, 2, hid), 1),
            mine_of(w_down.reshape(2, hid, rows), 0).T,
            mine_of(w_out.reshape(2, half, rows), 0).T,
        ],
        axis=1,
    ).astype(bf16)
    rest_shard, w_one = lax.optimization_barrier((rest_shard, w_one))
    rest_all = lax.all_gather(rest_shard, ("fsdp", "dp"), axis=0).reshape(count, 2, rows, cols)
    if rows % 16:
        rest_all = rest_all.transpose(1, 0, 2, 3).reshape(1, 2, width, cols)

    tok = tokens[0]
    tok_other = swap(tok)
    seg = segments[0]
    seg_here = jnp.where(dp == 0, seg, jnp.roll(seg, own))
    below = jnp.sum((seg[None, :] < seg_here[::block, None]).astype(jnp.int32), axis=1)
    until = jnp.sum((seg[None, :] <= seg_here[block - 1 :: block, None]).astype(jnp.int32), axis=1)
    lo = below // step
    hi = (until + step - 1) // step
    n = jnp.sum(hi - lo).reshape(1)
    shift = (dp * (own // step)).astype(jnp.int32).reshape(1)
    who = dp.astype(jnp.int32).reshape(1)

    normed, keys, queries_t, values_t, qtop, ktop = project(tok, tok_other, w_one, small, seg_here[None], heads)
    mix_m, mix_send, queries = attend(lo, hi, n, shift, keys, queries_t, values_t, qtop, ktop, block, step)
    mix_o = swap(mix_send)
    layer_out, grad_mid, do_m, do_send, gw_m, gw_send, gs_two, gb = feed(
        who, tok, cotangent[0], mix_m, mix_o, rest_all, small, bias, heads
    )
    gw_pair = (gw_m.astype(f32) + swap(gw_send).astype(f32)).astype(bf16)
    do_o, gw_pair = lax.optimization_barrier((swap(do_send), gw_pair))
    arrived = lax.all_to_all(gw_pair.reshape(count, rows, cols), "fsdp", 0, 0)
    dq, dk, dv = attend_back(lo, hi, n, shift, queries, keys, queries_t, values_t, do_m, do_o, block, step)
    dq, arrived = lax.optimization_barrier((dq, arrived))
    rest_grad = jnp.sum(arrived.astype(f32), axis=0)
    zero = jnp.zeros((width, wide), f32)
    gw_part, gn_send = unproject(normed, dq, dk, dv, w_one, zero, own, bf16)
    gn_o = swap(gn_send)
    gw_one, gn_m = unproject(normed, dq, dk, dv, w_one, gw_part, 0, f32)
    input_grad, gs_one = finish(tok, gn_m, gn_o, grad_mid, small)

    grad_small = (gs_one + gs_two)[:6].T.reshape(count, 6 * rows)
    gb_all = jnp.where(dp == 0, gb.reshape(2, hid), gb.reshape(2, hid)[::-1]).reshape(count, -1)
    grad_tiny = jnp.pad(
        jnp.concatenate([grad_small, gb_all], axis=1), ((0, 0), (0, lines * wide - tiny_len))
    ).reshape(count, lines, wide)
    last = jnp.concatenate([gw_one.reshape(count, rows, wide), grad_tiny], axis=1).astype(bf16)
    last_sum = jnp.sum(lax.all_to_all(last, "fsdp", 0, 0).astype(f32), axis=0)
    qkv_mine, tiny_mine = last_sum[:rows], last_sum[rows:].reshape(-1)[:tiny_len]
    qkv_other, tiny_other, rest_other = swap(qkv_mine), swap(tiny_mine), swap(rest_grad)

    own_qkv = in_order(qkv_mine.reshape(rows, 3, half), qkv_other.reshape(rows, 3, half), 2).reshape(rows, -1)
    own_up = in_order(rest_grad[:, :hid], rest_other[:, :hid], 1).reshape(rows, -1)
    own_down = in_order(rest_grad[:, hid : 2 * hid], rest_other[:, hid : 2 * hid], 1).reshape(rows, -1).T
    own_out = in_order(rest_grad[:, 2 * hid :], rest_other[:, 2 * hid :], 1).reshape(rows, -1).T
    tiny_sum = tiny_mine + tiny_other
    own_small = tiny_sum[: 6 * rows].reshape(rows, 6).T
    own_bias = tiny_sum[6 * rows :]
    local_squares = (
        jnp.sum(qkv_mine * qkv_mine)
        + jnp.sum(qkv_other * qkv_other)
        + jnp.sum(rest_grad * rest_grad)
        + jnp.sum(rest_other * rest_other)
        + jnp.sum(tiny_sum * tiny_sum)
    )
    local_squares = jnp.where(dp == 0, local_squares, swap(local_squares))
    spread = lax.all_to_all(jnp.broadcast_to(local_squares, (count, 1, LANES)), "fsdp", 0, 0)
    grad_norm = jnp.sqrt(jnp.sum(spread[:, 0, 0]))
    factor = jnp.minimum(1.0, CLIP_NORM / (grad_norm + 1e-06))
    new_qkv, new_first_qkv, new_second_qkv = adamw(
        w_qkv, own_qkv * factor, first_qkv, second_qkv, RATE_MATRIX, DECAY_MATRIX
    )
    new_out, new_first_out, new_second_out = adamw(
        w_out, own_out * factor, first_out, second_out, rate_out, DECAY_MATRIX
    )
    new_up, new_first_up, new_second_up = adamw(
        w_up, own_up * factor, first_up, second_up, RATE_MATRIX, DECAY_MATRIX
    )
    new_down, new_first_down, new_second_down = adamw(
        w_down, own_down * factor, first_down, second_down, RATE_MATRIX, DECAY_MATRIX
    )
    new_small, new_first_small, new_second_small = adamw(
        small_params, own_small * factor, first_small, second_small, RATE_VECTOR, 0.0
    )
    new_bias, new_first_bias, new_second_bias = adamw(
        up_bias, own_bias * factor, first_bias, second_bias, RATE_VECTOR, 0.0
    )
    return (
        layer_out[None],
        input_grad[None],
        grad_norm,
        new_qkv,
        new_out,
        new_up,
        new_down,
        new_small,
        new_bias,
        new_first_qkv,
        new_first_out,
        new_first_up,
        new_first_down,
        new_first_small,
        new_first_bias,
        new_second_qkv,
        new_second_out,
        new_second_up,
        new_second_down,
        new_second_small,
        new_second_bias,
    )


def solution(mesh):
    rows, cols, flat = P("fsdp", None), P(None, "fsdp"), P("fsdp")
    by_token = P("fsdp", "dp", None)
    weights = (rows, cols, rows, cols, cols, flat)
    in_specs = (by_token, rows, by_token) + 3 * weights
    out_specs = (by_token, by_token, P()) + 3 * weights
    body = functools.partial(local, count=mesh.shape["fsdp"])
    return jax.shard_map(body, mesh=mesh, in_specs=in_specs, out_specs=out_specs, check_vma=False)
```

```python
import functools
import math

import jax
import jax.numpy as jnp
from jax import lax
from jax.experimental import pallas as pl
from jax.experimental.pallas import tpu as pltpu
from jax.sharding import PartitionSpec as P

HEADS = 8
DOCS = 4
STEP = 10


LN_EPS = 1e-05
CLIP_NORM = 1.0
BETA_ONE = 0.9
BETA_TWO = 0.999
ADAM_EPS = 1e-08
RATE_MATRIX = 0.04
RATE_VECTOR = 0.5
DECAY_MATRIX = 0.1
MASKED_SCORE = -1e30
LOWEST = -3e38
SAFE_SCORE = 60.0

HEAD = 64
LANES = 128
SEG_AT = HEAD
LSE_AT = HEAD + 16
VMEM = 60 << 20

bf16 = jnp.bfloat16
f32 = jnp.float32
NN = (((1,), (0,)), ((), ()))
NT = (((1,), (1,)), ((), ()))
TN = (((0,), (0,)), ((), ()))


def mm(left, right, dims):
    return lax.dot_general(left, right, dims, preferred_element_type=f32)


def params():
    return pltpu.CompilerParams(vmem_limit_bytes=VMEM)


def whole(*shape):
    return pl.BlockSpec(shape, lambda i, *_: (0,) * len(shape))


def cost(flops, nbytes, trans=0):
    return pl.CostEstimate(flops=int(flops), bytes_accessed=int(nbytes), transcendentals=int(trans))


def normalize(values):
    centre = jnp.mean(values, axis=-1, keepdims=True)
    centered = values - centre
    spread = jnp.mean(centered * centered, axis=-1, keepdims=True)
    rstd = lax.rsqrt(spread + LN_EPS)
    return centered * rstd, rstd


def normalize_back(grad, hat, rstd):
    along = jnp.mean(grad, axis=-1, keepdims=True)
    across = jnp.mean(grad * hat, axis=-1, keepdims=True)
    return rstd * (grad - along - hat * across)


def project_body(tok_m, tok_o, w, small, seg, normed_o, k_o, qt_o, vt_o, qtop_o, ktop_o, wqt, wvt, pick, *, heads):
    half = heads * HEAD
    i = pl.program_id(0)
    size = tok_m.shape[0]

    @pl.when(i == 0)
    def _():
        wqt[...] = w[:, :half].T
        wvt[...] = w[:, 2 * half :].T
        rows = lax.broadcasted_iota(jnp.int32, pick.shape, 0)
        cols = lax.broadcasted_iota(jnp.int32, pick.shape, 1)
        pick[...] = jnp.where(rows // HEAD == cols, 1.0, 0.0).astype(bf16)
        qtop_o[...] = jnp.zeros_like(qtop_o)
        ktop_o[...] = jnp.zeros_like(ktop_o)

    tok = jnp.where(i < pl.num_programs(0) // 2, tok_m[...], tok_o[...])
    hat, _ = normalize(tok.astype(f32))
    normed = (hat * small[0:1] + small[1:2]).astype(bf16)
    normed_o[...] = normed
    keys = mm(normed, w[:, half : 2 * half], NN).astype(bf16)
    queries = mm(wqt[...], normed, NT).astype(bf16).astype(f32) * (1.0 / math.sqrt(HEAD))
    values = mm(wvt[...], normed, NT).astype(bf16)
    rows = lax.broadcasted_iota(jnp.int32, (HEAD, size), 0)
    ones = jnp.where(rows < 2, 1.0, 0.0).astype(bf16)
    known = rows <= DOCS
    same = rows == seg[...]
    qmask = jnp.where(known & ~same, 1.0, 0.0).astype(bf16)
    lse_rows = (rows >= LSE_AT - HEAD) & (rows < LSE_AT - HEAD + 3)
    kmask = jnp.where(known & same, MASKED_SCORE, jnp.where(lse_rows, -1.0, 0.0)).T.astype(bf16)
    keys_f = keys.astype(f32)
    lengths = mm((keys_f * keys_f).astype(bf16), pick[...], NN)
    ktop_o[0:1] = jnp.maximum(ktop_o[0:1], jnp.max(lengths, axis=0, keepdims=True))
    for h in range(heads):
        part = slice(h * HEAD, (h + 1) * HEAD)
        qtop_o[h : h + 1] = jnp.maximum(
            qtop_o[h : h + 1], jnp.sum(queries[part] * queries[part], axis=0, keepdims=True)
        )
        k_o[h] = jnp.concatenate([keys[:, part], kmask], axis=1)
        qt_o[h] = jnp.concatenate([queries[part].astype(bf16), qmask], axis=0)
        vt_o[h] = jnp.concatenate([values[part], ones], axis=0)


def project(tok_m, tok_o, w, small, seg, heads, block=1024):
    own, width = tok_m.shape
    length = 2 * own
    half = heads * HEAD
    steps = own // block
    return pl.pallas_call(
        functools.partial(project_body, heads=heads),
        grid=(2 * steps,),
        in_specs=[
            pl.BlockSpec((block, width), lambda i: (jnp.minimum(i, steps - 1), 0)),
            pl.BlockSpec((block, width), lambda i: (jnp.maximum(i - steps, 0), 0)),
            whole(width, 3 * half),
            whole(8, width),
            pl.BlockSpec((1, block), lambda i: (0, i)),
        ],
        out_specs=[
            pl.BlockSpec((block, width), lambda i: (i, 0)),
            pl.BlockSpec((heads, block, LANES), lambda i: (0, i, 0)),
            pl.BlockSpec((heads, LANES, block), lambda i: (0, 0, i)),
            pl.BlockSpec((heads, LANES, block), lambda i: (0, 0, i)),
            whole(8, block),
            whole(8, LANES),
        ],
        out_shape=[
            jax.ShapeDtypeStruct((length, width), bf16),
            jax.ShapeDtypeStruct((heads, length, LANES), bf16),
            jax.ShapeDtypeStruct((heads, LANES, length), bf16),
            jax.ShapeDtypeStruct((heads, LANES, length), bf16),
            jax.ShapeDtypeStruct((8, block), f32),
            jax.ShapeDtypeStruct((8, LANES), f32),
        ],
        scratch_shapes=[
            pltpu.VMEM((half, width), bf16),
            pltpu.VMEM((half, width), bf16),
            pltpu.VMEM((half, LANES), bf16),
        ],
        compiler_params=params(),
        cost_estimate=cost(6 * length * width * half, 20 << 20),
        name="project",
    )(tok_m, tok_o, w, small, seg)


def tiles(lo, hi, shift, count, block, step):
    def after(q, k):
        last = k + 1 >= hi[q]
        q_next = jnp.where(last, q + 1, q)
        return q_next, jnp.where(last, lo[q_next], k + 1)

    def slices(q, k):
        at = lax.rem(k + shift[0], count)
        return pl.ds(pl.multiple_of(q * block, block), block), pl.ds(pl.multiple_of(at * step, step), step)

    return (jnp.int32(0), lo[0]), after, slices


def run_tiles(n, first, after, fill, use):
    @pl.when(n > 0)
    def _():
        fill(0, *first)

        def pair(_, at):
            mid = after(*at)
            end = after(*mid)
            use(0, *at)
            fill(1, *mid)
            use(1, *mid)
            fill(0, *end)
            return end

        at = lax.fori_loop(0, (n - 1) // 2, pair, first)

        @pl.when(n % 2 == 1)
        def _():
            use(0, *at)

        @pl.when(n % 2 == 0)
        def _():
            mid = after(*at)
            fill(1, *mid)
            use(0, *at)
            use(1, *mid)


def attend_body(
    lo, hi, n, shift, k, qt, vt, qtop, ktop, mine_o, other_o, qa_o, acc, top, slot_a, slot_b, *, block, step, heads, depth
):
    length = k.shape[1]
    own = length // 2
    acc[...] = jnp.zeros_like(acc)
    first, after, slices = tiles(lo, hi, shift, length // step, block, step)
    slots = (slot_a, slot_b)

    def fill(s, q, kk):
        qs, ks = slices(q, kk)
        for h in range(heads):
            slots[s][h] = jnp.exp(mm(k[h, ks, :], qt[h, :, qs], NN)).astype(bf16)

    def use(s, q, kk):
        qs, ks = slices(q, kk)
        for h in range(heads):
            acc[h, :, qs] += mm(vt[h, :depth, ks], slots[s][h], NN)

    def careful(_, at):
        qs, ks = slices(*at)
        for h in range(heads):
            score = mm(k[h, ks, :], qt[h, :, qs], NN)
            old = top[h : h + 1, qs]
            now = jnp.maximum(old, jnp.max(score, axis=0, keepdims=True))
            probs = jnp.exp(score - now).astype(bf16)
            acc[h, :, qs] = acc[h, :, qs] * jnp.exp(old - now) + mm(vt[h, :depth, ks], probs, NN)
            top[h : h + 1, qs] = now
        return after(*at)

    small = jnp.max(qtop[...]) * jnp.max(ktop[...]) <= SAFE_SCORE * SAFE_SCORE
    top[...] = jnp.where(small, 0.0, LOWEST) + jnp.zeros_like(top)
    run_tiles(jnp.where(small, n[0], 0), first, after, fill, use)
    lax.fori_loop(0, jnp.where(small, 0, n[0]), careful, first)

    wide = 512
    row = lax.broadcasted_iota(jnp.int32, (16, wide), 0)
    for part, out in ((0, mine_o), (1, other_o)):

        def finish(i, carry):
            at = pl.ds(pl.multiple_of(i * wide, wide), wide)
            qs = pl.ds(pl.multiple_of(i * wide + part * own, wide), wide)
            mixed = []
            for h in range(heads):
                totals = acc[h, HEAD : HEAD + 1, qs]
                mixed.append((acc[h, :HEAD, qs] / totals).astype(bf16))
                lse = top[h : h + 1, qs] + jnp.log(totals)
                one = lse.astype(bf16).astype(f32)
                two = (lse - one).astype(bf16).astype(f32)
                three = lse - one - two
                tail = jnp.where(row == 0, one, jnp.where(row == 1, two, jnp.where(row == 2, three, 0.0)))
                rest = jnp.zeros((LANES - LSE_AT - 16, wide), bf16)
                full = jnp.concatenate([qt[h, :LSE_AT, qs], tail.astype(bf16), rest], axis=0)
                qa_o[h, qs, :] = full.T
            out[at, :] = jnp.concatenate(mixed, axis=0).T
            return carry

        lax.fori_loop(0, own // wide, finish, 0)


IN_VMEM = pl.BlockSpec(memory_space=pltpu.VMEM)
IN_SMEM = pl.BlockSpec(memory_space=pltpu.SMEM)


def attend(lo, hi, n, shift, k, qt, vt, qtop, ktop, block, step):
    heads, length, _ = k.shape
    half = heads * HEAD
    depth = HEAD + 16
    return pl.pallas_call(
        functools.partial(attend_body, block=block, step=step, heads=heads, depth=depth),
        in_specs=[IN_SMEM] * 4 + [IN_VMEM] * 5,
        out_specs=[IN_VMEM] * 3,
        scratch_shapes=[
            pltpu.VMEM((heads, depth, length), f32),
            pltpu.VMEM((8, length), f32),
            pltpu.VMEM((heads, step, block), bf16),
            pltpu.VMEM((heads, step, block), bf16),
        ],
        out_shape=[
            jax.ShapeDtypeStruct((length // 2, half), bf16),
            jax.ShapeDtypeStruct((length // 2, half), bf16),
            jax.ShapeDtypeStruct((heads, length, LANES), bf16),
        ],
        compiler_params=params(),
        cost_estimate=cost(8 * heads * length * length * LANES, 20 << 20, heads * length * length),
        name="attend",
    )(lo, hi, n, shift, k, qt, vt, qtop, ktop)


def feed_body(
    who, tok, cot, mix_m, mix_o, w_m, w_o, small, bias, out_o, mid_o, do_m, do_o, gw_m, gw_o, gs_o, gb_o, acc_m, acc_o, pick, *, heads, width, hid
):
    i = pl.program_id(0)
    half = heads * HEAD
    down = hid
    top = 2 * hid

    @pl.when(i == 0)
    def _():
        acc_m[...] = jnp.zeros_like(acc_m)
        acc_o[...] = jnp.zeros_like(acc_o)
        gs_o[...] = jnp.zeros_like(gs_o)
        gb_o[...] = jnp.zeros_like(gb_o)
        rows = lax.broadcasted_iota(jnp.int32, pick.shape, 0)
        cols = lax.broadcasted_iota(jnp.int32, pick.shape, 1)
        inside = (cols >= rows // HEAD * LANES + HEAD) & (cols < rows // HEAD * LANES + HEAD + 2)
        pick[...] = jnp.where(inside, 1.0, 0.0).astype(bf16)

    grad_top = cot[...]
    grad_top_f = grad_top.astype(f32)
    mixed = (mix_m[...], mix_o[...])

    def weight(s, first, last):
        part = (w_m, w_o)[s][:, 0, :, first:last]
        return part.reshape(width, last - first)

    last = top + half
    branch = mm(mixed[0], weight(0, top, last), NT) + mm(mixed[1], weight(1, top, last), NT)
    middle = tok[...].astype(f32) + branch + small[4:5]
    hat, rstd = normalize(middle)
    normed = (hat * small[2:3] + small[3:4]).astype(bf16)
    result = middle + small[5:6]
    grad_normed = jnp.zeros_like(middle)
    for s in range(2):
        w_up = weight(s, 0, hid)
        w_down = weight(s, down, top)
        pre = mm(normed, w_up, NN) + bias[:, s * hid : (s + 1) * hid]
        square = pre * pre
        slope = math.sqrt(2.0 / math.pi)
        bent = jnp.tanh(pre * (slope + slope * 0.044715 * square))
        gate = 0.5 + 0.5 * bent
        hidden = (pre * gate).astype(bf16)
        result = result + mm(hidden, w_down, NT)
        grad_hidden = mm(grad_top, w_down, NN)
        bend = (0.5 * pre) * (1.0 - bent * bent) * (slope + 3.0 * slope * 0.044715 * square)
        grad_pre = (grad_hidden * (gate + bend)).astype(bf16)
        gb_o[:, s * hid : (s + 1) * hid] += jnp.sum(grad_pre.astype(f32), axis=0, keepdims=True)
        gw = acc_m if s == 0 else acc_o
        gw[:, down:top] += mm(grad_top, hidden, TN)
        gw[:, :hid] += mm(normed, grad_pre, TN)
        grad_normed = grad_normed + mm(grad_pre, w_up, NT)
    out_o[...] = result.astype(bf16)
    grad_middle = grad_top_f + normalize_back(grad_normed * small[2:3], hat, rstd)
    mid_o[...] = grad_middle
    gs_o[...] += jnp.concatenate(
        [
            jnp.zeros((2, width), f32),
            jnp.sum(grad_normed * hat, axis=0, keepdims=True),
            jnp.sum(grad_normed, axis=0, keepdims=True),
            jnp.sum(grad_middle, axis=0, keepdims=True),
            jnp.sum(grad_top_f, axis=0, keepdims=True),
            jnp.zeros((2, width), f32),
        ],
        axis=0,
    )
    grad_branch = grad_middle.astype(bf16)
    lane = lax.broadcasted_iota(jnp.int32, (tok.shape[0], HEAD), 1)
    for s in range(2):
        gw = acc_m if s == 0 else acc_o
        gw[:, top:] += mm(grad_branch, mixed[s], TN)
        grad_mixed = mm(grad_branch, weight(s, top, last), NN).astype(bf16)
        product = grad_mixed.astype(f32) * mixed[s].astype(f32)
        rough = product.astype(bf16)
        fine = (product - rough.astype(f32)).astype(bf16)
        inner = mm(rough, pick[...], NN) + mm(fine, pick[...], NN)
        out = do_m if s == 0 else do_o
        for h in range(heads):
            total = -inner[:, h * LANES + HEAD : (h + 1) * LANES]
            first = total.astype(bf16)
            rest = (total - first.astype(f32)).astype(bf16)
            tail = jnp.where(lane == 0, first.astype(f32), rest.astype(f32)).astype(bf16)
            out[h] = jnp.concatenate([grad_mixed[:, h * HEAD : (h + 1) * HEAD], tail], axis=1)

    @pl.when(i == pl.num_programs(0) - 1)
    def _():
        gw_m[...] = acc_m[...].astype(bf16)
        gw_o[...] = acc_o[...].astype(bf16)


def feed(who, tok, cot, mix_m, mix_o, weights, small, bias, heads, block=512):
    length, width = tok.shape
    half = heads * HEAD
    outer, _, inner, cols = weights.shape
    hid = (cols - half) // 2
    by_rows = lambda n: pl.BlockSpec((block, n), lambda i, *_: (i, 0))
    by_heads = pl.BlockSpec((heads, block, LANES), lambda i, *_: (0, i, 0))
    return pl.pallas_call(
        functools.partial(feed_body, heads=heads, width=width, hid=hid),
        grid_spec=pltpu.PrefetchScalarGridSpec(
            num_scalar_prefetch=1,
            grid=(length // block,),
            in_specs=[
                by_rows(width),
                by_rows(width),
                by_rows(half),
                by_rows(half),
                pl.BlockSpec((outer, 1, inner, cols), lambda i, who: (0, who[0], 0, 0)),
                pl.BlockSpec((outer, 1, inner, cols), lambda i, who: (0, 1 - who[0], 0, 0)),
                whole(8, width),
                whole(1, 2 * hid),
            ],
            out_specs=[
                by_rows(width),
                by_rows(width),
                by_heads,
                by_heads,
                whole(width, cols),
                whole(width, cols),
                whole(8, width),
                whole(1, 2 * hid),
            ],
            scratch_shapes=[
                pltpu.VMEM((width, cols), f32),
                pltpu.VMEM((width, cols), f32),
                pltpu.VMEM((half, heads * LANES), bf16),
            ],
        ),
        out_shape=[
            jax.ShapeDtypeStruct((length, width), bf16),
            jax.ShapeDtypeStruct((length, width), f32),
            jax.ShapeDtypeStruct((heads, length, LANES), bf16),
            jax.ShapeDtypeStruct((heads, length, LANES), bf16),
            jax.ShapeDtypeStruct((width, cols), bf16),
            jax.ShapeDtypeStruct((width, cols), bf16),
            jax.ShapeDtypeStruct((8, width), f32),
            jax.ShapeDtypeStruct((1, 2 * hid), f32),
        ],
        compiler_params=params(),
        cost_estimate=cost(12 * length * width * cols, 40 << 20, length * 2 * hid),
        name="feed",
    )(who, tok, cot, mix_m, mix_o, weights, weights, small, bias)


def attend_back_body(
    lo, hi, n, shift, do_m, do_o, k_h, vt_h, qa_h, qt_h, dq_h, dk_h, dv_h,
    k, vt, qa, qt, do, dot, dk, dv, dq, dq_s, dk_s, dv_s, pa, pb, ga, gb, sems, outs, *, block, step, heads
):
    length = k.shape[1]
    own = length // 2
    wide = 512
    inward = [
        pltpu.make_async_copy(do_m, do.at[:, :own, :], sems.at[0]),
        pltpu.make_async_copy(do_o, do.at[:, own:, :], sems.at[1]),
        pltpu.make_async_copy(k_h, k, sems.at[2]),
        pltpu.make_async_copy(vt_h, vt, sems.at[3]),
        pltpu.make_async_copy(qa_h, qa, sems.at[4]),
        pltpu.make_async_copy(qt_h, qt, sems.at[5]),
    ]
    for copy in inward:
        copy.start()
    dk[...] = jnp.zeros_like(dk)
    dv[...] = jnp.zeros_like(dv)
    dq[...] = jnp.zeros_like(dq)

    def begin(i, carry):
        qs = pl.ds(pl.multiple_of(i * wide, wide), wide)
        for h in range(heads):
            dot[h, :, qs] = do[h, qs, :].T[:HEAD]
        return carry

    inward[0].wait()
    lax.fori_loop(0, own // wide, begin, 0)
    inward[1].wait()
    lax.fori_loop(own // wide, length // wide, begin, 0)
    for copy in inward[2:]:
        copy.wait()
    first, after, slices = tiles(lo, hi, shift, length // step, block, step)
    probs_at, grads_at = (pa, pb), (ga, gb)

    def fill(s, q, kk):
        qs, ks = slices(q, kk)
        for h in range(heads):
            probs = jnp.exp(mm(qa[h, qs, :], k[h, ks, :], NT))
            probs_at[s][h] = probs.astype(bf16)
            grads_at[s][h] = (probs * mm(do[h, qs, :], vt[h, :, ks], NN)).astype(bf16)

    def use(s, q, kk):
        qs, ks = slices(q, kk)
        for h in range(heads):
            dv[h, :, ks] += mm(dot[h, :, qs], probs_at[s][h], NN)
            dk[h, :, ks] += mm(qt[h, :HEAD, qs], grads_at[s][h], NN)
            dq[h, qs, :] += mm(grads_at[s][h], k[h, ks, :], NN)

    run_tiles(n[0], first, after, fill, use)
    outward = []
    for h in range(heads):
        rows = slice(h * HEAD, (h + 1) * HEAD)
        dk_s[rows, :] = dk[h].astype(bf16)
        dv_s[rows, :] = dv[h].astype(bf16)
        outward.append(pltpu.make_async_copy(dk_s.at[rows, :], dk_h.at[rows, :], outs.at[2 * h]))
        outward.append(pltpu.make_async_copy(dv_s.at[rows, :], dv_h.at[rows, :], outs.at[2 * h + 1]))
        outward[-2].start()
        outward[-1].start()
    scale = 1.0 / math.sqrt(HEAD)

    def finish(i, carry):
        qs = pl.ds(pl.multiple_of(i * wide, wide), wide)
        dq_s[qs, :] = jnp.concatenate([dq[h, qs, :][:, :HEAD] * scale for h in range(heads)], axis=1).astype(bf16)
        return carry

    for part in range(2):
        rows = slice(part * own, (part + 1) * own)
        lax.fori_loop(part * own // wide, (part + 1) * own // wide, finish, 0)
        outward.append(pltpu.make_async_copy(dq_s.at[rows, :], dq_h.at[rows, :], outs.at[2 * heads + part]))
        outward[-1].start()
    for copy in outward:
        copy.wait()


IN_HBM = pl.BlockSpec(memory_space=pl.ANY)


def attend_back(lo, hi, n, shift, qa, k, qt, vt, do_m, do_o, block, step):
    heads, length, _ = k.shape
    half = heads * HEAD
    return pl.pallas_call(
        functools.partial(attend_back_body, block=block, step=step, heads=heads),
        in_specs=[IN_SMEM] * 4 + [IN_HBM] * 6,
        out_specs=[IN_HBM] * 3,
        scratch_shapes=[
            pltpu.VMEM((heads, length, LANES), bf16),
            pltpu.VMEM((heads, LANES, length), bf16),
            pltpu.VMEM((heads, length, LANES), bf16),
            pltpu.VMEM((heads, LANES, length), bf16),
            pltpu.VMEM((heads, length, LANES), bf16),
            pltpu.VMEM((heads, HEAD, length), bf16),
            pltpu.VMEM((heads, HEAD, length), f32),
            pltpu.VMEM((heads, HEAD, length), f32),
            pltpu.VMEM((heads, length, LANES), f32),
            pltpu.VMEM((length, half), bf16),
            pltpu.VMEM((half, length), bf16),
            pltpu.VMEM((half, length), bf16),
        ]
        + [pltpu.VMEM((heads, block, step), bf16)] * 4
        + [pltpu.SemaphoreType.DMA((6,)), pltpu.SemaphoreType.DMA((2 * heads + 2,))],
        out_shape=[
            jax.ShapeDtypeStruct((length, half), bf16),
            jax.ShapeDtypeStruct((half, length), bf16),
            jax.ShapeDtypeStruct((half, length), bf16),
        ],
        compiler_params=params(),
        cost_estimate=cost(20 * heads * length * length * LANES, 24 << 20, heads * length * length),
        name="attend_back",
    )(lo, hi, n, shift, do_m, do_o, k, vt, qa, qt)


def unproject_body(normed, dq, dk, dv, gw, acc_q, acc_kv):
    half = dq.shape[1]

    @pl.when(pl.program_id(0) == 0)
    def _():
        acc_q[...] = jnp.zeros_like(acc_q)
        acc_kv[...] = jnp.zeros_like(acc_kv)

    rows = normed[...]
    acc_q[...] += mm(rows, dq[...], TN)
    acc_kv[:half] += mm(dk[...], rows, NN)
    acc_kv[half:] += mm(dv[...], rows, NN)

    @pl.when(pl.program_id(0) == pl.num_programs(0) - 1)
    def _():
        gw[...] = jnp.concatenate([acc_q[...].astype(bf16), acc_kv[...].T.astype(bf16)], axis=1)


def unproject(normed, dq, dk, dv, block=1024):
    length, width = normed.shape
    half = dq.shape[1]
    return pl.pallas_call(
        unproject_body,
        grid=(length // block,),
        in_specs=[
            pl.BlockSpec((block, width), lambda i: (i, 0)),
            pl.BlockSpec((block, half), lambda i: (i, 0)),
            pl.BlockSpec((half, block), lambda i: (0, i)),
            pl.BlockSpec((half, block), lambda i: (0, i)),
        ],
        out_specs=whole(width, 3 * half),
        out_shape=jax.ShapeDtypeStruct((width, 3 * half), bf16),
        scratch_shapes=[pltpu.VMEM((width, half), f32), pltpu.VMEM((2 * half, width), f32)],
        compiler_params=params(),
        cost_estimate=cost(6 * length * width * half, 12 << 20),
        name="unproject",
    )(normed, dq, dk, dv)


def normed_grad(dq, dk, dv, w):
    half = dq.shape[1]
    return (
        mm(dq[...], w[:, :half], NT)
        + mm(dk[...].T, w[:, half : 2 * half], NT)
        + mm(dv[...].T, w[:, 2 * half :], NT)
    )


def partial_body(dq, dk, dv, w, gn):
    gn[...] = normed_grad(dq, dk, dv, w).astype(bf16)


def partial_grad(dq, dk, dv, w, block=1024):
    length, half = dq.shape
    own, width = length // 2, w.shape[0]
    off = own // block
    return pl.pallas_call(
        partial_body,
        grid=(off,),
        in_specs=[
            pl.BlockSpec((block, half), lambda i: (i + off, 0)),
            pl.BlockSpec((half, block), lambda i: (0, i + off)),
            pl.BlockSpec((half, block), lambda i: (0, i + off)),
            whole(width, 3 * half),
        ],
        out_specs=pl.BlockSpec((block, width), lambda i: (i, 0)),
        out_shape=jax.ShapeDtypeStruct((own, width), bf16),
        compiler_params=params(),
        cost_estimate=cost(0, 1 << 20),
        name="partial_grad",
    )(dq, dk, dv, w)


def finish_body(dq, dk, dv, w, tok, gn_o, mid, small, out, gs):
    @pl.when(pl.program_id(0) == 0)
    def _():
        gs[...] = jnp.zeros_like(gs)

    hat, rstd = normalize(tok[...].astype(f32))
    grad = normed_grad(dq, dk, dv, w) + gn_o[...].astype(f32)
    out[...] = (mid[...] + normalize_back(grad * small[0:1], hat, rstd)).astype(bf16)
    gs[...] += jnp.concatenate(
        [
            jnp.sum(grad * hat, axis=0, keepdims=True),
            jnp.sum(grad, axis=0, keepdims=True),
            jnp.zeros((6, grad.shape[1]), f32),
        ],
        axis=0,
    )


def finish(dq, dk, dv, w, tok, gn_o, mid, small, block=512):
    length, width = tok.shape
    half = dq.shape[1]
    rows = pl.BlockSpec((block, width), lambda i: (i, 0))
    cols = pl.BlockSpec((half, block), lambda i: (0, i))
    return pl.pallas_call(
        finish_body,
        grid=(length // block,),
        in_specs=[
            pl.BlockSpec((block, half), lambda i: (i, 0)),
            cols,
            cols,
            whole(width, 3 * half),
            rows,
            rows,
            rows,
            whole(8, width),
        ],
        out_specs=[rows, whole(8, width)],
        out_shape=[jax.ShapeDtypeStruct((length, width), bf16), jax.ShapeDtypeStruct((8, width), f32)],
        compiler_params=params(),
        cost_estimate=cost(0, 1 << 20),
        name="finish",
    )(dq, dk, dv, w, tok, gn_o, mid, small)


def adamw(weight, grad, first, second, rate, decay):
    first = BETA_ONE * first + (1.0 - BETA_ONE) * grad
    second = BETA_TWO * second + (1.0 - BETA_TWO) * grad * grad
    fixed_one = first / (1.0 - BETA_ONE**STEP)
    fixed_two = second / (1.0 - BETA_TWO**STEP)
    weight = weight - rate * (fixed_one / (jnp.sqrt(fixed_two) + ADAM_EPS) + decay * weight)
    return (weight, first, second)


def swap(values):
    return lax.ppermute(values, "dp", [(0, 1), (1, 0)])


def across(values, count, bit):
    return lax.ppermute(values, "fsdp", [(i, i ^ bit) for i in range(count)])


def gather(shard, count, beside):
    if count < 8 or count & (count - 1):
        return lax.all_gather(shard, "fsdp", axis=0), beside
    me = lax.axis_index("fsdp")
    held = shard
    depth = 0
    bit = count // 2
    while bit > 2:
        there = across(held, count, bit)
        above = (me & bit) != 0
        held = jnp.where(above, jnp.stack([there, held], axis=depth), jnp.stack([held, there], axis=depth))
        depth += 1
        bit //= 2
    many = count // 4
    held, beside = lax.optimization_barrier((held.reshape((many,) + shard.shape), beside))
    side, line = across(held, count, 1), across(held, count, 2)
    corner = jnp.concatenate([across(side[: many // 2], count, 2), across(line[many // 2 :], count, 1)], axis=0)
    place = me & 3

    def block(j):
        at = place ^ j
        return jnp.where(at == 0, held, jnp.where(at == 1, side, jnp.where(at == 2, line, corner)))

    return jnp.stack([block(j) for j in range(4)], axis=1).reshape((count,) + shard.shape), beside


def local(
    tokens,
    segments,
    cotangent,
    w_qkv,
    w_out,
    w_up,
    w_down,
    small_params,
    up_bias,
    first_qkv,
    first_out,
    first_up,
    first_down,
    first_small,
    first_bias,
    second_qkv,
    second_out,
    second_up,
    second_down,
    second_small,
    second_bias,
    *,
    count,
):
    own, width = tokens.shape[1:]
    length = segments.shape[1]
    heads = HEADS // 2
    half = heads * HEAD
    hid = w_up.shape[1] // 2
    cols = 2 * hid + half
    rows = w_qkv.shape[0]
    out_fan = max(1, width * (DOCS + 1) // length)
    rate_out = RATE_MATRIX * math.sqrt(width / out_fan)
    dp = lax.axis_index("dp")
    block, step = 256, 512

    def mine_of(values, axis):
        return lax.dynamic_index_in_dim(values, dp, axis, keepdims=False)

    def in_order(mine, other, axis):
        return jnp.where(
            dp == 0, jnp.stack([mine, other], axis=axis), jnp.stack([other, mine], axis=axis)
        )

    tok = tokens[0]
    tok_other = swap(tok)
    seg = segments[0]
    seg_here = jnp.where(dp == 0, seg, jnp.roll(seg, own))
    below = jnp.sum((seg[None, :] < seg_here[::block, None]).astype(jnp.int32), axis=1)
    until = jnp.sum((seg[None, :] <= seg_here[block - 1 :: block, None]).astype(jnp.int32), axis=1)
    lo = below // step
    hi = (until + step - 1) // step
    n = jnp.sum(hi - lo).reshape(1)
    shift = (dp * (own // step)).astype(jnp.int32).reshape(1)
    who = dp.astype(jnp.int32).reshape(1)

    wide = 3 * half
    tiny_len = 6 * rows + up_bias.shape[0]
    lines = -(-tiny_len // wide)
    qkv_shard = mine_of(w_qkv.reshape(rows, 3, 2, half), 2).reshape(rows, wide)
    tiny = jnp.concatenate([small_params.T.reshape(-1), up_bias])
    tiny = jnp.pad(tiny, (0, lines * wide - tiny_len)).reshape(lines, wide)
    first_all, (seg_here, lo, hi, n, tok_other) = gather(
        jnp.concatenate([qkv_shard, tiny], axis=0).astype(bf16), count, (seg_here, lo, hi, n, tok_other)
    )
    w_one = first_all[:, :rows].reshape(width, wide)
    tiny_all = first_all[:, rows:].reshape(count, -1)[:, :tiny_len].astype(f32)
    small = jnp.pad(tiny_all[:, : 6 * rows].reshape(width, 6).T, ((0, 2), (0, 0)))
    bias_all = tiny_all[:, 6 * rows :].reshape(1, 2, hid)
    bias = jnp.where(dp == 0, bias_all, bias_all[:, ::-1]).reshape(1, 2 * hid)
    rest_shard = jnp.concatenate(
        [
            mine_of(w_up.reshape(rows, 2, hid), 1),
            mine_of(w_down.reshape(2, hid, rows), 0).T,
            mine_of(w_out.reshape(2, half, rows), 0).T,
        ],
        axis=1,
    ).astype(bf16)
    rest_shard, w_one = lax.optimization_barrier((rest_shard, w_one))
    rest_all = lax.all_gather(rest_shard, ("fsdp", "dp"), axis=0).reshape(count, 2, rows, cols)
    if rows % 16:
        rest_all = rest_all.transpose(1, 0, 2, 3).reshape(1, 2, width, cols)

    normed, keys, queries_t, values_t, qtop, ktop = project(tok, tok_other, w_one, small, seg_here[None], heads)
    mix_m, mix_send, queries = attend(lo, hi, n, shift, keys, queries_t, values_t, qtop, ktop, block, step)
    mix_o = swap(mix_send)
    layer_out, grad_mid, do_m, do_send, gw_m, gw_send, gs_two, gb = feed(
        who, tok, cotangent[0], mix_m, mix_o, rest_all, small, bias, heads
    )
    gb_all = jnp.where(dp == 0, gb.reshape(2, hid), gb.reshape(2, hid)[::-1]).reshape(count, -1)
    grad_tiny = jnp.concatenate([gs_two[:6].T.reshape(count, 6 * rows), gb_all], axis=1)
    grad_tiny = jnp.pad(grad_tiny, ((0, 0), (0, cols - tiny_len))).reshape(count, 1, cols)
    gw_pair = (gw_m.astype(f32) + swap(gw_send).astype(f32)).reshape(count, rows, cols)
    gw_pair = jnp.concatenate([gw_pair, grad_tiny], axis=1).astype(bf16)
    do_o, gw_pair = lax.optimization_barrier((swap(do_send), gw_pair))
    arrived = lax.all_to_all(gw_pair, "fsdp", 0, 0)
    dq, dk, dv = attend_back(lo, hi, n, shift, queries, keys, queries_t, values_t, do_m, do_o, block, step)
    dq, arrived = lax.optimization_barrier((dq, arrived))
    gw_one = unproject(normed, dq, dk, dv)
    spread_one = lax.all_to_all(gw_one.reshape(count, rows, wide), "fsdp", 0, 0)
    dq, gw_one = lax.optimization_barrier((dq, gw_one))
    gn_o = swap(partial_grad(dq, dk, dv, w_one))
    input_grad, gs_one = finish(dq, dk, dv, w_one, tok, gn_o, grad_mid, small)
    spread_one, gs_one = lax.optimization_barrier((spread_one, gs_one))
    rest_sum = jnp.sum(arrived.astype(f32), axis=0)
    rest_grad, tiny_mine = rest_sum[:rows], rest_sum[rows]
    rest_other = swap(rest_grad)
    rest_squares = jnp.sum(rest_grad * rest_grad)
    qkv_mine = jnp.sum(spread_one.astype(f32), axis=0)
    squares = jnp.sum(qkv_mine * qkv_mine) + rest_squares
    every = jnp.concatenate(
        [gs_one[:2].reshape(-1), jnp.broadcast_to(squares, (LANES,)), tiny_mine[:tiny_len]]
    )
    every = jnp.broadcast_to(every, (2 * count, 1, every.shape[0]))
    qkv_mine, every = lax.optimization_barrier((qkv_mine, every))
    every = lax.all_to_all(every, ("dp", "fsdp"), 0, 0)[:, 0]
    qkv_other = swap(qkv_mine)
    norm_one = jnp.sum(every[:, : 2 * width], axis=0).reshape(2, width)
    tiny_all = jnp.sum(every[:, 2 * width + LANES :].reshape(2, count, tiny_len), axis=0)
    total_squares = jnp.sum(every[:, 2 * width]) + jnp.sum(norm_one * norm_one) + jnp.sum(tiny_all * tiny_all)
    grad_norm = jnp.sqrt(total_squares)
    me = lax.axis_index("fsdp")
    tiny_own = lax.dynamic_index_in_dim(tiny_all, me, 0, keepdims=False)
    norm_own = lax.dynamic_slice_in_dim(norm_one, me * rows, rows, 1)

    own_qkv = in_order(qkv_mine.reshape(rows, 3, half), qkv_other.reshape(rows, 3, half), 2).reshape(rows, -1)
    own_up = in_order(rest_grad[:, :hid], rest_other[:, :hid], 1).reshape(rows, -1)
    own_down = in_order(rest_grad[:, hid : 2 * hid], rest_other[:, hid : 2 * hid], 1).reshape(rows, -1).T
    own_out = in_order(rest_grad[:, 2 * hid :], rest_other[:, 2 * hid :], 1).reshape(rows, -1).T
    own_small = tiny_own[: 6 * rows].reshape(rows, 6).T + jnp.pad(norm_own, ((0, 4), (0, 0)))
    own_bias = tiny_own[6 * rows :]
    factor = jnp.minimum(1.0, CLIP_NORM / (grad_norm + 1e-06))
    new_qkv, new_first_qkv, new_second_qkv = adamw(
        w_qkv, own_qkv * factor, first_qkv, second_qkv, RATE_MATRIX, DECAY_MATRIX
    )
    new_out, new_first_out, new_second_out = adamw(
        w_out, own_out * factor, first_out, second_out, rate_out, DECAY_MATRIX
    )
    new_up, new_first_up, new_second_up = adamw(
        w_up, own_up * factor, first_up, second_up, RATE_MATRIX, DECAY_MATRIX
    )
    new_down, new_first_down, new_second_down = adamw(
        w_down, own_down * factor, first_down, second_down, RATE_MATRIX, DECAY_MATRIX
    )
    new_small, new_first_small, new_second_small = adamw(
        small_params, own_small * factor, first_small, second_small, RATE_VECTOR, 0.0
    )
    new_bias, new_first_bias, new_second_bias = adamw(
        up_bias, own_bias * factor, first_bias, second_bias, RATE_VECTOR, 0.0
    )
    return (
        layer_out[None],
        input_grad[None],
        grad_norm,
        new_qkv,
        new_out,
        new_up,
        new_down,
        new_small,
        new_bias,
        new_first_qkv,
        new_first_out,
        new_first_up,
        new_first_down,
        new_first_small,
        new_first_bias,
        new_second_qkv,
        new_second_out,
        new_second_up,
        new_second_down,
        new_second_small,
        new_second_bias,
    )


def solution(mesh):
    rows, cols, flat = P("fsdp", None), P(None, "fsdp"), P("fsdp")
    by_token = P("fsdp", "dp", None)
    weights = (rows, cols, rows, cols, cols, flat)
    in_specs = (by_token, rows, by_token) + 3 * weights
    out_specs = (by_token, by_token, P()) + 3 * weights
    body = functools.partial(local, count=mesh.shape["fsdp"])
    return jax.shard_map(body, mesh=mesh, in_specs=in_specs, out_specs=out_specs, check_vma=False)
```

```python
import functools
import math

import jax
import jax.numpy as jnp
from jax import lax
from jax.experimental import pallas as pl
from jax.experimental.pallas import tpu as pltpu
from jax.sharding import PartitionSpec as P

HEADS = 8
DOCS = 4
STEP = 10


LN_EPS = 1e-05
CLIP_NORM = 1.0
BETA_ONE = 0.9
BETA_TWO = 0.999
ADAM_EPS = 1e-08
RATE_MATRIX = 0.04
RATE_VECTOR = 0.5
DECAY_MATRIX = 0.1
MASKED_SCORE = -1e30
LOWEST = -3e38
SAFE_SCORE = 60.0

HEAD = 64
LANES = 128
SEG_AT = HEAD
LSE_AT = HEAD + 16
VMEM = 60 << 20

bf16 = jnp.bfloat16
f32 = jnp.float32
NN = (((1,), (0,)), ((), ()))
NT = (((1,), (1,)), ((), ()))
TN = (((0,), (0,)), ((), ()))


def mm(left, right, dims):
    return lax.dot_general(left, right, dims, preferred_element_type=f32)


def params():
    return pltpu.CompilerParams(vmem_limit_bytes=VMEM)


def whole(*shape):
    return pl.BlockSpec(shape, lambda i, *_: (0,) * len(shape))


def cost(flops, nbytes, trans=0):
    return pl.CostEstimate(flops=int(flops), bytes_accessed=int(nbytes), transcendentals=int(trans))


def normalize(values):
    centre = jnp.mean(values, axis=-1, keepdims=True)
    centered = values - centre
    spread = jnp.mean(centered * centered, axis=-1, keepdims=True)
    rstd = lax.rsqrt(spread + LN_EPS)
    return centered * rstd, rstd


def normalize_back(grad, hat, rstd):
    along = jnp.mean(grad, axis=-1, keepdims=True)
    across = jnp.mean(grad * hat, axis=-1, keepdims=True)
    return rstd * (grad - along - hat * across)


def tiles(base, many, block, step):
    def after(q, t):
        last = t + 1 >= many[q]
        return jnp.where(last, jnp.minimum(q + 1, many.shape[0] - 1), q), jnp.where(last, 0, t + 1)

    def slices(q, t):
        return (
            pl.ds(pl.multiple_of(q * block, block), block),
            pl.ds(pl.multiple_of(base[q] + t * step, LANES), step),
        )

    return (jnp.int32(0), jnp.int32(0)), after, slices


def run_tiles(n, first, after, fill, use):
    @pl.when(n > 0)
    def _():
        fill(0, *first)

        def pair(_, at):
            mid = after(*at)
            end = after(*mid)
            use(0, *at)
            fill(1, *mid)
            use(1, *mid)
            fill(0, *end)
            return end

        at = lax.fori_loop(0, (n - 1) // 2, pair, first)

        @pl.when(n % 2 == 1)
        def _():
            use(0, *at)

        @pl.when(n % 2 == 0)
        def _():
            mid = after(*at)
            fill(1, *mid)
            use(0, *at)
            use(1, *mid)


def attend_body(
    base, many, n, who, tok_m, tok_o, w, small, seg, mine_h, other_h, qa_h, normed_h, k_h, qt_h, vt_h,
    tok, normed_s, k, qt, vt, qa, mixed_s, wqt, wvt, pick, qtop, ktop, acc, top, slot_a, slot_b, sem_in, sem_out, sem_end,
    *, block, step, heads, depth, part,
):
    length, width = tok.shape
    own = length // 2
    half = heads * HEAD
    mine = pl.multiple_of(who[0] * own, own)
    other = pl.multiple_of((1 - who[0]) * own, own)
    inward = [
        pltpu.make_async_copy(tok_m, tok.at[pl.ds(mine, own), :], sem_in.at[0]),
        pltpu.make_async_copy(tok_o, tok.at[pl.ds(other, own), :], sem_in.at[1]),
    ]
    for copy in inward:
        copy.start()
    wqt[...] = w[:, :half].T
    wvt[...] = w[:, 2 * half :].T
    rows = lax.broadcasted_iota(jnp.int32, pick.shape, 0)
    cols = lax.broadcasted_iota(jnp.int32, pick.shape, 1)
    pick[...] = jnp.where(rows // HEAD == cols, 1.0, 0.0).astype(bf16)
    qtop[...] = jnp.zeros_like(qtop)
    ktop[...] = jnp.zeros_like(ktop)
    acc[...] = jnp.zeros_like(acc)
    for copy in inward:
        copy.wait()

    def outward(i):
        at = pl.ds(pl.multiple_of(i * part, part), part)
        return [
            pltpu.make_async_copy(normed_s.at[at, :], normed_h.at[at, :], sem_out.at[0, i]),
            pltpu.make_async_copy(k.at[:, at, :], k_h.at[:, at, :], sem_out.at[1, i]),
            pltpu.make_async_copy(qt.at[:, :HEAD, at], qt_h.at[:, :, at], sem_out.at[2, i]),
            pltpu.make_async_copy(vt.at[:, :, at], vt_h.at[:, :, at], sem_out.at[3, i]),
        ]

    def project(i, carry):
        at = pl.ds(pl.multiple_of(i * part, part), part)
        hat, _ = normalize(tok[at, :].astype(f32))
        normed = (hat * small[0:1] + small[1:2]).astype(bf16)
        normed_s[at, :] = normed
        keys = mm(normed, w[:, half : 2 * half], NN).astype(bf16)
        queries = mm(wqt[...], normed, NT).astype(bf16).astype(f32) * (1.0 / math.sqrt(HEAD))
        values = mm(wvt[...], normed, NT).astype(bf16)
        rows = lax.broadcasted_iota(jnp.int32, (HEAD, part), 0)
        ones = jnp.where(rows < 2, 1.0, 0.0).astype(bf16)
        known = rows <= DOCS
        same = rows == seg[:, at]
        qmask = jnp.where(known & ~same, 1.0, 0.0).astype(bf16)
        lse_rows = (rows >= LSE_AT - HEAD) & (rows < LSE_AT - HEAD + 3)
        kmask = jnp.where(known & same, MASKED_SCORE, jnp.where(lse_rows, -1.0, 0.0)).T.astype(bf16)
        keys_f = keys.astype(f32)
        lengths = mm((keys_f * keys_f).astype(bf16), pick[...], NN)
        ktop[0:1] = jnp.maximum(ktop[0:1], jnp.max(lengths, axis=0, keepdims=True))
        for h in range(heads):
            own_rows = slice(h * HEAD, (h + 1) * HEAD)
            qtop[h : h + 1] = jnp.maximum(
                qtop[h : h + 1], jnp.sum(queries[own_rows] * queries[own_rows], axis=0, keepdims=True)
            )
            k[h, at, :] = jnp.concatenate([keys[:, own_rows], kmask], axis=1)
            qt[h, :, at] = jnp.concatenate([queries[own_rows].astype(bf16), qmask], axis=0)
            vt[h, :, at] = jnp.concatenate([values[own_rows], ones], axis=0)
        for copy in outward(i):
            copy.start()
        return carry

    lax.fori_loop(0, length // part, project, 0)

    first, after, slices = tiles(base, many, block, step)
    slots = (slot_a, slot_b)

    def fill(s, q, t):
        qs, ks = slices(q, t)
        for h in range(heads):
            slots[s][h] = jnp.exp(mm(k[h, ks, :], qt[h, :, qs], NN)).astype(bf16)

    def use(s, q, t):
        qs, ks = slices(q, t)
        for h in range(heads):
            acc[h, :, qs] += mm(vt[h, :depth, ks], slots[s][h], NN)

    def careful(_, at):
        qs, ks = slices(*at)
        for h in range(heads):
            score = mm(k[h, ks, :], qt[h, :, qs], NN)
            old = top[h : h + 1, qs]
            now = jnp.maximum(old, jnp.max(score, axis=0, keepdims=True))
            probs = jnp.exp(score - now).astype(bf16)
            acc[h, :, qs] = acc[h, :, qs] * jnp.exp(old - now) + mm(vt[h, :depth, ks], probs, NN)
            top[h : h + 1, qs] = now
        return after(*at)

    fits = jnp.max(qtop[...]) * jnp.max(ktop[...]) <= SAFE_SCORE * SAFE_SCORE
    top[...] = jnp.where(fits, 0.0, LOWEST) + jnp.zeros_like(top)
    run_tiles(jnp.where(fits, n[0], 0), first, after, fill, use)
    lax.fori_loop(0, jnp.where(fits, 0, n[0]), careful, first)

    wide = 512
    row = lax.broadcasted_iota(jnp.int32, (16, wide), 0)

    def ending(i):
        qs = pl.ds(pl.multiple_of(i * wide, wide), wide)
        return pltpu.make_async_copy(qa.at[:, qs, :], qa_h.at[:, qs, :], sem_end.at[i])

    def finish(i, carry):
        qs = pl.ds(pl.multiple_of(i * wide, wide), wide)
        mixed = []
        for h in range(heads):
            totals = acc[h, HEAD : HEAD + 1, qs]
            mixed.append((acc[h, :HEAD, qs] / totals).astype(bf16))
            lse = top[h : h + 1, qs] + jnp.log(totals)
            one = lse.astype(bf16).astype(f32)
            two = (lse - one).astype(bf16).astype(f32)
            three = lse - one - two
            tail = jnp.where(row == 0, one, jnp.where(row == 1, two, jnp.where(row == 2, three, 0.0)))
            rest = jnp.zeros((LANES - LSE_AT - 16, wide), bf16)
            full = jnp.concatenate([qt[h, :LSE_AT, qs], tail.astype(bf16), rest], axis=0)
            qa[h, qs, :] = full.T
        mixed_s[qs, :] = jnp.concatenate(mixed, axis=0).T
        ending(i).start()
        return carry

    lax.fori_loop(0, length // wide, finish, 0)
    last = [
        pltpu.make_async_copy(mixed_s.at[pl.ds(mine, own), :], mine_h, sem_in.at[0]),
        pltpu.make_async_copy(mixed_s.at[pl.ds(other, own), :], other_h, sem_in.at[1]),
    ]
    for copy in last:
        copy.start()
    for i in range(length // part):
        for copy in outward(i):
            copy.wait()
    for i in range(length // wide):
        ending(i).wait()
    for copy in last:
        copy.wait()


IN_VMEM = pl.BlockSpec(memory_space=pltpu.VMEM)
IN_SMEM = pl.BlockSpec(memory_space=pltpu.SMEM)
IN_HBM = pl.BlockSpec(memory_space=pl.ANY)


def attend(base, many, n, who, tok_m, tok_o, w, small, seg, heads, block, step, part=1024):
    own, width = tok_m.shape
    length = 2 * own
    half = heads * HEAD
    depth = HEAD + 16
    return pl.pallas_call(
        functools.partial(attend_body, block=block, step=step, heads=heads, depth=depth, part=part),
        in_specs=[IN_SMEM] * 4 + [IN_HBM] * 2 + [IN_VMEM] * 3,
        out_specs=[IN_HBM] * 7,
        scratch_shapes=[
            pltpu.VMEM((length, width), bf16),
            pltpu.VMEM((length, width), bf16),
            pltpu.VMEM((heads, length, LANES), bf16),
            pltpu.VMEM((heads, LANES, length), bf16),
            pltpu.VMEM((heads, LANES, length), bf16),
            pltpu.VMEM((heads, length, LANES), bf16),
            pltpu.VMEM((length, half), bf16),
            pltpu.VMEM((half, width), bf16),
            pltpu.VMEM((half, width), bf16),
            pltpu.VMEM((half, LANES), bf16),
            pltpu.VMEM((8, part), f32),
            pltpu.VMEM((8, LANES), f32),
            pltpu.VMEM((heads, depth, length), f32),
            pltpu.VMEM((8, length), f32),
            pltpu.VMEM((heads, step, block), bf16),
            pltpu.VMEM((heads, step, block), bf16),
            pltpu.SemaphoreType.DMA((2,)),
            pltpu.SemaphoreType.DMA((4, length // part)),
            pltpu.SemaphoreType.DMA((length // 512,)),
        ],
        out_shape=[
            jax.ShapeDtypeStruct((own, half), bf16),
            jax.ShapeDtypeStruct((own, half), bf16),
            jax.ShapeDtypeStruct((heads, length, LANES), bf16),
            jax.ShapeDtypeStruct((length, width), bf16),
            jax.ShapeDtypeStruct((heads, length, LANES), bf16),
            jax.ShapeDtypeStruct((heads, HEAD, length), bf16),
            jax.ShapeDtypeStruct((heads, LANES, length), bf16),
        ],
        compiler_params=params(),
        cost_estimate=cost(8 * heads * length * length * LANES, 20 << 20, heads * length * length),
        name="attend",
    )(base, many, n, who, tok_m, tok_o, w, small, seg)


def feed_body(
    who, tok, cot, mix_m, mix_o, w_m, w_o, small, bias, out_o, mid_o, do_m, do_o, gw_m, gw_o, gs_o, gb_o, acc_m, acc_o, pick, *, heads, width, hid
):
    i = pl.program_id(0)
    half = heads * HEAD
    down = hid
    top = 2 * hid

    @pl.when(i == 0)
    def _():
        acc_m[...] = jnp.zeros_like(acc_m)
        acc_o[...] = jnp.zeros_like(acc_o)
        gs_o[...] = jnp.zeros_like(gs_o)
        gb_o[...] = jnp.zeros_like(gb_o)
        rows = lax.broadcasted_iota(jnp.int32, pick.shape, 0)
        cols = lax.broadcasted_iota(jnp.int32, pick.shape, 1)
        inside = (cols >= rows // HEAD * LANES + HEAD) & (cols < rows // HEAD * LANES + HEAD + 2)
        pick[...] = jnp.where(inside, 1.0, 0.0).astype(bf16)

    grad_top = cot[...]
    grad_top_f = grad_top.astype(f32)
    mixed = (mix_m[...], mix_o[...])

    def weight(s, first, last):
        part = (w_m, w_o)[s][:, 0, :, first:last]
        return part.reshape(width, last - first)

    last = top + half
    branch = mm(mixed[0], weight(0, top, last), NT) + mm(mixed[1], weight(1, top, last), NT)
    middle = tok[...].astype(f32) + branch + small[4:5]
    hat, rstd = normalize(middle)
    normed = (hat * small[2:3] + small[3:4]).astype(bf16)
    result = middle + small[5:6]
    grad_normed = jnp.zeros_like(middle)
    for s in range(2):
        w_up = weight(s, 0, hid)
        w_down = weight(s, down, top)
        pre = mm(normed, w_up, NN) + bias[:, s * hid : (s + 1) * hid]
        square = pre * pre
        slope = math.sqrt(2.0 / math.pi)
        bent = jnp.tanh(pre * (slope + slope * 0.044715 * square))
        gate = 0.5 + 0.5 * bent
        hidden = (pre * gate).astype(bf16)
        result = result + mm(hidden, w_down, NT)
        grad_hidden = mm(grad_top, w_down, NN)
        bend = (0.5 * pre) * (1.0 - bent * bent) * (slope + 3.0 * slope * 0.044715 * square)
        grad_pre = (grad_hidden * (gate + bend)).astype(bf16)
        gb_o[:, s * hid : (s + 1) * hid] += jnp.sum(grad_pre.astype(f32), axis=0, keepdims=True)
        gw = acc_m if s == 0 else acc_o
        gw[:, down:top] += mm(grad_top, hidden, TN)
        gw[:, :hid] += mm(normed, grad_pre, TN)
        grad_normed = grad_normed + mm(grad_pre, w_up, NT)
    out_o[...] = result.astype(bf16)
    grad_middle = grad_top_f + normalize_back(grad_normed * small[2:3], hat, rstd)
    mid_o[...] = grad_middle
    gs_o[...] += jnp.concatenate(
        [
            jnp.zeros((2, width), f32),
            jnp.sum(grad_normed * hat, axis=0, keepdims=True),
            jnp.sum(grad_normed, axis=0, keepdims=True),
            jnp.sum(grad_middle, axis=0, keepdims=True),
            jnp.sum(grad_top_f, axis=0, keepdims=True),
            jnp.zeros((2, width), f32),
        ],
        axis=0,
    )
    grad_branch = grad_middle.astype(bf16)
    lane = lax.broadcasted_iota(jnp.int32, (tok.shape[0], HEAD), 1)
    for s in range(2):
        gw = acc_m if s == 0 else acc_o
        gw[:, top:] += mm(grad_branch, mixed[s], TN)
        grad_mixed = mm(grad_branch, weight(s, top, last), NN).astype(bf16)
        product = grad_mixed.astype(f32) * mixed[s].astype(f32)
        rough = product.astype(bf16)
        fine = (product - rough.astype(f32)).astype(bf16)
        inner = mm(rough, pick[...], NN) + mm(fine, pick[...], NN)
        out = do_m if s == 0 else do_o
        for h in range(heads):
            total = -inner[:, h * LANES + HEAD : (h + 1) * LANES]
            first = total.astype(bf16)
            rest = (total - first.astype(f32)).astype(bf16)
            tail = jnp.where(lane == 0, first.astype(f32), rest.astype(f32)).astype(bf16)
            out[h] = jnp.concatenate([grad_mixed[:, h * HEAD : (h + 1) * HEAD], tail], axis=1)

    @pl.when(i == pl.num_programs(0) - 1)
    def _():
        gw_m[...] = acc_m[...].astype(bf16)
        gw_o[...] = acc_o[...].astype(bf16)


def feed(who, tok, cot, mix_m, mix_o, weights, small, bias, heads, block=512):
    length, width = tok.shape
    half = heads * HEAD
    outer, _, inner, cols = weights.shape
    hid = (cols - half) // 2
    by_rows = lambda n: pl.BlockSpec((block, n), lambda i, *_: (i, 0))
    by_heads = pl.BlockSpec((heads, block, LANES), lambda i, *_: (0, i, 0))
    return pl.pallas_call(
        functools.partial(feed_body, heads=heads, width=width, hid=hid),
        grid_spec=pltpu.PrefetchScalarGridSpec(
            num_scalar_prefetch=1,
            grid=(length // block,),
            in_specs=[
                by_rows(width),
                by_rows(width),
                by_rows(half),
                by_rows(half),
                pl.BlockSpec((outer, 1, inner, cols), lambda i, who: (0, who[0], 0, 0)),
                pl.BlockSpec((outer, 1, inner, cols), lambda i, who: (0, 1 - who[0], 0, 0)),
                whole(8, width),
                whole(1, 2 * hid),
            ],
            out_specs=[
                by_rows(width),
                by_rows(width),
                by_heads,
                by_heads,
                whole(width, cols),
                whole(width, cols),
                whole(8, width),
                whole(1, 2 * hid),
            ],
            scratch_shapes=[
                pltpu.VMEM((width, cols), f32),
                pltpu.VMEM((width, cols), f32),
                pltpu.VMEM((half, heads * LANES), bf16),
            ],
        ),
        out_shape=[
            jax.ShapeDtypeStruct((length, width), bf16),
            jax.ShapeDtypeStruct((length, width), f32),
            jax.ShapeDtypeStruct((heads, length, LANES), bf16),
            jax.ShapeDtypeStruct((heads, length, LANES), bf16),
            jax.ShapeDtypeStruct((width, cols), bf16),
            jax.ShapeDtypeStruct((width, cols), bf16),
            jax.ShapeDtypeStruct((8, width), f32),
            jax.ShapeDtypeStruct((1, 2 * hid), f32),
        ],
        compiler_params=params(),
        cost_estimate=cost(12 * length * width * cols, 40 << 20, length * 2 * hid),
        name="feed",
    )(who, tok, cot, mix_m, mix_o, weights, weights, small, bias)


def attend_back_body(
    base, many, n, who, do_m, do_o, k_h, vt_h, qa_h, qt_h, dq_h, dk_h, dv_h,
    k, vt, qa, qt, do, dot, dk, dv, dq, dq_s, dk_s, dv_s, pa, pb, ga, gb, sems, outs, *, block, step, heads
):
    length = k.shape[1]
    own = length // 2
    wide = 512
    mine = pl.multiple_of(who[0] * own, own)
    other = pl.multiple_of((1 - who[0]) * own, own)
    inward = [
        pltpu.make_async_copy(do_m, do.at[:, pl.ds(mine, own), :], sems.at[0]),
        pltpu.make_async_copy(do_o, do.at[:, pl.ds(other, own), :], sems.at[1]),
        pltpu.make_async_copy(k_h, k, sems.at[2]),
        pltpu.make_async_copy(vt_h, vt, sems.at[3]),
        pltpu.make_async_copy(qa_h, qa, sems.at[4]),
        pltpu.make_async_copy(qt_h, qt, sems.at[5]),
    ]
    for copy in inward:
        copy.start()
    dk[...] = jnp.zeros_like(dk)
    dv[...] = jnp.zeros_like(dv)
    dq[...] = jnp.zeros_like(dq)

    def begin(i, carry):
        qs = pl.ds(pl.multiple_of(i * wide, wide), wide)
        for h in range(heads):
            dot[h, :, qs] = do[h, qs, :].T[:HEAD]
        return carry

    inward[0].wait()
    inward[1].wait()
    lax.fori_loop(0, length // wide, begin, 0)
    for copy in inward[2:]:
        copy.wait()
    first, after, slices = tiles(base, many, block, step)
    probs_at, grads_at = (pa, pb), (ga, gb)

    def fill(s, q, kk):
        qs, ks = slices(q, kk)
        for h in range(heads):
            probs = jnp.exp(mm(qa[h, qs, :], k[h, ks, :], NT))
            probs_at[s][h] = probs.astype(bf16)
            grads_at[s][h] = (probs * mm(do[h, qs, :], vt[h, :, ks], NN)).astype(bf16)

    def use(s, q, kk):
        qs, ks = slices(q, kk)
        for h in range(heads):
            dv[h, :, ks] += mm(dot[h, :, qs], probs_at[s][h], NN)
            dk[h, :, ks] += mm(qt[h, :, qs], grads_at[s][h], NN)
            dq[h, qs, :] += mm(grads_at[s][h], k[h, ks, :], NN)

    run_tiles(n[0], first, after, fill, use)
    outward = []
    for h in range(heads):
        rows = slice(h * HEAD, (h + 1) * HEAD)
        dk_s[rows, :] = dk[h].astype(bf16)
        dv_s[rows, :] = dv[h].astype(bf16)
        outward.append(pltpu.make_async_copy(dk_s.at[rows, :], dk_h.at[rows, :], outs.at[2 * h]))
        outward.append(pltpu.make_async_copy(dv_s.at[rows, :], dv_h.at[rows, :], outs.at[2 * h + 1]))
        outward[-2].start()
        outward[-1].start()
    scale = 1.0 / math.sqrt(HEAD)

    def finish(i, carry):
        qs = pl.ds(pl.multiple_of(i * wide, wide), wide)
        dq_s[qs, :] = jnp.concatenate([dq[h, qs, :][:, :HEAD] * scale for h in range(heads)], axis=1).astype(bf16)
        return carry

    for part in range(2):
        rows = slice(part * own, (part + 1) * own)
        lax.fori_loop(part * own // wide, (part + 1) * own // wide, finish, 0)
        outward.append(pltpu.make_async_copy(dq_s.at[rows, :], dq_h.at[rows, :], outs.at[2 * heads + part]))
        outward[-1].start()
    for copy in outward:
        copy.wait()


def attend_back(base, many, n, who, qa, k, qt, vt, do_m, do_o, block, step):
    heads, length, _ = k.shape
    half = heads * HEAD
    return pl.pallas_call(
        functools.partial(attend_back_body, block=block, step=step, heads=heads),
        in_specs=[IN_SMEM] * 4 + [IN_HBM] * 6,
        out_specs=[IN_HBM] * 3,
        scratch_shapes=[
            pltpu.VMEM((heads, length, LANES), bf16),
            pltpu.VMEM((heads, LANES, length), bf16),
            pltpu.VMEM((heads, length, LANES), bf16),
            pltpu.VMEM((heads, HEAD, length), bf16),
            pltpu.VMEM((heads, length, LANES), bf16),
            pltpu.VMEM((heads, HEAD, length), bf16),
            pltpu.VMEM((heads, HEAD, length), f32),
            pltpu.VMEM((heads, HEAD, length), f32),
            pltpu.VMEM((heads, length, LANES), f32),
            pltpu.VMEM((length, half), bf16),
            pltpu.VMEM((half, length), bf16),
            pltpu.VMEM((half, length), bf16),
        ]
        + [pltpu.VMEM((heads, block, step), bf16)] * 4
        + [pltpu.SemaphoreType.DMA((6,)), pltpu.SemaphoreType.DMA((2 * heads + 2,))],
        out_shape=[
            jax.ShapeDtypeStruct((length, half), bf16),
            jax.ShapeDtypeStruct((half, length), bf16),
            jax.ShapeDtypeStruct((half, length), bf16),
        ],
        compiler_params=params(),
        cost_estimate=cost(20 * heads * length * length * LANES, 24 << 20, heads * length * length),
        name="attend_back",
    )(base, many, n, who, do_m, do_o, k, vt, qa, qt)


def unproject_body(normed, dq, dk, dv, gw, acc_q, acc_kv):
    half = dq.shape[1]

    @pl.when(pl.program_id(0) == 0)
    def _():
        acc_q[...] = jnp.zeros_like(acc_q)
        acc_kv[...] = jnp.zeros_like(acc_kv)

    rows = normed[...]
    acc_q[...] += mm(rows, dq[...], TN)
    acc_kv[:half] += mm(dk[...], rows, NN)
    acc_kv[half:] += mm(dv[...], rows, NN)

    @pl.when(pl.program_id(0) == pl.num_programs(0) - 1)
    def _():
        gw[...] = jnp.concatenate([acc_q[...].astype(bf16), acc_kv[...].T.astype(bf16)], axis=1)


def unproject(normed, dq, dk, dv, block=1024):
    length, width = normed.shape
    half = dq.shape[1]
    return pl.pallas_call(
        unproject_body,
        grid=(length // block,),
        in_specs=[
            pl.BlockSpec((block, width), lambda i: (i, 0)),
            pl.BlockSpec((block, half), lambda i: (i, 0)),
            pl.BlockSpec((half, block), lambda i: (0, i)),
            pl.BlockSpec((half, block), lambda i: (0, i)),
        ],
        out_specs=whole(width, 3 * half),
        out_shape=jax.ShapeDtypeStruct((width, 3 * half), bf16),
        scratch_shapes=[pltpu.VMEM((width, half), f32), pltpu.VMEM((2 * half, width), f32)],
        compiler_params=params(),
        cost_estimate=cost(6 * length * width * half, 12 << 20),
        name="unproject",
    )(normed, dq, dk, dv)


def normed_grad(dq, dk, dv, w):
    half = dq.shape[1]
    return (
        mm(dq[...], w[:, :half], NT)
        + mm(dk[...].T, w[:, half : 2 * half], NT)
        + mm(dv[...].T, w[:, 2 * half :], NT)
    )


def partial_body(who, dq, dk, dv, w, gn):
    gn[...] = normed_grad(dq, dk, dv, w).astype(bf16)


def partial_grad(who, dq, dk, dv, w, block=1024):
    length, half = dq.shape
    own, width = length // 2, w.shape[0]
    steps = own // block
    cols = pl.BlockSpec((half, block), lambda i, who: (0, i + (1 - who[0]) * steps))
    return pl.pallas_call(
        partial_body,
        grid_spec=pltpu.PrefetchScalarGridSpec(
            num_scalar_prefetch=1,
            grid=(steps,),
            in_specs=[
                pl.BlockSpec((block, half), lambda i, who: (i + (1 - who[0]) * steps, 0)),
                cols,
                cols,
                whole(width, 3 * half),
            ],
            out_specs=pl.BlockSpec((block, width), lambda i, who: (i, 0)),
        ),
        out_shape=jax.ShapeDtypeStruct((own, width), bf16),
        compiler_params=params(),
        cost_estimate=cost(0, 1 << 20),
        name="partial_grad",
    )(who, dq, dk, dv, w)


def finish_body(who, dq, dk, dv, w, tok, gn_o, mid, small, out, gs):
    @pl.when(pl.program_id(0) == 0)
    def _():
        gs[...] = jnp.zeros_like(gs)

    hat, rstd = normalize(tok[...].astype(f32))
    grad = normed_grad(dq, dk, dv, w) + gn_o[...].astype(f32)
    out[...] = (mid[...] + normalize_back(grad * small[0:1], hat, rstd)).astype(bf16)
    gs[...] += jnp.concatenate(
        [
            jnp.sum(grad * hat, axis=0, keepdims=True),
            jnp.sum(grad, axis=0, keepdims=True),
            jnp.zeros((6, grad.shape[1]), f32),
        ],
        axis=0,
    )


def finish(who, dq, dk, dv, w, tok, gn_o, mid, small, block=512):
    own, width = tok.shape
    half = dq.shape[1]
    steps = own // block
    rows = pl.BlockSpec((block, width), lambda i, who: (i, 0))
    cols = pl.BlockSpec((half, block), lambda i, who: (0, i + who[0] * steps))
    return pl.pallas_call(
        finish_body,
        grid_spec=pltpu.PrefetchScalarGridSpec(
            num_scalar_prefetch=1,
            grid=(steps,),
            in_specs=[
                pl.BlockSpec((block, half), lambda i, who: (i + who[0] * steps, 0)),
                cols,
                cols,
                whole(width, 3 * half),
                rows,
                rows,
                rows,
                whole(8, width),
            ],
            out_specs=[rows, whole(8, width)],
        ),
        out_shape=[jax.ShapeDtypeStruct((own, width), bf16), jax.ShapeDtypeStruct((8, width), f32)],
        compiler_params=params(),
        cost_estimate=cost(0, 1 << 20),
        name="finish",
    )(who, dq, dk, dv, w, tok, gn_o, mid, small)


def adamw(weight, grad, first, second, rate, decay):
    first = BETA_ONE * first + (1.0 - BETA_ONE) * grad
    second = BETA_TWO * second + (1.0 - BETA_TWO) * grad * grad
    fixed_one = first / (1.0 - BETA_ONE**STEP)
    fixed_two = second / (1.0 - BETA_TWO**STEP)
    weight = weight - rate * (fixed_one / (jnp.sqrt(fixed_two) + ADAM_EPS) + decay * weight)
    return (weight, first, second)


def swap(values):
    return lax.ppermute(values, "dp", [(0, 1), (1, 0)])


def across(values, count, bit):
    return lax.ppermute(values, "fsdp", [(i, i ^ bit) for i in range(count)])


def gather(shard, count, beside):
    if count < 8 or count & (count - 1):
        return lax.all_gather(shard, "fsdp", axis=0), beside
    me = lax.axis_index("fsdp")
    held = shard
    depth = 0
    bit = count // 2
    while bit > 2:
        there = across(held, count, bit)
        above = (me & bit) != 0
        held = jnp.where(above, jnp.stack([there, held], axis=depth), jnp.stack([held, there], axis=depth))
        depth += 1
        bit //= 2
    many = count // 4
    held, beside = lax.optimization_barrier((held.reshape((many,) + shard.shape), beside))
    side, line = across(held, count, 1), across(held, count, 2)
    corner = jnp.concatenate([across(side[: many // 2], count, 2), across(line[many // 2 :], count, 1)], axis=0)
    place = me & 3

    def block(j):
        at = place ^ j
        return jnp.where(at == 0, held, jnp.where(at == 1, side, jnp.where(at == 2, line, corner)))

    return jnp.stack([block(j) for j in range(4)], axis=1).reshape((count,) + shard.shape), beside


def local(
    tokens,
    segments,
    cotangent,
    w_qkv,
    w_out,
    w_up,
    w_down,
    small_params,
    up_bias,
    first_qkv,
    first_out,
    first_up,
    first_down,
    first_small,
    first_bias,
    second_qkv,
    second_out,
    second_up,
    second_down,
    second_small,
    second_bias,
    *,
    count,
):
    own, width = tokens.shape[1:]
    length = segments.shape[1]
    heads = HEADS // 2
    half = heads * HEAD
    hid = w_up.shape[1] // 2
    cols = 2 * hid + half
    rows = w_qkv.shape[0]
    out_fan = max(1, width * (DOCS + 1) // length)
    rate_out = RATE_MATRIX * math.sqrt(width / out_fan)
    dp = lax.axis_index("dp")
    block, step = 256, 512

    def mine_of(values, axis):
        return lax.dynamic_index_in_dim(values, dp, axis, keepdims=False)

    def in_order(mine, other, axis):
        return jnp.where(
            dp == 0, jnp.stack([mine, other], axis=axis), jnp.stack([other, mine], axis=axis)
        )

    tok = tokens[0]
    tok_other = swap(tok)
    seg = segments[0]
    below = jnp.sum((seg[None, :] < seg[::block, None]).astype(jnp.int32), axis=1)
    until = jnp.sum((seg[None, :] <= seg[block - 1 :: block, None]).astype(jnp.int32), axis=1)
    low = below // LANES * LANES
    high = -(-until // LANES) * LANES
    many = -(-(high - low) // step)
    base = jnp.maximum(high - many * step, 0)
    n = jnp.sum(many).reshape(1)
    who = dp.astype(jnp.int32).reshape(1)

    wide = 3 * half
    tiny_len = 6 * rows + up_bias.shape[0]
    lines = -(-tiny_len // wide)
    qkv_shard = mine_of(w_qkv.reshape(rows, 3, 2, half), 2).reshape(rows, wide)
    tiny = jnp.concatenate([small_params.T.reshape(-1), up_bias])
    tiny = jnp.pad(tiny, (0, lines * wide - tiny_len)).reshape(lines, wide)
    first_all, (base, many, n, tok_other) = gather(
        jnp.concatenate([qkv_shard, tiny], axis=0).astype(bf16), count, (base, many, n, tok_other)
    )
    w_one = first_all[:, :rows].reshape(width, wide)
    tiny_all = first_all[:, rows:].reshape(count, -1)[:, :tiny_len].astype(f32)
    small = jnp.pad(tiny_all[:, : 6 * rows].reshape(width, 6).T, ((0, 2), (0, 0)))
    bias_all = tiny_all[:, 6 * rows :].reshape(1, 2, hid)
    bias = jnp.where(dp == 0, bias_all, bias_all[:, ::-1]).reshape(1, 2 * hid)
    rest_shard = jnp.concatenate(
        [
            mine_of(w_up.reshape(rows, 2, hid), 1),
            mine_of(w_down.reshape(2, hid, rows), 0).T,
            mine_of(w_out.reshape(2, half, rows), 0).T,
        ],
        axis=1,
    ).astype(bf16)
    rest_shard, w_one = lax.optimization_barrier((rest_shard, w_one))
    rest_all = lax.all_gather(rest_shard, ("fsdp", "dp"), axis=0).reshape(count, 2, rows, cols)
    if rows % 16:
        rest_all = rest_all.transpose(1, 0, 2, 3).reshape(1, 2, width, cols)

    mix_m, mix_send, queries, normed, keys, queries_t, values_t = attend(
        base, many, n, who, tok, tok_other, w_one, small, segments, heads, block, step
    )
    mix_o = swap(mix_send)
    layer_out, grad_mid, do_m, do_send, gw_m, gw_send, gs_two, gb = feed(
        who, tok, cotangent[0], mix_m, mix_o, rest_all, small, bias, heads
    )
    gb_all = jnp.where(dp == 0, gb.reshape(2, hid), gb.reshape(2, hid)[::-1]).reshape(count, -1)
    grad_tiny = jnp.concatenate([gs_two[:6].T.reshape(count, 6 * rows), gb_all], axis=1)
    grad_tiny = jnp.pad(grad_tiny, ((0, 0), (0, cols - tiny_len))).reshape(count, 1, cols)
    gw_pair = (gw_m.astype(f32) + swap(gw_send).astype(f32)).reshape(count, rows, cols)
    gw_pair = jnp.concatenate([gw_pair, grad_tiny], axis=1).astype(bf16)
    do_o, gw_pair = lax.optimization_barrier((swap(do_send), gw_pair))
    arrived = lax.all_to_all(gw_pair, "fsdp", 0, 0)
    dq, dk, dv = attend_back(base, many, n, who, queries, keys, queries_t, values_t, do_m, do_o, block, step)
    dq, arrived = lax.optimization_barrier((dq, arrived))
    gw_one = unproject(normed, dq, dk, dv)
    spread_one = lax.all_to_all(gw_one.reshape(count, rows, wide), "fsdp", 0, 0)
    dq, gw_one = lax.optimization_barrier((dq, gw_one))
    gn_o = swap(partial_grad(who, dq, dk, dv, w_one))
    input_grad, gs_one = finish(who, dq, dk, dv, w_one, tok, gn_o, grad_mid, small)
    spread_one, gs_one = lax.optimization_barrier((spread_one, gs_one))
    rest_sum = jnp.sum(arrived.astype(f32), axis=0)
    rest_grad, tiny_mine = rest_sum[:rows], rest_sum[rows]
    rest_other = swap(rest_grad)
    rest_squares = jnp.sum(rest_grad * rest_grad)
    qkv_mine = jnp.sum(spread_one.astype(f32), axis=0)
    squares = jnp.sum(qkv_mine * qkv_mine) + rest_squares
    every = jnp.concatenate(
        [gs_one[:2].reshape(-1), jnp.broadcast_to(squares, (LANES,)), tiny_mine[:tiny_len]]
    )
    every = jnp.broadcast_to(every, (2 * count, 1, every.shape[0]))
    qkv_mine, every = lax.optimization_barrier((qkv_mine, every))
    every = lax.all_to_all(every, ("dp", "fsdp"), 0, 0)[:, 0]
    qkv_other = swap(qkv_mine)
    norm_one = jnp.sum(every[:, : 2 * width], axis=0).reshape(2, width)
    tiny_all = jnp.sum(every[:, 2 * width + LANES :].reshape(2, count, tiny_len), axis=0)
    total_squares = jnp.sum(every[:, 2 * width]) + jnp.sum(norm_one * norm_one) + jnp.sum(tiny_all * tiny_all)
    grad_norm = jnp.sqrt(total_squares)
    me = lax.axis_index("fsdp")
    tiny_own = lax.dynamic_index_in_dim(tiny_all, me, 0, keepdims=False)
    norm_own = lax.dynamic_slice_in_dim(norm_one, me * rows, rows, 1)

    own_qkv = in_order(qkv_mine.reshape(rows, 3, half), qkv_other.reshape(rows, 3, half), 2).reshape(rows, -1)
    own_up = in_order(rest_grad[:, :hid], rest_other[:, :hid], 1).reshape(rows, -1)
    own_down = in_order(rest_grad[:, hid : 2 * hid], rest_other[:, hid : 2 * hid], 1).reshape(rows, -1).T
    own_out = in_order(rest_grad[:, 2 * hid :], rest_other[:, 2 * hid :], 1).reshape(rows, -1).T
    own_small = tiny_own[: 6 * rows].reshape(rows, 6).T + jnp.pad(norm_own, ((0, 4), (0, 0)))
    own_bias = tiny_own[6 * rows :]
    factor = jnp.minimum(1.0, CLIP_NORM / (grad_norm + 1e-06))
    new_qkv, new_first_qkv, new_second_qkv = adamw(
        w_qkv, own_qkv * factor, first_qkv, second_qkv, RATE_MATRIX, DECAY_MATRIX
    )
    new_out, new_first_out, new_second_out = adamw(
        w_out, own_out * factor, first_out, second_out, rate_out, DECAY_MATRIX
    )
    new_up, new_first_up, new_second_up = adamw(
        w_up, own_up * factor, first_up, second_up, RATE_MATRIX, DECAY_MATRIX
    )
    new_down, new_first_down, new_second_down = adamw(
        w_down, own_down * factor, first_down, second_down, RATE_MATRIX, DECAY_MATRIX
    )
    new_small, new_first_small, new_second_small = adamw(
        small_params, own_small * factor, first_small, second_small, RATE_VECTOR, 0.0
    )
    new_bias, new_first_bias, new_second_bias = adamw(
        up_bias, own_bias * factor, first_bias, second_bias, RATE_VECTOR, 0.0
    )
    return (
        layer_out[None],
        input_grad[None],
        grad_norm,
        new_qkv,
        new_out,
        new_up,
        new_down,
        new_small,
        new_bias,
        new_first_qkv,
        new_first_out,
        new_first_up,
        new_first_down,
        new_first_small,
        new_first_bias,
        new_second_qkv,
        new_second_out,
        new_second_up,
        new_second_down,
        new_second_small,
        new_second_bias,
    )


def solution(mesh):
    rows, cols, flat = P("fsdp", None), P(None, "fsdp"), P("fsdp")
    by_token = P("fsdp", "dp", None)
    weights = (rows, cols, rows, cols, cols, flat)
    in_specs = (by_token, rows, by_token) + 3 * weights
    out_specs = (by_token, by_token, P()) + 3 * weights
    body = functools.partial(local, count=mesh.shape["fsdp"])
    return jax.shard_map(body, mesh=mesh, in_specs=in_specs, out_specs=out_specs, check_vma=False)
```

```python
import functools
import math

import jax
import jax.numpy as jnp
from jax import lax
from jax.experimental import pallas as pl
from jax.experimental.pallas import tpu as pltpu
from jax.sharding import PartitionSpec as P

HEADS = 8
DOCS = 4
STEP = 10


LN_EPS = 1e-05
CLIP_NORM = 1.0
BETA_ONE = 0.9
BETA_TWO = 0.999
ADAM_EPS = 1e-08
RATE_MATRIX = 0.04
RATE_VECTOR = 0.5
DECAY_MATRIX = 0.1
MASKED_SCORE = -1e30
LOWEST = -3e38
SAFE_SCORE = 60.0

HEAD = 64
LANES = 128
SEG_AT = HEAD
LSE_AT = HEAD + 16
VMEM = 60 << 20

bf16 = jnp.bfloat16
f32 = jnp.float32
NN = (((1,), (0,)), ((), ()))
NT = (((1,), (1,)), ((), ()))
TN = (((0,), (0,)), ((), ()))


def mm(left, right, dims):
    return lax.dot_general(left, right, dims, preferred_element_type=f32)


def params():
    return pltpu.CompilerParams(vmem_limit_bytes=VMEM)


def whole(*shape):
    return pl.BlockSpec(shape, lambda i, *_: (0,) * len(shape))


def cost(flops, nbytes, trans=0):
    return pl.CostEstimate(flops=int(flops), bytes_accessed=int(nbytes), transcendentals=int(trans))


def normalize(values):
    centre = jnp.mean(values, axis=-1, keepdims=True)
    centered = values - centre
    spread = jnp.mean(centered * centered, axis=-1, keepdims=True)
    rstd = lax.rsqrt(spread + LN_EPS)
    return centered * rstd, rstd


def normalize_back(grad, hat, rstd):
    along = jnp.mean(grad, axis=-1, keepdims=True)
    across = jnp.mean(grad * hat, axis=-1, keepdims=True)
    return rstd * (grad - along - hat * across)


def tiles(base, many, block, step):
    def after(q, t):
        last = t + 1 >= many[q]
        return jnp.where(last, jnp.minimum(q + 1, many.shape[0] - 1), q), jnp.where(last, 0, t + 1)

    def slices(q, t):
        return (
            pl.ds(pl.multiple_of(q * block, block), block),
            pl.ds(pl.multiple_of(base[q] + t * step, LANES), step),
        )

    return (jnp.int32(0), jnp.int32(0)), after, slices


def run_tiles(n, first, after, fill, use):
    @pl.when(n > 0)
    def _():
        fill(0, *first)

        def pair(_, at):
            mid = after(*at)
            end = after(*mid)
            use(0, *at)
            fill(1, *mid)
            use(1, *mid)
            fill(0, *end)
            return end

        at = lax.fori_loop(0, (n - 1) // 2, pair, first)

        @pl.when(n % 2 == 1)
        def _():
            use(0, *at)

        @pl.when(n % 2 == 0)
        def _():
            mid = after(*at)
            fill(1, *mid)
            use(0, *at)
            use(1, *mid)


def attend_body(
    base, many, n, who, tok_m, tok_o, w, small, seg, mine_h, other_h, qa_h, normed_h, k_h, qt_h, vt_h,
    tok, normed_s, k, qt, vt, qa, mixed_s, wqt, wvt, pick, qtop, ktop, acc, top, slot_a, slot_b, sem_in, sem_out, sem_end,
    *, block, step, heads, depth, part,
):
    length, width = tok.shape
    own = length // 2
    half = heads * HEAD
    mine = pl.multiple_of(who[0] * own, own)
    other = pl.multiple_of((1 - who[0]) * own, own)
    inward = [
        pltpu.make_async_copy(tok_m, tok.at[pl.ds(mine, own), :], sem_in.at[0]),
        pltpu.make_async_copy(tok_o, tok.at[pl.ds(other, own), :], sem_in.at[1]),
    ]
    for copy in inward:
        copy.start()
    wqt[...] = w[:, :half].T
    wvt[...] = w[:, 2 * half :].T
    rows = lax.broadcasted_iota(jnp.int32, pick.shape, 0)
    cols = lax.broadcasted_iota(jnp.int32, pick.shape, 1)
    pick[...] = jnp.where(rows // HEAD == cols, 1.0, 0.0).astype(bf16)
    qtop[...] = jnp.zeros_like(qtop)
    ktop[...] = jnp.zeros_like(ktop)
    acc[...] = jnp.zeros_like(acc)
    for copy in inward:
        copy.wait()

    def outward(i):
        at = pl.ds(pl.multiple_of(i * part, part), part)
        return [
            pltpu.make_async_copy(normed_s.at[at, :], normed_h.at[at, :], sem_out.at[0, i]),
            pltpu.make_async_copy(k.at[:, at, :], k_h.at[:, at, :], sem_out.at[1, i]),
            pltpu.make_async_copy(qt.at[:, :HEAD, at], qt_h.at[:, :, at], sem_out.at[2, i]),
            pltpu.make_async_copy(vt.at[:, :, at], vt_h.at[:, :, at], sem_out.at[3, i]),
        ]

    def project(i, carry):
        at = pl.ds(pl.multiple_of(i * part, part), part)
        hat, _ = normalize(tok[at, :].astype(f32))
        normed = (hat * small[0:1] + small[1:2]).astype(bf16)
        normed_s[at, :] = normed
        keys = mm(normed, w[:, half : 2 * half], NN).astype(bf16)
        queries = mm(wqt[...], normed, NT).astype(bf16).astype(f32) * (1.0 / math.sqrt(HEAD))
        values = mm(wvt[...], normed, NT).astype(bf16)
        rows = lax.broadcasted_iota(jnp.int32, (HEAD, part), 0)
        ones = jnp.where(rows < 2, 1.0, 0.0).astype(bf16)
        known = rows <= DOCS
        same = rows == seg[:, at]
        qmask = jnp.where(known & ~same, 1.0, 0.0).astype(bf16)
        lse_rows = (rows >= LSE_AT - HEAD) & (rows < LSE_AT - HEAD + 3)
        kmask = jnp.where(known & same, MASKED_SCORE, jnp.where(lse_rows, -1.0, 0.0)).T.astype(bf16)
        keys_f = keys.astype(f32)
        lengths = mm((keys_f * keys_f).astype(bf16), pick[...], NN)
        ktop[0:1] = jnp.maximum(ktop[0:1], jnp.max(lengths, axis=0, keepdims=True))
        for h in range(heads):
            own_rows = slice(h * HEAD, (h + 1) * HEAD)
            qtop[h : h + 1] = jnp.maximum(
                qtop[h : h + 1], jnp.sum(queries[own_rows] * queries[own_rows], axis=0, keepdims=True)
            )
            k[h, at, :] = jnp.concatenate([keys[:, own_rows], kmask], axis=1)
            qt[h, :, at] = jnp.concatenate([queries[own_rows].astype(bf16), qmask], axis=0)
            vt[h, :, at] = jnp.concatenate([values[own_rows], ones], axis=0)
        for copy in outward(i):
            copy.start()
        return carry

    lax.fori_loop(0, length // part, project, 0)

    first, after, slices = tiles(base, many, block, step)
    slots = (slot_a, slot_b)

    def fill(s, q, t):
        qs, ks = slices(q, t)
        for h in range(heads):
            slots[s][h] = jnp.exp(mm(k[h, ks, :], qt[h, :, qs], NN)).astype(bf16)

    def use(s, q, t):
        qs, ks = slices(q, t)
        for h in range(heads):
            acc[h, :, qs] += mm(vt[h, :depth, ks], slots[s][h], NN)

    def careful(_, at):
        qs, ks = slices(*at)
        for h in range(heads):
            score = mm(k[h, ks, :], qt[h, :, qs], NN)
            old = top[h : h + 1, qs]
            now = jnp.maximum(old, jnp.max(score, axis=0, keepdims=True))
            probs = jnp.exp(score - now).astype(bf16)
            acc[h, :, qs] = acc[h, :, qs] * jnp.exp(old - now) + mm(vt[h, :depth, ks], probs, NN)
            top[h : h + 1, qs] = now
        return after(*at)

    fits = jnp.max(qtop[...]) * jnp.max(ktop[...]) <= SAFE_SCORE * SAFE_SCORE
    top[...] = jnp.where(fits, 0.0, LOWEST) + jnp.zeros_like(top)
    run_tiles(jnp.where(fits, n[0], 0), first, after, fill, use)
    lax.fori_loop(0, jnp.where(fits, 0, n[0]), careful, first)

    wide = 512
    row = lax.broadcasted_iota(jnp.int32, (16, wide), 0)

    def ending(i):
        qs = pl.ds(pl.multiple_of(i * wide, wide), wide)
        return pltpu.make_async_copy(qa.at[:, qs, :], qa_h.at[:, qs, :], sem_end.at[i])

    def finish(i, carry):
        qs = pl.ds(pl.multiple_of(i * wide, wide), wide)
        mixed = []
        for h in range(heads):
            totals = acc[h, HEAD : HEAD + 1, qs]
            mixed.append((acc[h, :HEAD, qs] / totals).astype(bf16))
            lse = top[h : h + 1, qs] + jnp.log(totals)
            one = lse.astype(bf16).astype(f32)
            two = (lse - one).astype(bf16).astype(f32)
            three = lse - one - two
            tail = jnp.where(row == 0, one, jnp.where(row == 1, two, jnp.where(row == 2, three, 0.0)))
            rest = jnp.zeros((LANES - LSE_AT - 16, wide), bf16)
            full = jnp.concatenate([qt[h, :LSE_AT, qs], tail.astype(bf16), rest], axis=0)
            qa[h, qs, :] = full.T
        mixed_s[qs, :] = jnp.concatenate(mixed, axis=0).T
        ending(i).start()
        return carry

    lax.fori_loop(0, length // wide, finish, 0)
    last = [
        pltpu.make_async_copy(mixed_s.at[pl.ds(mine, own), :], mine_h, sem_in.at[0]),
        pltpu.make_async_copy(mixed_s.at[pl.ds(other, own), :], other_h, sem_in.at[1]),
    ]
    for copy in last:
        copy.start()
    for i in range(length // part):
        for copy in outward(i):
            copy.wait()
    for i in range(length // wide):
        ending(i).wait()
    for copy in last:
        copy.wait()


IN_VMEM = pl.BlockSpec(memory_space=pltpu.VMEM)
IN_SMEM = pl.BlockSpec(memory_space=pltpu.SMEM)
IN_HBM = pl.BlockSpec(memory_space=pl.ANY)


def attend(base, many, n, who, tok_m, tok_o, w, small, seg, heads, block, step, part=1024):
    own, width = tok_m.shape
    length = 2 * own
    half = heads * HEAD
    depth = HEAD + 16
    return pl.pallas_call(
        functools.partial(attend_body, block=block, step=step, heads=heads, depth=depth, part=part),
        in_specs=[IN_SMEM] * 4 + [IN_HBM] * 2 + [IN_VMEM] * 3,
        out_specs=[IN_HBM] * 7,
        scratch_shapes=[
            pltpu.VMEM((length, width), bf16),
            pltpu.VMEM((length, width), bf16),
            pltpu.VMEM((heads, length, LANES), bf16),
            pltpu.VMEM((heads, LANES, length), bf16),
            pltpu.VMEM((heads, LANES, length), bf16),
            pltpu.VMEM((heads, length, LANES), bf16),
            pltpu.VMEM((length, half), bf16),
            pltpu.VMEM((half, width), bf16),
            pltpu.VMEM((half, width), bf16),
            pltpu.VMEM((half, LANES), bf16),
            pltpu.VMEM((8, part), f32),
            pltpu.VMEM((8, LANES), f32),
            pltpu.VMEM((heads, depth, length), f32),
            pltpu.VMEM((8, length), f32),
            pltpu.VMEM((heads, step, block), bf16),
            pltpu.VMEM((heads, step, block), bf16),
            pltpu.SemaphoreType.DMA((2,)),
            pltpu.SemaphoreType.DMA((4, length // part)),
            pltpu.SemaphoreType.DMA((length // 512,)),
        ],
        out_shape=[
            jax.ShapeDtypeStruct((own, half), bf16),
            jax.ShapeDtypeStruct((own, half), bf16),
            jax.ShapeDtypeStruct((heads, length, LANES), bf16),
            jax.ShapeDtypeStruct((length, width), bf16),
            jax.ShapeDtypeStruct((heads, length, LANES), bf16),
            jax.ShapeDtypeStruct((heads, HEAD, length), bf16),
            jax.ShapeDtypeStruct((heads, LANES, length), bf16),
        ],
        compiler_params=params(),
        cost_estimate=cost(8 * heads * length * length * LANES, 20 << 20, heads * length * length),
        name="attend",
    )(base, many, n, who, tok_m, tok_o, w, small, seg)


def feed_body(
    tok, cot, mix_m, mix_o, w_m, w_o, small, bias, out_o, mid_o, do_m, do_o, gw_m, gw_o, gs_o, gb_o, acc_m, acc_o, pick, *, heads, width, hid
):
    i = pl.program_id(0)
    half = heads * HEAD
    down = hid
    top = 2 * hid

    @pl.when(i == 0)
    def _():
        acc_m[...] = jnp.zeros_like(acc_m)
        acc_o[...] = jnp.zeros_like(acc_o)
        gs_o[...] = jnp.zeros_like(gs_o)
        gb_o[...] = jnp.zeros_like(gb_o)
        rows = lax.broadcasted_iota(jnp.int32, pick.shape, 0)
        cols = lax.broadcasted_iota(jnp.int32, pick.shape, 1)
        inside = (cols >= rows // HEAD * LANES + HEAD) & (cols < rows // HEAD * LANES + HEAD + 2)
        pick[...] = jnp.where(inside, 1.0, 0.0).astype(bf16)

    grad_top = cot[...]
    grad_top_f = grad_top.astype(f32)
    mixed = (mix_m[...], mix_o[...])

    def weight(s, first, last):
        part = (w_m, w_o)[s][:, :, first:last]
        return part.reshape(width, last - first)

    last = top + half
    branch = mm(mixed[0], weight(0, top, last), NT) + mm(mixed[1], weight(1, top, last), NT)
    middle = tok[...].astype(f32) + branch + small[4:5]
    hat, rstd = normalize(middle)
    normed = (hat * small[2:3] + small[3:4]).astype(bf16)
    result = middle + small[5:6]
    grad_normed = jnp.zeros_like(middle)
    for s in range(2):
        w_up = weight(s, 0, hid)
        w_down = weight(s, down, top)
        pre = mm(normed, w_up, NN) + bias[:, s * hid : (s + 1) * hid]
        square = pre * pre
        slope = math.sqrt(2.0 / math.pi)
        bent = jnp.tanh(pre * (slope + slope * 0.044715 * square))
        gate = 0.5 + 0.5 * bent
        hidden = (pre * gate).astype(bf16)
        result = result + mm(hidden, w_down, NT)
        grad_hidden = mm(grad_top, w_down, NN)
        bend = (0.5 * pre) * (1.0 - bent * bent) * (slope + 3.0 * slope * 0.044715 * square)
        grad_pre = (grad_hidden * (gate + bend)).astype(bf16)
        gb_o[:, s * hid : (s + 1) * hid] += jnp.sum(grad_pre.astype(f32), axis=0, keepdims=True)
        gw = acc_m if s == 0 else acc_o
        gw[:, down:top] += mm(grad_top, hidden, TN)
        gw[:, :hid] += mm(normed, grad_pre, TN)
        grad_normed = grad_normed + mm(grad_pre, w_up, NT)
    out_o[...] = result.astype(bf16)
    grad_middle = grad_top_f + normalize_back(grad_normed * small[2:3], hat, rstd)
    mid_o[...] = grad_middle
    gs_o[...] += jnp.concatenate(
        [
            jnp.zeros((2, width), f32),
            jnp.sum(grad_normed * hat, axis=0, keepdims=True),
            jnp.sum(grad_normed, axis=0, keepdims=True),
            jnp.sum(grad_middle, axis=0, keepdims=True),
            jnp.sum(grad_top_f, axis=0, keepdims=True),
            jnp.zeros((2, width), f32),
        ],
        axis=0,
    )
    grad_branch = grad_middle.astype(bf16)
    lane = lax.broadcasted_iota(jnp.int32, (tok.shape[0], HEAD), 1)
    for s in range(2):
        gw = acc_m if s == 0 else acc_o
        gw[:, top:] += mm(grad_branch, mixed[s], TN)
        grad_mixed = mm(grad_branch, weight(s, top, last), NN).astype(bf16)
        product = grad_mixed.astype(f32) * mixed[s].astype(f32)
        rough = product.astype(bf16)
        fine = (product - rough.astype(f32)).astype(bf16)
        inner = mm(rough, pick[...], NN) + mm(fine, pick[...], NN)
        out = do_m if s == 0 else do_o
        for h in range(heads):
            total = -inner[:, h * LANES + HEAD : (h + 1) * LANES]
            first = total.astype(bf16)
            rest = (total - first.astype(f32)).astype(bf16)
            tail = jnp.where(lane == 0, first.astype(f32), rest.astype(f32)).astype(bf16)
            out[h] = jnp.concatenate([grad_mixed[:, h * HEAD : (h + 1) * HEAD], tail], axis=1)

    @pl.when(i == pl.num_programs(0) - 1)
    def _():
        gw_m[...] = acc_m[...].astype(bf16)
        gw_o[...] = acc_o[...].astype(bf16)


def feed(tok, cot, mix_m, mix_o, w_m, w_o, small, bias, heads, block=512):
    length, width = tok.shape
    half = heads * HEAD
    cols = w_m.shape[2]
    hid = (cols - half) // 2
    by_rows = lambda n: pl.BlockSpec((block, n), lambda i, *_: (i, 0))
    by_heads = pl.BlockSpec((heads, block, LANES), lambda i, *_: (0, i, 0))
    return pl.pallas_call(
        functools.partial(feed_body, heads=heads, width=width, hid=hid),
        grid_spec=pltpu.PrefetchScalarGridSpec(
            num_scalar_prefetch=0,
            grid=(length // block,),
            in_specs=[
                by_rows(width),
                by_rows(width),
                by_rows(half),
                by_rows(half),
                whole(*w_m.shape),
                whole(*w_o.shape),
                whole(8, width),
                whole(1, 2 * hid),
            ],
            out_specs=[
                by_rows(width),
                by_rows(width),
                by_heads,
                by_heads,
                whole(width, cols),
                whole(width, cols),
                whole(8, width),
                whole(1, 2 * hid),
            ],
            scratch_shapes=[
                pltpu.VMEM((width, cols), f32),
                pltpu.VMEM((width, cols), f32),
                pltpu.VMEM((half, heads * LANES), bf16),
            ],
        ),
        out_shape=[
            jax.ShapeDtypeStruct((length, width), bf16),
            jax.ShapeDtypeStruct((length, width), f32),
            jax.ShapeDtypeStruct((heads, length, LANES), bf16),
            jax.ShapeDtypeStruct((heads, length, LANES), bf16),
            jax.ShapeDtypeStruct((width, cols), bf16),
            jax.ShapeDtypeStruct((width, cols), bf16),
            jax.ShapeDtypeStruct((8, width), f32),
            jax.ShapeDtypeStruct((1, 2 * hid), f32),
        ],
        compiler_params=params(),
        cost_estimate=cost(12 * length * width * cols, 40 << 20, length * 2 * hid),
        name="feed",
    )(tok, cot, mix_m, mix_o, w_m, w_o, small, bias)


def attend_back_body(
    base, many, n, who, do_m, do_o, k_h, vt_h, qa_h, qt_h, dq_h, dk_h, dv_h,
    k, vt, qa, qt, do, dot, dk, dv, dq, dq_s, dk_s, dv_s, pa, pb, ga, gb, sems, outs, *, block, step, heads
):
    length = k.shape[1]
    own = length // 2
    wide = 512
    mine = pl.multiple_of(who[0] * own, own)
    other = pl.multiple_of((1 - who[0]) * own, own)
    inward = [
        pltpu.make_async_copy(do_m, do.at[:, pl.ds(mine, own), :], sems.at[0]),
        pltpu.make_async_copy(do_o, do.at[:, pl.ds(other, own), :], sems.at[1]),
        pltpu.make_async_copy(k_h, k, sems.at[2]),
        pltpu.make_async_copy(vt_h, vt, sems.at[3]),
        pltpu.make_async_copy(qa_h, qa, sems.at[4]),
        pltpu.make_async_copy(qt_h, qt, sems.at[5]),
    ]
    for copy in inward:
        copy.start()
    dk[...] = jnp.zeros_like(dk)
    dv[...] = jnp.zeros_like(dv)
    dq[...] = jnp.zeros_like(dq)

    def begin(i, carry):
        qs = pl.ds(pl.multiple_of(i * wide, wide), wide)
        for h in range(heads):
            dot[h, :, qs] = do[h, qs, :].T[:HEAD]
        return carry

    inward[0].wait()
    inward[1].wait()
    lax.fori_loop(0, length // wide, begin, 0)
    for copy in inward[2:]:
        copy.wait()
    first, after, slices = tiles(base, many, block, step)
    probs_at, grads_at = (pa, pb), (ga, gb)

    def fill(s, q, kk):
        qs, ks = slices(q, kk)
        for h in range(heads):
            probs = jnp.exp(mm(qa[h, qs, :], k[h, ks, :], NT))
            probs_at[s][h] = probs.astype(bf16)
            grads_at[s][h] = (probs * mm(do[h, qs, :], vt[h, :, ks], NN)).astype(bf16)

    def use(s, q, kk):
        qs, ks = slices(q, kk)
        for h in range(heads):
            dv[h, :, ks] += mm(dot[h, :, qs], probs_at[s][h], NN)
            dk[h, :, ks] += mm(qt[h, :, qs], grads_at[s][h], NN)
            dq[h, qs, :] += mm(grads_at[s][h], k[h, ks, :], NN)

    run_tiles(n[0], first, after, fill, use)
    outward = []
    for h in range(heads):
        rows = slice(h * HEAD, (h + 1) * HEAD)
        dk_s[rows, :] = dk[h].astype(bf16)
        dv_s[rows, :] = dv[h].astype(bf16)
        outward.append(pltpu.make_async_copy(dk_s.at[rows, :], dk_h.at[rows, :], outs.at[2 * h]))
        outward.append(pltpu.make_async_copy(dv_s.at[rows, :], dv_h.at[rows, :], outs.at[2 * h + 1]))
        outward[-2].start()
        outward[-1].start()
    scale = 1.0 / math.sqrt(HEAD)

    def finish(i, carry):
        qs = pl.ds(pl.multiple_of(i * wide, wide), wide)
        dq_s[qs, :] = jnp.concatenate([dq[h, qs, :][:, :HEAD] * scale for h in range(heads)], axis=1).astype(bf16)
        return carry

    for part in range(2):
        rows = slice(part * own, (part + 1) * own)
        lax.fori_loop(part * own // wide, (part + 1) * own // wide, finish, 0)
        outward.append(pltpu.make_async_copy(dq_s.at[rows, :], dq_h.at[rows, :], outs.at[2 * heads + part]))
        outward[-1].start()
    for copy in outward:
        copy.wait()


def attend_back(base, many, n, who, qa, k, qt, vt, do_m, do_o, block, step):
    heads, length, _ = k.shape
    half = heads * HEAD
    return pl.pallas_call(
        functools.partial(attend_back_body, block=block, step=step, heads=heads),
        in_specs=[IN_SMEM] * 4 + [IN_HBM] * 6,
        out_specs=[IN_HBM] * 3,
        scratch_shapes=[
            pltpu.VMEM((heads, length, LANES), bf16),
            pltpu.VMEM((heads, LANES, length), bf16),
            pltpu.VMEM((heads, length, LANES), bf16),
            pltpu.VMEM((heads, HEAD, length), bf16),
            pltpu.VMEM((heads, length, LANES), bf16),
            pltpu.VMEM((heads, HEAD, length), bf16),
            pltpu.VMEM((heads, HEAD, length), f32),
            pltpu.VMEM((heads, HEAD, length), f32),
            pltpu.VMEM((heads, length, LANES), f32),
            pltpu.VMEM((length, half), bf16),
            pltpu.VMEM((half, length), bf16),
            pltpu.VMEM((half, length), bf16),
        ]
        + [pltpu.VMEM((heads, block, step), bf16)] * 4
        + [pltpu.SemaphoreType.DMA((6,)), pltpu.SemaphoreType.DMA((2 * heads + 2,))],
        out_shape=[
            jax.ShapeDtypeStruct((length, half), bf16),
            jax.ShapeDtypeStruct((half, length), bf16),
            jax.ShapeDtypeStruct((half, length), bf16),
        ],
        compiler_params=params(),
        cost_estimate=cost(20 * heads * length * length * LANES, 24 << 20, heads * length * length),
        name="attend_back",
    )(base, many, n, who, do_m, do_o, k, vt, qa, qt)


def unproject_body(normed, dq, dk, dv, gw, acc_q, acc_kv):
    half = dq.shape[1]

    @pl.when(pl.program_id(0) == 0)
    def _():
        acc_q[...] = jnp.zeros_like(acc_q)
        acc_kv[...] = jnp.zeros_like(acc_kv)

    rows = normed[...]
    acc_q[...] += mm(rows, dq[...], TN)
    acc_kv[:half] += mm(dk[...], rows, NN)
    acc_kv[half:] += mm(dv[...], rows, NN)

    @pl.when(pl.program_id(0) == pl.num_programs(0) - 1)
    def _():
        gw[...] = jnp.concatenate([acc_q[...].astype(bf16), acc_kv[...].T.astype(bf16)], axis=1)


def unproject(normed, dq, dk, dv, block=1024):
    length, width = normed.shape
    half = dq.shape[1]
    return pl.pallas_call(
        unproject_body,
        grid=(length // block,),
        in_specs=[
            pl.BlockSpec((block, width), lambda i: (i, 0)),
            pl.BlockSpec((block, half), lambda i: (i, 0)),
            pl.BlockSpec((half, block), lambda i: (0, i)),
            pl.BlockSpec((half, block), lambda i: (0, i)),
        ],
        out_specs=whole(width, 3 * half),
        out_shape=jax.ShapeDtypeStruct((width, 3 * half), bf16),
        scratch_shapes=[pltpu.VMEM((width, half), f32), pltpu.VMEM((2 * half, width), f32)],
        compiler_params=params(),
        cost_estimate=cost(6 * length * width * half, 12 << 20),
        name="unproject",
    )(normed, dq, dk, dv)


def normed_grad(dq, dk, dv, w):
    half = dq.shape[1]
    return (
        mm(dq[...], w[:, :half], NT)
        + mm(dk[...].T, w[:, half : 2 * half], NT)
        + mm(dv[...].T, w[:, 2 * half :], NT)
    )


def partial_body(who, dq, dk, dv, w, gn):
    gn[...] = normed_grad(dq, dk, dv, w).astype(bf16)


def partial_grad(who, dq, dk, dv, w, block=1024):
    length, half = dq.shape
    own, width = length // 2, w.shape[0]
    steps = own // block
    cols = pl.BlockSpec((half, block), lambda i, who: (0, i + (1 - who[0]) * steps))
    return pl.pallas_call(
        partial_body,
        grid_spec=pltpu.PrefetchScalarGridSpec(
            num_scalar_prefetch=1,
            grid=(steps,),
            in_specs=[
                pl.BlockSpec((block, half), lambda i, who: (i + (1 - who[0]) * steps, 0)),
                cols,
                cols,
                whole(width, 3 * half),
            ],
            out_specs=pl.BlockSpec((block, width), lambda i, who: (i, 0)),
        ),
        out_shape=jax.ShapeDtypeStruct((own, width), bf16),
        compiler_params=params(),
        cost_estimate=cost(0, 1 << 20),
        name="partial_grad",
    )(who, dq, dk, dv, w)


def finish_body(who, dq, dk, dv, w, tok, gn_o, mid, small, out, gs):
    @pl.when(pl.program_id(0) == 0)
    def _():
        gs[...] = jnp.zeros_like(gs)

    hat, rstd = normalize(tok[...].astype(f32))
    grad = normed_grad(dq, dk, dv, w) + gn_o[...].astype(f32)
    out[...] = (mid[...] + normalize_back(grad * small[0:1], hat, rstd)).astype(bf16)
    gs[...] += jnp.concatenate(
        [
            jnp.sum(grad * hat, axis=0, keepdims=True),
            jnp.sum(grad, axis=0, keepdims=True),
            jnp.zeros((6, grad.shape[1]), f32),
        ],
        axis=0,
    )


def finish(who, dq, dk, dv, w, tok, gn_o, mid, small, block=512):
    own, width = tok.shape
    half = dq.shape[1]
    steps = own // block
    rows = pl.BlockSpec((block, width), lambda i, who: (i, 0))
    cols = pl.BlockSpec((half, block), lambda i, who: (0, i + who[0] * steps))
    return pl.pallas_call(
        finish_body,
        grid_spec=pltpu.PrefetchScalarGridSpec(
            num_scalar_prefetch=1,
            grid=(steps,),
            in_specs=[
                pl.BlockSpec((block, half), lambda i, who: (i + who[0] * steps, 0)),
                cols,
                cols,
                whole(width, 3 * half),
                rows,
                rows,
                rows,
                whole(8, width),
            ],
            out_specs=[rows, whole(8, width)],
        ),
        out_shape=[jax.ShapeDtypeStruct((own, width), bf16), jax.ShapeDtypeStruct((8, width), f32)],
        compiler_params=params(),
        cost_estimate=cost(0, 1 << 20),
        name="finish",
    )(who, dq, dk, dv, w, tok, gn_o, mid, small)


def adamw(weight, grad, first, second, rate, decay):
    first = BETA_ONE * first + (1.0 - BETA_ONE) * grad
    second = BETA_TWO * second + (1.0 - BETA_TWO) * grad * grad
    fixed_one = first / (1.0 - BETA_ONE**STEP)
    fixed_two = second / (1.0 - BETA_TWO**STEP)
    weight = weight - rate * (fixed_one / (jnp.sqrt(fixed_two) + ADAM_EPS) + decay * weight)
    return (weight, first, second)


def swap(values):
    return lax.ppermute(values, "dp", [(0, 1), (1, 0)])


def across(values, count, bit):
    return lax.ppermute(values, "fsdp", [(i, i ^ bit) for i in range(count)])


def gather(shard, count, beside):
    if count < 8 or count & (count - 1):
        return lax.all_gather(shard, "fsdp", axis=0), beside
    me = lax.axis_index("fsdp")
    held = shard
    depth = 0
    bit = count // 2
    while bit > 2:
        there = across(held, count, bit)
        above = (me & bit) != 0
        held = jnp.where(above, jnp.stack([there, held], axis=depth), jnp.stack([held, there], axis=depth))
        depth += 1
        bit //= 2
    many = count // 4
    held, beside = lax.optimization_barrier((held.reshape((many,) + shard.shape), beside))
    side, line = across(held, count, 1), across(held, count, 2)
    corner = jnp.concatenate([across(side[: many // 2], count, 2), across(line[many // 2 :], count, 1)], axis=0)
    place = me & 3

    def block(j):
        at = place ^ j
        return jnp.where(at == 0, held, jnp.where(at == 1, side, jnp.where(at == 2, line, corner)))

    return jnp.stack([block(j) for j in range(4)], axis=1).reshape((count,) + shard.shape), beside


def local(
    tokens,
    segments,
    cotangent,
    w_qkv,
    w_out,
    w_up,
    w_down,
    small_params,
    up_bias,
    first_qkv,
    first_out,
    first_up,
    first_down,
    first_small,
    first_bias,
    second_qkv,
    second_out,
    second_up,
    second_down,
    second_small,
    second_bias,
    *,
    count,
):
    own, width = tokens.shape[1:]
    length = segments.shape[1]
    heads = HEADS // 2
    half = heads * HEAD
    hid = w_up.shape[1] // 2
    cols = 2 * hid + half
    rows = w_qkv.shape[0]
    out_fan = max(1, width * (DOCS + 1) // length)
    rate_out = RATE_MATRIX * math.sqrt(width / out_fan)
    dp = lax.axis_index("dp")
    block, step = 256, 512

    def mine_of(values, size, axis, start=0):
        return lax.dynamic_slice_in_dim(values, start + dp * size, size, axis)

    def in_order(mine, other, axis):
        return jnp.where(
            dp == 0, jnp.stack([mine, other], axis=axis), jnp.stack([other, mine], axis=axis)
        )

    tok = tokens[0]
    tok_other = swap(tok)
    seg = segments[0]
    below = jnp.sum((seg[None, :] < seg[::block, None]).astype(jnp.int32), axis=1)
    until = jnp.sum((seg[None, :] <= seg[block - 1 :: block, None]).astype(jnp.int32), axis=1)
    low = below // LANES * LANES
    high = -(-until // LANES) * LANES
    many = -(-(high - low) // step)
    base = jnp.maximum(high - many * step, 0)
    n = jnp.sum(many).reshape(1)
    who = dp.astype(jnp.int32).reshape(1)

    wide = 3 * half
    tiny_len = 6 * rows + up_bias.shape[0]
    lines = -(-tiny_len // wide)
    qkv_shard = jnp.concatenate([mine_of(w_qkv, half, 1, part * width) for part in range(3)], axis=1)
    tiny = jnp.concatenate([small_params.T.reshape(-1), up_bias])
    tiny = jnp.pad(tiny, (0, lines * wide - tiny_len)).reshape(lines, wide)
    first_all, (base, many, n, tok_other, up, down, out) = gather(
        jnp.concatenate([qkv_shard, tiny], axis=0).astype(bf16),
        count,
        (base, many, n, tok_other, w_up, w_down, w_out),
    )
    w_one = first_all[:, :rows].reshape(width, wide)
    tiny_all = first_all[:, rows:].reshape(count, -1)[:, :tiny_len].astype(f32)
    small = jnp.pad(tiny_all[:, : 6 * rows].reshape(width, 6).T, ((0, 2), (0, 0)))
    bias_all = tiny_all[:, 6 * rows :].reshape(1, 2, hid)
    bias = jnp.where(dp == 0, bias_all, bias_all[:, ::-1]).reshape(1, 2 * hid)
    rest_shard = jnp.concatenate(
        [mine_of(up, hid, 1), mine_of(down, hid, 0).T, mine_of(out, half, 0).T], axis=1
    ).astype(bf16)
    rest_all = lax.all_to_all(jnp.broadcast_to(rest_shard, (count, rows, cols)), "fsdp", 0, 0)

    mix_m, mix_send, queries, normed, keys, queries_t, values_t = attend(
        base, many, n, who, tok, tok_other, w_one, small, segments, heads, block, step
    )
    mix_send, rest_all = lax.optimization_barrier((mix_send, rest_all))
    mix_o, rest_other = swap(mix_send), swap(rest_all)
    if rows % 16:
        rest_all, rest_other = (half_of.reshape(1, width, cols) for half_of in (rest_all, rest_other))
    layer_out, grad_mid, do_m, do_send, gw_m, gw_send, gs_two, gb = feed(
        tok, cotangent[0], mix_m, mix_o, rest_all, rest_other, small, bias, heads
    )
    gb_all = jnp.where(dp == 0, gb.reshape(2, hid), gb.reshape(2, hid)[::-1]).reshape(count, -1)
    grad_tiny = jnp.concatenate([gs_two[:6].T.reshape(count, 6 * rows), gb_all], axis=1)
    grad_tiny = jnp.pad(grad_tiny, ((0, 0), (0, cols - tiny_len))).reshape(count, 1, cols)
    gw_pair = (gw_m.astype(f32) + swap(gw_send).astype(f32)).reshape(count, rows, cols)
    gw_pair = jnp.concatenate([gw_pair, grad_tiny], axis=1).astype(bf16)
    do_o, gw_pair = lax.optimization_barrier((swap(do_send), gw_pair))
    arrived = lax.all_to_all(gw_pair, "fsdp", 0, 0)
    dq, dk, dv = attend_back(base, many, n, who, queries, keys, queries_t, values_t, do_m, do_o, block, step)
    dq, arrived = lax.optimization_barrier((dq, arrived))
    gw_one = unproject(normed, dq, dk, dv)
    spread_one = lax.all_to_all(gw_one.reshape(count, rows, wide), "fsdp", 0, 0)
    dq, gw_one = lax.optimization_barrier((dq, gw_one))
    gn_o = swap(partial_grad(who, dq, dk, dv, w_one))
    input_grad, gs_one = finish(who, dq, dk, dv, w_one, tok, gn_o, grad_mid, small)
    spread_one, gs_one = lax.optimization_barrier((spread_one, gs_one))
    rest_sum = jnp.sum(arrived.astype(f32), axis=0)
    rest_grad, tiny_mine = rest_sum[:rows], rest_sum[rows]
    rest_grad_other = swap(rest_grad)
    rest_squares = jnp.sum(rest_grad * rest_grad)
    qkv_mine = jnp.sum(spread_one.astype(f32), axis=0)
    squares = jnp.sum(qkv_mine * qkv_mine) + rest_squares
    every = jnp.concatenate(
        [gs_one[:2].reshape(-1), jnp.broadcast_to(squares, (LANES,)), tiny_mine[:tiny_len]]
    )
    every = jnp.broadcast_to(every, (2 * count, 1, every.shape[0]))
    qkv_mine, every = lax.optimization_barrier((qkv_mine, every))
    every = lax.all_to_all(every, ("dp", "fsdp"), 0, 0)[:, 0]
    qkv_other = swap(qkv_mine)
    norm_one = jnp.sum(every[:, : 2 * width], axis=0).reshape(2, width)
    tiny_all = jnp.sum(every[:, 2 * width + LANES :].reshape(2, count, tiny_len), axis=0)
    total_squares = jnp.sum(every[:, 2 * width]) + jnp.sum(norm_one * norm_one) + jnp.sum(tiny_all * tiny_all)
    grad_norm = jnp.sqrt(total_squares)
    me = lax.axis_index("fsdp")
    tiny_own = lax.dynamic_index_in_dim(tiny_all, me, 0, keepdims=False)
    norm_own = lax.dynamic_slice_in_dim(norm_one, me * rows, rows, 1)

    own_qkv = in_order(qkv_mine.reshape(rows, 3, half), qkv_other.reshape(rows, 3, half), 2).reshape(rows, -1)
    own_up = in_order(rest_grad[:, :hid], rest_grad_other[:, :hid], 1).reshape(rows, -1)
    own_down = in_order(rest_grad[:, hid : 2 * hid], rest_grad_other[:, hid : 2 * hid], 1).reshape(rows, -1).T
    own_out = in_order(rest_grad[:, 2 * hid :], rest_grad_other[:, 2 * hid :], 1).reshape(rows, -1).T
    own_small = tiny_own[: 6 * rows].reshape(rows, 6).T + jnp.pad(norm_own, ((0, 4), (0, 0)))
    own_bias = tiny_own[6 * rows :]
    factor = jnp.minimum(1.0, CLIP_NORM / (grad_norm + 1e-06))
    new_qkv, new_first_qkv, new_second_qkv = adamw(
        w_qkv, own_qkv * factor, first_qkv, second_qkv, RATE_MATRIX, DECAY_MATRIX
    )
    new_out, new_first_out, new_second_out = adamw(
        w_out, own_out * factor, first_out, second_out, rate_out, DECAY_MATRIX
    )
    new_up, new_first_up, new_second_up = adamw(
        w_up, own_up * factor, first_up, second_up, RATE_MATRIX, DECAY_MATRIX
    )
    new_down, new_first_down, new_second_down = adamw(
        w_down, own_down * factor, first_down, second_down, RATE_MATRIX, DECAY_MATRIX
    )
    new_small, new_first_small, new_second_small = adamw(
        small_params, own_small * factor, first_small, second_small, RATE_VECTOR, 0.0
    )
    new_bias, new_first_bias, new_second_bias = adamw(
        up_bias, own_bias * factor, first_bias, second_bias, RATE_VECTOR, 0.0
    )
    return (
        layer_out[None],
        input_grad[None],
        grad_norm,
        new_qkv,
        new_out,
        new_up,
        new_down,
        new_small,
        new_bias,
        new_first_qkv,
        new_first_out,
        new_first_up,
        new_first_down,
        new_first_small,
        new_first_bias,
        new_second_qkv,
        new_second_out,
        new_second_up,
        new_second_down,
        new_second_small,
        new_second_bias,
    )


def solution(mesh):
    rows, cols, flat = P("fsdp", None), P(None, "fsdp"), P("fsdp")
    by_token = P("fsdp", "dp", None)
    weights = (rows, cols, rows, cols, cols, flat)
    in_specs = (by_token, rows, by_token) + 3 * weights
    out_specs = (by_token, by_token, P()) + 3 * weights
    body = functools.partial(local, count=mesh.shape["fsdp"])
    return jax.shard_map(body, mesh=mesh, in_specs=in_specs, out_specs=out_specs, check_vma=False)
```

```python
import functools
import math

import jax
import jax.numpy as jnp
from jax import lax
from jax.experimental import pallas as pl
from jax.experimental.pallas import tpu as pltpu
from jax.sharding import PartitionSpec as P

HEADS = 8
DOCS = 4
STEP = 10


LN_EPS = 1e-05
CLIP_NORM = 1.0
BETA_ONE = 0.9
BETA_TWO = 0.999
ADAM_EPS = 1e-08
RATE_MATRIX = 0.04
RATE_VECTOR = 0.5
DECAY_MATRIX = 0.1
MASKED_SCORE = -1e30
LOWEST = -3e38
SAFE_SCORE = 60.0

HEAD = 64
LANES = 128
SEG_AT = HEAD
LSE_AT = HEAD + 16
VMEM = 60 << 20

bf16 = jnp.bfloat16
f32 = jnp.float32
NN = (((1,), (0,)), ((), ()))
NT = (((1,), (1,)), ((), ()))
TN = (((0,), (0,)), ((), ()))


def mm(left, right, dims):
    return lax.dot_general(left, right, dims, preferred_element_type=f32)


def params():
    return pltpu.CompilerParams(vmem_limit_bytes=VMEM)


def whole(*shape):
    return pl.BlockSpec(shape, lambda i, *_: (0,) * len(shape))


def cost(flops, nbytes, trans=0):
    return pl.CostEstimate(flops=int(flops), bytes_accessed=int(nbytes), transcendentals=int(trans))


def normalize(values):
    centre = jnp.mean(values, axis=-1, keepdims=True)
    centered = values - centre
    spread = jnp.mean(centered * centered, axis=-1, keepdims=True)
    rstd = lax.rsqrt(spread + LN_EPS)
    return centered * rstd, rstd


def normalize_back(grad, hat, rstd):
    along = jnp.mean(grad, axis=-1, keepdims=True)
    across = jnp.mean(grad * hat, axis=-1, keepdims=True)
    return rstd * (grad - along - hat * across)


def tiles(base, many, block, step):
    def after(q, t):
        last = t + 1 >= many[q]
        return jnp.where(last, jnp.minimum(q + 1, many.shape[0] - 1), q), jnp.where(last, 0, t + 1)

    def slices(q, t):
        return (
            pl.ds(pl.multiple_of(q * block, block), block),
            pl.ds(pl.multiple_of(base[q] + t * step, LANES), step),
        )

    return (jnp.int32(0), jnp.int32(0)), after, slices


def run_tiles(n, first, after, fill, use):
    @pl.when(n > 0)
    def _():
        fill(0, *first)

        def pair(_, at):
            mid = after(*at)
            end = after(*mid)
            use(0, *at)
            fill(1, *mid)
            use(1, *mid)
            fill(0, *end)
            return end

        at = lax.fori_loop(0, (n - 1) // 2, pair, first)

        @pl.when(n % 2 == 1)
        def _():
            use(0, *at)

        @pl.when(n % 2 == 0)
        def _():
            mid = after(*at)
            fill(1, *mid)
            use(0, *at)
            use(1, *mid)


def attend_body(
    base, many, n, who, tok_m, tok_o, w, small, seg, mine_h, other_h, qa_h, normed_h, k_h, qt_h, vt_h,
    tok, normed_s, k, qt, vt, qa, mixed_s, wqt, wvt, pick, qtop, ktop, acc, top, slot_a, slot_b, sem_in, sem_out, sem_end,
    *, block, step, heads, depth, part,
):
    length, width = tok.shape
    own = length // 2
    half = heads * HEAD
    mine = pl.multiple_of(who[0] * own, own)
    other = pl.multiple_of((1 - who[0]) * own, own)
    inward = [
        pltpu.make_async_copy(tok_m, tok.at[pl.ds(mine, own), :], sem_in.at[0]),
        pltpu.make_async_copy(tok_o, tok.at[pl.ds(other, own), :], sem_in.at[1]),
    ]
    for copy in inward:
        copy.start()
    wqt[...] = w[:, :half].T
    wvt[...] = w[:, 2 * half :].T
    rows = lax.broadcasted_iota(jnp.int32, pick.shape, 0)
    cols = lax.broadcasted_iota(jnp.int32, pick.shape, 1)
    pick[...] = jnp.where(rows // HEAD == cols, 1.0, 0.0).astype(bf16)
    qtop[...] = jnp.zeros_like(qtop)
    ktop[...] = jnp.zeros_like(ktop)
    acc[...] = jnp.zeros_like(acc)
    for copy in inward:
        copy.wait()

    def outward(i):
        at = pl.ds(pl.multiple_of(i * part, part), part)
        return [
            pltpu.make_async_copy(normed_s.at[at, :], normed_h.at[at, :], sem_out.at[0, i]),
            pltpu.make_async_copy(k.at[:, at, :], k_h.at[:, at, :], sem_out.at[1, i]),
            pltpu.make_async_copy(qt.at[:, :HEAD, at], qt_h.at[:, :, at], sem_out.at[2, i]),
            pltpu.make_async_copy(vt.at[:, :, at], vt_h.at[:, :, at], sem_out.at[3, i]),
        ]

    def project(i, carry):
        at = pl.ds(pl.multiple_of(i * part, part), part)
        hat, _ = normalize(tok[at, :].astype(f32))
        normed = (hat * small[0:1] + small[1:2]).astype(bf16)
        normed_s[at, :] = normed
        keys = mm(normed, w[:, half : 2 * half], NN).astype(bf16)
        queries = mm(wqt[...], normed, NT).astype(bf16).astype(f32) * (1.0 / math.sqrt(HEAD))
        values = mm(wvt[...], normed, NT).astype(bf16)
        rows = lax.broadcasted_iota(jnp.int32, (HEAD, part), 0)
        ones = jnp.where(rows < 2, 1.0, 0.0).astype(bf16)
        known = rows <= DOCS
        same = rows == seg[:, at]
        qmask = jnp.where(known & ~same, 1.0, 0.0).astype(bf16)
        lse_rows = (rows >= LSE_AT - HEAD) & (rows < LSE_AT - HEAD + 3)
        kmask = jnp.where(known & same, MASKED_SCORE, jnp.where(lse_rows, -1.0, 0.0)).T.astype(bf16)
        keys_f = keys.astype(f32)
        lengths = mm((keys_f * keys_f).astype(bf16), pick[...], NN)
        ktop[0:1] = jnp.maximum(ktop[0:1], jnp.max(lengths, axis=0, keepdims=True))
        for h in range(heads):
            own_rows = slice(h * HEAD, (h + 1) * HEAD)
            qtop[h : h + 1] = jnp.maximum(
                qtop[h : h + 1], jnp.sum(queries[own_rows] * queries[own_rows], axis=0, keepdims=True)
            )
            k[h, at, :] = jnp.concatenate([keys[:, own_rows], kmask], axis=1)
            qt[h, :, at] = jnp.concatenate([queries[own_rows].astype(bf16), qmask], axis=0)
            vt[h, :, at] = jnp.concatenate([values[own_rows], ones], axis=0)
        for copy in outward(i):
            copy.start()
        return carry

    lax.fori_loop(0, length // part, project, 0)

    first, after, slices = tiles(base, many, block, step)
    slots = (slot_a, slot_b)

    def fill(s, q, t):
        qs, ks = slices(q, t)
        for h in range(heads):
            slots[s][h] = jnp.exp(mm(k[h, ks, :], qt[h, :, qs], NN)).astype(bf16)

    def use(s, q, t):
        qs, ks = slices(q, t)
        for h in range(heads):
            acc[h, :, qs] += mm(vt[h, :depth, ks], slots[s][h], NN)

    def careful(_, at):
        qs, ks = slices(*at)
        for h in range(heads):
            score = mm(k[h, ks, :], qt[h, :, qs], NN)
            old = top[h : h + 1, qs]
            now = jnp.maximum(old, jnp.max(score, axis=0, keepdims=True))
            probs = jnp.exp(score - now).astype(bf16)
            acc[h, :, qs] = acc[h, :, qs] * jnp.exp(old - now) + mm(vt[h, :depth, ks], probs, NN)
            top[h : h + 1, qs] = now
        return after(*at)

    fits = jnp.max(qtop[...]) * jnp.max(ktop[...]) <= SAFE_SCORE * SAFE_SCORE
    top[...] = jnp.where(fits, 0.0, LOWEST) + jnp.zeros_like(top)
    run_tiles(jnp.where(fits, n[0], 0), first, after, fill, use)
    lax.fori_loop(0, jnp.where(fits, 0, n[0]), careful, first)

    wide = 512
    row = lax.broadcasted_iota(jnp.int32, (16, wide), 0)

    def ending(i):
        qs = pl.ds(pl.multiple_of(i * wide, wide), wide)
        return pltpu.make_async_copy(qa.at[:, qs, :], qa_h.at[:, qs, :], sem_end.at[i])

    def finish(i, carry):
        qs = pl.ds(pl.multiple_of(i * wide, wide), wide)
        mixed = []
        for h in range(heads):
            totals = acc[h, HEAD : HEAD + 1, qs]
            mixed.append((acc[h, :HEAD, qs] / totals).astype(bf16))
            lse = top[h : h + 1, qs] + jnp.log(totals)
            one = lse.astype(bf16).astype(f32)
            two = (lse - one).astype(bf16).astype(f32)
            three = lse - one - two
            tail = jnp.where(row == 0, one, jnp.where(row == 1, two, jnp.where(row == 2, three, 0.0)))
            rest = jnp.zeros((LANES - LSE_AT - 16, wide), bf16)
            full = jnp.concatenate([qt[h, :LSE_AT, qs], tail.astype(bf16), rest], axis=0)
            qa[h, qs, :] = full.T
        mixed_s[qs, :] = jnp.concatenate(mixed, axis=0).T
        ending(i).start()
        return carry

    lax.fori_loop(0, length // wide, finish, 0)
    last = [
        pltpu.make_async_copy(mixed_s.at[pl.ds(mine, own), :], mine_h, sem_in.at[0]),
        pltpu.make_async_copy(mixed_s.at[pl.ds(other, own), :], other_h, sem_in.at[1]),
    ]
    for copy in last:
        copy.start()
    for i in range(length // part):
        for copy in outward(i):
            copy.wait()
    for i in range(length // wide):
        ending(i).wait()
    for copy in last:
        copy.wait()


IN_VMEM = pl.BlockSpec(memory_space=pltpu.VMEM)
IN_SMEM = pl.BlockSpec(memory_space=pltpu.SMEM)
IN_HBM = pl.BlockSpec(memory_space=pl.ANY)


def attend(base, many, n, who, tok_m, tok_o, w, small, seg, heads, block, step, part=1024):
    own, width = tok_m.shape
    length = 2 * own
    half = heads * HEAD
    depth = HEAD + 16
    return pl.pallas_call(
        functools.partial(attend_body, block=block, step=step, heads=heads, depth=depth, part=part),
        in_specs=[IN_SMEM] * 4 + [IN_HBM] * 2 + [IN_VMEM] * 3,
        out_specs=[IN_HBM] * 7,
        scratch_shapes=[
            pltpu.VMEM((length, width), bf16),
            pltpu.VMEM((length, width), bf16),
            pltpu.VMEM((heads, length, LANES), bf16),
            pltpu.VMEM((heads, LANES, length), bf16),
            pltpu.VMEM((heads, LANES, length), bf16),
            pltpu.VMEM((heads, length, LANES), bf16),
            pltpu.VMEM((length, half), bf16),
            pltpu.VMEM((half, width), bf16),
            pltpu.VMEM((half, width), bf16),
            pltpu.VMEM((half, LANES), bf16),
            pltpu.VMEM((8, part), f32),
            pltpu.VMEM((8, LANES), f32),
            pltpu.VMEM((heads, depth, length), f32),
            pltpu.VMEM((8, length), f32),
            pltpu.VMEM((heads, step, block), bf16),
            pltpu.VMEM((heads, step, block), bf16),
            pltpu.SemaphoreType.DMA((2,)),
            pltpu.SemaphoreType.DMA((4, length // part)),
            pltpu.SemaphoreType.DMA((length // 512,)),
        ],
        out_shape=[
            jax.ShapeDtypeStruct((own, half), bf16),
            jax.ShapeDtypeStruct((own, half), bf16),
            jax.ShapeDtypeStruct((heads, length, LANES), bf16),
            jax.ShapeDtypeStruct((length, width), bf16),
            jax.ShapeDtypeStruct((heads, length, LANES), bf16),
            jax.ShapeDtypeStruct((heads, HEAD, length), bf16),
            jax.ShapeDtypeStruct((heads, LANES, length), bf16),
        ],
        compiler_params=params(),
        cost_estimate=cost(8 * heads * length * length * LANES, 20 << 20, heads * length * length),
        name="attend",
    )(base, many, n, who, tok_m, tok_o, w, small, seg)


def feed_body(
    tok, cot, mix_m, mix_o, w_m, w_o, small, bias, out_o, mid_o, do_m, do_o, gw_m, gw_o, gs_o, gb_o, acc_m, acc_o, pick, *, heads, width, hid
):
    i = pl.program_id(0)
    half = heads * HEAD
    down = hid
    top = 2 * hid

    @pl.when(i == 0)
    def _():
        acc_m[...] = jnp.zeros_like(acc_m)
        acc_o[...] = jnp.zeros_like(acc_o)
        gs_o[...] = jnp.zeros_like(gs_o)
        gb_o[...] = jnp.zeros_like(gb_o)
        rows = lax.broadcasted_iota(jnp.int32, pick.shape, 0)
        cols = lax.broadcasted_iota(jnp.int32, pick.shape, 1)
        inside = (cols >= rows // HEAD * LANES + HEAD) & (cols < rows // HEAD * LANES + HEAD + 2)
        pick[...] = jnp.where(inside, 1.0, 0.0).astype(bf16)

    grad_top = cot[...]
    grad_top_f = grad_top.astype(f32)
    mixed = (mix_m[...], mix_o[...])

    def weight(s, first, last):
        part = (w_m, w_o)[s][:, :, first:last]
        return part.reshape(width, last - first)

    last = top + half
    branch = mm(mixed[0], weight(0, top, last), NT) + mm(mixed[1], weight(1, top, last), NT)
    middle = tok[...].astype(f32) + branch + small[4:5]
    hat, rstd = normalize(middle)
    normed = (hat * small[2:3] + small[3:4]).astype(bf16)
    result = middle + small[5:6]
    grad_normed = jnp.zeros_like(middle)
    for s in range(2):
        w_up = weight(s, 0, hid)
        w_down = weight(s, down, top)
        pre = mm(normed, w_up, NN) + bias[:, s * hid : (s + 1) * hid]
        square = pre * pre
        slope = math.sqrt(2.0 / math.pi)
        bent = jnp.tanh(pre * (slope + slope * 0.044715 * square))
        gate = 0.5 + 0.5 * bent
        hidden = (pre * gate).astype(bf16)
        result = result + mm(hidden, w_down, NT)
        grad_hidden = mm(grad_top, w_down, NN)
        bend = (0.5 * pre) * (1.0 - bent * bent) * (slope + 3.0 * slope * 0.044715 * square)
        grad_pre = (grad_hidden * (gate + bend)).astype(bf16)
        gb_o[:, s * hid : (s + 1) * hid] += jnp.sum(grad_pre.astype(f32), axis=0, keepdims=True)
        gw = acc_m if s == 0 else acc_o
        gw[:, down:top] += mm(grad_top, hidden, TN)
        gw[:, :hid] += mm(normed, grad_pre, TN)
        grad_normed = grad_normed + mm(grad_pre, w_up, NT)
    out_o[...] = result.astype(bf16)
    grad_middle = grad_top_f + normalize_back(grad_normed * small[2:3], hat, rstd)
    mid_o[...] = grad_middle
    gs_o[...] += jnp.concatenate(
        [
            jnp.zeros((2, width), f32),
            jnp.sum(grad_normed * hat, axis=0, keepdims=True),
            jnp.sum(grad_normed, axis=0, keepdims=True),
            jnp.sum(grad_middle, axis=0, keepdims=True),
            jnp.sum(grad_top_f, axis=0, keepdims=True),
            jnp.zeros((2, width), f32),
        ],
        axis=0,
    )
    grad_branch = grad_middle.astype(bf16)
    lane = lax.broadcasted_iota(jnp.int32, (tok.shape[0], HEAD), 1)
    for s in range(2):
        gw = acc_m if s == 0 else acc_o
        gw[:, top:] += mm(grad_branch, mixed[s], TN)
        grad_mixed = mm(grad_branch, weight(s, top, last), NN).astype(bf16)
        product = grad_mixed.astype(f32) * mixed[s].astype(f32)
        rough = product.astype(bf16)
        fine = (product - rough.astype(f32)).astype(bf16)
        inner = mm(rough, pick[...], NN) + mm(fine, pick[...], NN)
        out = do_m if s == 0 else do_o
        for h in range(heads):
            total = -inner[:, h * LANES + HEAD : (h + 1) * LANES]
            first = total.astype(bf16)
            rest = (total - first.astype(f32)).astype(bf16)
            tail = jnp.where(lane == 0, first.astype(f32), rest.astype(f32)).astype(bf16)
            out[h] = jnp.concatenate([grad_mixed[:, h * HEAD : (h + 1) * HEAD], tail], axis=1)

    @pl.when(i == pl.num_programs(0) - 1)
    def _():
        gw_m[...] = acc_m[...].astype(bf16)
        gw_o[...] = acc_o[...].astype(bf16)


def feed(tok, cot, mix_m, mix_o, w_m, w_o, small, bias, heads, block=512):
    length, width = tok.shape
    half = heads * HEAD
    cols = w_m.shape[2]
    hid = (cols - half) // 2
    by_rows = lambda n: pl.BlockSpec((block, n), lambda i, *_: (i, 0))
    by_heads = pl.BlockSpec((heads, block, LANES), lambda i, *_: (0, i, 0))
    return pl.pallas_call(
        functools.partial(feed_body, heads=heads, width=width, hid=hid),
        grid_spec=pltpu.PrefetchScalarGridSpec(
            num_scalar_prefetch=0,
            grid=(length // block,),
            in_specs=[
                by_rows(width),
                by_rows(width),
                by_rows(half),
                by_rows(half),
                whole(*w_m.shape),
                whole(*w_o.shape),
                whole(8, width),
                whole(1, 2 * hid),
            ],
            out_specs=[
                by_rows(width),
                by_rows(width),
                by_heads,
                by_heads,
                whole(width, cols),
                whole(width, cols),
                whole(8, width),
                whole(1, 2 * hid),
            ],
            scratch_shapes=[
                pltpu.VMEM((width, cols), f32),
                pltpu.VMEM((width, cols), f32),
                pltpu.VMEM((half, heads * LANES), bf16),
            ],
        ),
        out_shape=[
            jax.ShapeDtypeStruct((length, width), bf16),
            jax.ShapeDtypeStruct((length, width), f32),
            jax.ShapeDtypeStruct((heads, length, LANES), bf16),
            jax.ShapeDtypeStruct((heads, length, LANES), bf16),
            jax.ShapeDtypeStruct((width, cols), bf16),
            jax.ShapeDtypeStruct((width, cols), bf16),
            jax.ShapeDtypeStruct((8, width), f32),
            jax.ShapeDtypeStruct((1, 2 * hid), f32),
        ],
        compiler_params=params(),
        cost_estimate=cost(12 * length * width * cols, 40 << 20, length * 2 * hid),
        name="feed",
    )(tok, cot, mix_m, mix_o, w_m, w_o, small, bias)


def attend_back_body(
    base, many, n, who, do_m, do_o, k_h, vt_h, qa_h, qt_h, dq_h, dk_h, dv_h,
    k, vt, qa, qt, do, dot, dk, dv, dq, dq_s, dk_s, dv_s, pa, pb, ga, gb, sems, outs, *, block, step, heads
):
    length = k.shape[1]
    own = length // 2
    wide = 512
    mine = pl.multiple_of(who[0] * own, own)
    other = pl.multiple_of((1 - who[0]) * own, own)
    inward = [
        pltpu.make_async_copy(do_m, do.at[:, pl.ds(mine, own), :], sems.at[0]),
        pltpu.make_async_copy(do_o, do.at[:, pl.ds(other, own), :], sems.at[1]),
        pltpu.make_async_copy(k_h, k, sems.at[2]),
        pltpu.make_async_copy(vt_h, vt, sems.at[3]),
        pltpu.make_async_copy(qa_h, qa, sems.at[4]),
        pltpu.make_async_copy(qt_h, qt, sems.at[5]),
    ]
    for copy in inward:
        copy.start()
    dk[...] = jnp.zeros_like(dk)
    dv[...] = jnp.zeros_like(dv)
    dq[...] = jnp.zeros_like(dq)

    def begin(i, carry):
        qs = pl.ds(pl.multiple_of(i * wide, wide), wide)
        for h in range(heads):
            dot[h, :, qs] = do[h, qs, :].T[:HEAD]
        return carry

    inward[0].wait()
    inward[1].wait()
    lax.fori_loop(0, length // wide, begin, 0)
    for copy in inward[2:]:
        copy.wait()
    first, after, slices = tiles(base, many, block, step)
    probs_at, grads_at = (pa, pb), (ga, gb)

    def fill(s, q, kk):
        qs, ks = slices(q, kk)
        for h in range(heads):
            probs = jnp.exp(mm(qa[h, qs, :], k[h, ks, :], NT))
            probs_at[s][h] = probs.astype(bf16)
            grads_at[s][h] = (probs * mm(do[h, qs, :], vt[h, :, ks], NN)).astype(bf16)

    def use(s, q, kk):
        qs, ks = slices(q, kk)
        for h in range(heads):
            dv[h, :, ks] += mm(dot[h, :, qs], probs_at[s][h], NN)
            dk[h, :, ks] += mm(qt[h, :, qs], grads_at[s][h], NN)
            dq[h, qs, :] += mm(grads_at[s][h], k[h, ks, :], NN)

    run_tiles(n[0], first, after, fill, use)
    outward = []
    for h in range(heads):
        rows = slice(h * HEAD, (h + 1) * HEAD)
        dk_s[rows, :] = dk[h].astype(bf16)
        dv_s[rows, :] = dv[h].astype(bf16)
        outward.append(pltpu.make_async_copy(dk_s.at[rows, :], dk_h.at[rows, :], outs.at[2 * h]))
        outward.append(pltpu.make_async_copy(dv_s.at[rows, :], dv_h.at[rows, :], outs.at[2 * h + 1]))
        outward[-2].start()
        outward[-1].start()
    scale = 1.0 / math.sqrt(HEAD)

    def finish(i, carry):
        qs = pl.ds(pl.multiple_of(i * wide, wide), wide)
        dq_s[qs, :] = jnp.concatenate([dq[h, qs, :][:, :HEAD] * scale for h in range(heads)], axis=1).astype(bf16)
        return carry

    for part in range(2):
        rows = slice(part * own, (part + 1) * own)
        lax.fori_loop(part * own // wide, (part + 1) * own // wide, finish, 0)
        outward.append(pltpu.make_async_copy(dq_s.at[rows, :], dq_h.at[rows, :], outs.at[2 * heads + part]))
        outward[-1].start()
    for copy in outward:
        copy.wait()


def attend_back(base, many, n, who, qa, k, qt, vt, do_m, do_o, block, step):
    heads, length, _ = k.shape
    half = heads * HEAD
    return pl.pallas_call(
        functools.partial(attend_back_body, block=block, step=step, heads=heads),
        in_specs=[IN_SMEM] * 4 + [IN_HBM] * 6,
        out_specs=[IN_HBM] * 3,
        scratch_shapes=[
            pltpu.VMEM((heads, length, LANES), bf16),
            pltpu.VMEM((heads, LANES, length), bf16),
            pltpu.VMEM((heads, length, LANES), bf16),
            pltpu.VMEM((heads, HEAD, length), bf16),
            pltpu.VMEM((heads, length, LANES), bf16),
            pltpu.VMEM((heads, HEAD, length), bf16),
            pltpu.VMEM((heads, HEAD, length), f32),
            pltpu.VMEM((heads, HEAD, length), f32),
            pltpu.VMEM((heads, length, LANES), f32),
            pltpu.VMEM((length, half), bf16),
            pltpu.VMEM((half, length), bf16),
            pltpu.VMEM((half, length), bf16),
        ]
        + [pltpu.VMEM((heads, block, step), bf16)] * 4
        + [pltpu.SemaphoreType.DMA((6,)), pltpu.SemaphoreType.DMA((2 * heads + 2,))],
        out_shape=[
            jax.ShapeDtypeStruct((length, half), bf16),
            jax.ShapeDtypeStruct((half, length), bf16),
            jax.ShapeDtypeStruct((half, length), bf16),
        ],
        compiler_params=params(),
        cost_estimate=cost(20 * heads * length * length * LANES, 24 << 20, heads * length * length),
        name="attend_back",
    )(base, many, n, who, do_m, do_o, k, vt, qa, qt)


def normed_grad(dq, dk, dv, w):
    half = dq.shape[1]
    return (
        mm(dq[...], w[:, :half], NT)
        + mm(dk[...].T, w[:, half : 2 * half], NT)
        + mm(dv[...].T, w[:, 2 * half :], NT)
    )


def unproject_body(who, normed, dq, dk, dv, w, gw, gn, acc_q, acc_kv):
    half = dq.shape[1]
    i = pl.program_id(0)
    steps = pl.num_programs(0) // 2

    @pl.when(i == 0)
    def _():
        acc_q[...] = jnp.zeros_like(acc_q)
        acc_kv[...] = jnp.zeros_like(acc_kv)

    rows = normed[...]
    acc_q[...] += mm(rows, dq[...], TN)
    acc_kv[:half] += mm(dk[...], rows, NN)
    acc_kv[half:] += mm(dv[...], rows, NN)

    @pl.when((i >= steps) == (who[0] == 0))
    def _():
        gn[...] = normed_grad(dq, dk, dv, w).astype(bf16)

    @pl.when(i == pl.num_programs(0) - 1)
    def _():
        gw[...] = jnp.concatenate([acc_q[...].astype(bf16), acc_kv[...].T.astype(bf16)], axis=1)


def unproject(who, normed, dq, dk, dv, w, block=1024):
    length, width = normed.shape
    own, half = length // 2, dq.shape[1]
    steps = own // block
    cols = pl.BlockSpec((half, block), lambda i, who: (0, i))
    return pl.pallas_call(
        unproject_body,
        grid_spec=pltpu.PrefetchScalarGridSpec(
            num_scalar_prefetch=1,
            grid=(length // block,),
            in_specs=[
                pl.BlockSpec((block, width), lambda i, who: (i, 0)),
                pl.BlockSpec((block, half), lambda i, who: (i, 0)),
                cols,
                cols,
                whole(width, 3 * half),
            ],
            out_specs=[
                whole(width, 3 * half),
                pl.BlockSpec((block, width), lambda i, who: (jnp.clip(i - (1 - who[0]) * steps, 0, steps - 1), 0)),
            ],
            scratch_shapes=[pltpu.VMEM((width, half), f32), pltpu.VMEM((2 * half, width), f32)],
        ),
        out_shape=[jax.ShapeDtypeStruct((width, 3 * half), bf16), jax.ShapeDtypeStruct((own, width), bf16)],
        compiler_params=params(),
        cost_estimate=cost(9 * length * width * half, 12 << 20),
        name="unproject",
    )(who, normed, dq, dk, dv, w)


def finish_body(who, dq, dk, dv, w, tok, gn_o, mid, small, out, gs):
    @pl.when(pl.program_id(0) == 0)
    def _():
        gs[...] = jnp.zeros_like(gs)

    hat, rstd = normalize(tok[...].astype(f32))
    grad = normed_grad(dq, dk, dv, w) + gn_o[...].astype(f32)
    out[...] = (mid[...] + normalize_back(grad * small[0:1], hat, rstd)).astype(bf16)
    gs[...] += jnp.concatenate(
        [
            jnp.sum(grad * hat, axis=0, keepdims=True),
            jnp.sum(grad, axis=0, keepdims=True),
            jnp.zeros((6, grad.shape[1]), f32),
        ],
        axis=0,
    )


def finish(who, dq, dk, dv, w, tok, gn_o, mid, small, block=512):
    own, width = tok.shape
    half = dq.shape[1]
    steps = own // block
    rows = pl.BlockSpec((block, width), lambda i, who: (i, 0))
    cols = pl.BlockSpec((half, block), lambda i, who: (0, i + who[0] * steps))
    return pl.pallas_call(
        finish_body,
        grid_spec=pltpu.PrefetchScalarGridSpec(
            num_scalar_prefetch=1,
            grid=(steps,),
            in_specs=[
                pl.BlockSpec((block, half), lambda i, who: (i + who[0] * steps, 0)),
                cols,
                cols,
                whole(width, 3 * half),
                rows,
                rows,
                rows,
                whole(8, width),
            ],
            out_specs=[rows, whole(8, width)],
        ),
        out_shape=[jax.ShapeDtypeStruct((own, width), bf16), jax.ShapeDtypeStruct((8, width), f32)],
        compiler_params=params(),
        cost_estimate=cost(0, 1 << 20),
        name="finish",
    )(who, dq, dk, dv, w, tok, gn_o, mid, small)


def adamw(weight, grad, first, second, rate, decay):
    first = BETA_ONE * first + (1.0 - BETA_ONE) * grad
    second = BETA_TWO * second + (1.0 - BETA_TWO) * grad * grad
    fixed_one = first / (1.0 - BETA_ONE**STEP)
    fixed_two = second / (1.0 - BETA_TWO**STEP)
    weight = weight - rate * (fixed_one / (jnp.sqrt(fixed_two) + ADAM_EPS) + decay * weight)
    return (weight, first, second)


def update_body(*refs, width, tiny_len, rates):
    many = len(rates)
    every, taken = refs[0], refs[1 : 1 + 4 * many]
    given, norm_o = refs[1 + 4 * many : -1], refs[-1]
    count = every.shape[0] // 2
    parts = every[...].astype(f32)
    norm_one = jnp.sum(parts[:, : 2 * width], axis=0, keepdims=True)
    tiny = parts[:count, 2 * width + LANES :] + parts[count:, 2 * width + LANES :]
    total = jnp.sum(parts[:, 2 * width : 2 * width + LANES]) + jnp.sum(norm_one * norm_one) + jnp.sum(tiny * tiny)
    grad_norm = jnp.sqrt(jnp.full((8, LANES), total, f32))
    norm_o[...] = grad_norm
    factor = jnp.minimum(1.0, CLIP_NORM / (grad_norm[:1, :1] + 1e-06))
    for m in range(many):
        weight, grad, first, second = (ref[...] for ref in taken[4 * m : 4 * m + 4])
        new = adamw(weight, grad * factor, first, second, rates[m], DECAY_MATRIX)
        for ref, value in zip(given[3 * m : 3 * m + 3], new):
            ref[...] = value


def update(every, matrices, rates, width, tiny_len):
    flat = [array for group in matrices for array in group]
    shapes = [jax.ShapeDtypeStruct(group[0].shape, f32) for group in matrices for _ in range(3)]
    shapes.append(jax.ShapeDtypeStruct((8, LANES), f32))
    out = pl.pallas_call(
        functools.partial(update_body, width=width, tiny_len=tiny_len, rates=rates),
        in_specs=[IN_VMEM] * (1 + len(flat)),
        out_specs=[IN_VMEM] * len(shapes),
        out_shape=shapes,
        compiler_params=params(),
        name="update",
    )(every, *flat)
    return [out[3 * m : 3 * m + 3] for m in range(len(matrices))], out[-1][0, 0]


def swap(values):
    return lax.ppermute(values, "dp", [(0, 1), (1, 0)])


def across(values, count, bit):
    return lax.ppermute(values, "fsdp", [(i, i ^ bit) for i in range(count)])


def gather(shard, count, beside):
    if count < 8 or count & (count - 1):
        return lax.all_gather(shard, "fsdp", axis=0), beside
    me = lax.axis_index("fsdp")
    held = shard
    depth = 0
    bit = count // 2
    while bit > 2:
        there = across(held, count, bit)
        above = (me & bit) != 0
        held = jnp.where(above, jnp.stack([there, held], axis=depth), jnp.stack([held, there], axis=depth))
        depth += 1
        bit //= 2
    many = count // 4
    held, beside = lax.optimization_barrier((held.reshape((many,) + shard.shape), beside))
    side, line = across(held, count, 1), across(held, count, 2)
    corner = jnp.concatenate([across(side[: many // 2], count, 2), across(line[many // 2 :], count, 1)], axis=0)
    place = me & 3

    def block(j):
        at = place ^ j
        return jnp.where(at == 0, held, jnp.where(at == 1, side, jnp.where(at == 2, line, corner)))

    return jnp.stack([block(j) for j in range(4)], axis=1).reshape((count,) + shard.shape), beside


def local(
    tokens,
    segments,
    cotangent,
    w_qkv,
    w_out,
    w_up,
    w_down,
    small_params,
    up_bias,
    first_qkv,
    first_out,
    first_up,
    first_down,
    first_small,
    first_bias,
    second_qkv,
    second_out,
    second_up,
    second_down,
    second_small,
    second_bias,
    *,
    count,
):
    own, width = tokens.shape[1:]
    length = segments.shape[1]
    heads = HEADS // 2
    half = heads * HEAD
    hid = w_up.shape[1] // 2
    cols = 2 * hid + half
    rows = w_qkv.shape[0]
    out_fan = max(1, width * (DOCS + 1) // length)
    rate_out = RATE_MATRIX * math.sqrt(width / out_fan)
    dp = lax.axis_index("dp")
    block, step = 256, 512

    def mine_of(values, size, axis, start=0):
        return lax.dynamic_slice_in_dim(values, start + dp * size, size, axis)

    def in_order(mine, other, axis):
        return jnp.where(
            dp == 0, jnp.stack([mine, other], axis=axis), jnp.stack([other, mine], axis=axis)
        )

    tok = tokens[0]
    tok_other = swap(tok)
    seg = segments[0]
    below = jnp.sum((seg[None, :] < seg[::block, None]).astype(jnp.int32), axis=1)
    until = jnp.sum((seg[None, :] <= seg[block - 1 :: block, None]).astype(jnp.int32), axis=1)
    low = below // LANES * LANES
    high = -(-until // LANES) * LANES
    many = -(-(high - low) // step)
    base = jnp.maximum(high - many * step, 0)
    n = jnp.sum(many).reshape(1)
    who = dp.astype(jnp.int32).reshape(1)

    wide = 3 * half
    tiny_len = 6 * rows + up_bias.shape[0]
    lines = -(-tiny_len // wide)
    qkv_shard = jnp.concatenate([mine_of(w_qkv, half, 1, part * width) for part in range(3)], axis=1)
    tiny = jnp.concatenate([small_params.T.reshape(-1), up_bias])
    tiny = jnp.pad(tiny, (0, lines * wide - tiny_len)).reshape(lines, wide)
    first_all, (base, many, n, tok_other, up, down, out) = gather(
        jnp.concatenate([qkv_shard, tiny], axis=0).astype(bf16),
        count,
        (base, many, n, tok_other, w_up, w_down, w_out),
    )
    w_one = first_all[:, :rows].reshape(width, wide)
    tiny_all = first_all[:, rows:].reshape(count, -1)[:, :tiny_len].astype(f32)
    small = jnp.pad(tiny_all[:, : 6 * rows].reshape(width, 6).T, ((0, 2), (0, 0)))
    bias_all = tiny_all[:, 6 * rows :].reshape(1, 2, hid)
    bias = jnp.where(dp == 0, bias_all, bias_all[:, ::-1]).reshape(1, 2 * hid)
    rest_shard = jnp.concatenate(
        [mine_of(up, hid, 1), mine_of(down, hid, 0).T, mine_of(out, half, 0).T], axis=1
    ).astype(bf16)
    rest_all = lax.all_to_all(jnp.broadcast_to(rest_shard, (count, rows, cols)), "fsdp", 0, 0)

    mix_m, mix_send, queries, normed, keys, queries_t, values_t = attend(
        base, many, n, who, tok, tok_other, w_one, small, segments, heads, block, step
    )
    mix_send, rest_all = lax.optimization_barrier((mix_send, rest_all))
    mix_o, rest_other = swap(mix_send), swap(rest_all)
    if rows % 16:
        rest_all, rest_other = (half_of.reshape(1, width, cols) for half_of in (rest_all, rest_other))
    layer_out, grad_mid, do_m, do_send, gw_m, gw_send, gs_two, gb = feed(
        tok, cotangent[0], mix_m, mix_o, rest_all, rest_other, small, bias, heads
    )
    gb_all = jnp.where(dp == 0, gb.reshape(2, hid), gb.reshape(2, hid)[::-1]).reshape(count, -1)
    grad_tiny = jnp.concatenate([gs_two[:6].T.reshape(count, 6 * rows), gb_all], axis=1)
    grad_tiny = jnp.pad(grad_tiny, ((0, 0), (0, cols - tiny_len))).reshape(count, 1, cols)
    gw_pair = (gw_m.astype(f32) + swap(gw_send).astype(f32)).reshape(count, rows, cols)
    gw_pair = jnp.concatenate([gw_pair, grad_tiny], axis=1).astype(bf16)
    do_o, gw_pair = lax.optimization_barrier((swap(do_send), gw_pair))
    arrived = lax.all_to_all(gw_pair, "fsdp", 0, 0)
    dq, dk, dv = attend_back(base, many, n, who, queries, keys, queries_t, values_t, do_m, do_o, block, step)
    dq, arrived = lax.optimization_barrier((dq, arrived))
    gw_one, gn_send = unproject(who, normed, dq, dk, dv, w_one)
    spread_one = lax.all_to_all(gw_one.reshape(count, rows, wide), "fsdp", 0, 0)
    gn_o = swap(gn_send)
    input_grad, gs_one = finish(who, dq, dk, dv, w_one, tok, gn_o, grad_mid, small)
    spread_one, gs_one = lax.optimization_barrier((spread_one, gs_one))
    rest_sum = jnp.sum(arrived.astype(f32), axis=0)
    rest_grad, tiny_mine = rest_sum[:rows], rest_sum[rows]
    rest_grad_other = swap(rest_grad)
    rest_squares = jnp.sum(rest_grad * rest_grad)
    qkv_mine = jnp.sum(spread_one.astype(f32), axis=0)
    squares = jnp.sum(qkv_mine * qkv_mine) + rest_squares
    high = squares.astype(bf16)
    middle = (squares - high.astype(f32)).astype(bf16)
    low = (squares - high.astype(f32) - middle.astype(f32)).astype(bf16)
    place = jnp.arange(LANES)
    sums = jnp.where(place == 0, high, jnp.where(place == 1, middle, jnp.where(place == 2, low, 0)))
    every = jnp.concatenate([gs_one[:2].reshape(-1).astype(bf16), sums, tiny_mine[:tiny_len].astype(bf16)])
    every = jnp.broadcast_to(every, (2 * count, 1, every.shape[0]))
    qkv_mine, every = lax.optimization_barrier((qkv_mine, every))
    every = lax.all_to_all(every, ("dp", "fsdp"), 0, 0)[:, 0]
    qkv_other = swap(qkv_mine)
    own_qkv = in_order(qkv_mine.reshape(rows, 3, half), qkv_other.reshape(rows, 3, half), 2).reshape(rows, -1)
    own_up = in_order(rest_grad[:, :hid], rest_grad_other[:, :hid], 1).reshape(rows, -1)
    own_down = in_order(rest_grad[:, hid : 2 * hid], rest_grad_other[:, hid : 2 * hid], 1).reshape(rows, -1)
    own_out = in_order(rest_grad[:, 2 * hid :], rest_grad_other[:, 2 * hid :], 1).reshape(rows, -1)
    new, grad_norm = update(
        every,
        (
            (w_qkv, own_qkv, first_qkv, second_qkv),
            (w_out.T, own_out, first_out.T, second_out.T),
            (w_up, own_up, first_up, second_up),
            (w_down.T, own_down, first_down.T, second_down.T),
        ),
        (RATE_MATRIX, rate_out, RATE_MATRIX, RATE_MATRIX),
        width,
        tiny_len,
    )
    new_qkv, new_first_qkv, new_second_qkv = new[0]
    new_out, new_first_out, new_second_out = (array.T for array in new[1])
    new_up, new_first_up, new_second_up = new[2]
    new_down, new_first_down, new_second_down = (array.T for array in new[3])
    factor = jnp.minimum(1.0, CLIP_NORM / (grad_norm + 1e-06))
    me = lax.axis_index("fsdp")
    parts = every.reshape(2, count, -1).astype(f32)
    tiny_own = lax.dynamic_index_in_dim(parts[:, :, 2 * width + LANES :], me, 1, keepdims=False).sum(axis=0)
    norm_one = jnp.sum(parts[:, :, : 2 * width], axis=(0, 1)).reshape(2, width)
    norm_own = lax.dynamic_slice_in_dim(norm_one, me * rows, rows, 1)
    own_small = tiny_own[: 6 * rows].reshape(rows, 6).T + jnp.pad(norm_own, ((0, 4), (0, 0)))
    own_bias = tiny_own[6 * rows :]
    new_small, new_first_small, new_second_small = adamw(
        small_params, own_small * factor, first_small, second_small, RATE_VECTOR, 0.0
    )
    new_bias, new_first_bias, new_second_bias = adamw(
        up_bias, own_bias * factor, first_bias, second_bias, RATE_VECTOR, 0.0
    )
    return (
        layer_out[None],
        input_grad[None],
        grad_norm,
        new_qkv,
        new_out,
        new_up,
        new_down,
        new_small,
        new_bias,
        new_first_qkv,
        new_first_out,
        new_first_up,
        new_first_down,
        new_first_small,
        new_first_bias,
        new_second_qkv,
        new_second_out,
        new_second_up,
        new_second_down,
        new_second_small,
        new_second_bias,
    )


def solution(mesh):
    rows, cols, flat = P("fsdp", None), P(None, "fsdp"), P("fsdp")
    by_token = P("fsdp", "dp", None)
    weights = (rows, cols, rows, cols, cols, flat)
    in_specs = (by_token, rows, by_token) + 3 * weights
    out_specs = (by_token, by_token, P()) + 3 * weights
    body = functools.partial(local, count=mesh.shape["fsdp"])
    return jax.shard_map(body, mesh=mesh, in_specs=in_specs, out_specs=out_specs, check_vma=False)
```
